32 devices in a mesh: tok: 8 (over y, x, core), head: 4 (over z).
Axes of the slice: x: 2, y: 2, z: 4, core: 2. Of those that a mesh axis runs over, the one named last changes fastest.
Arguments:
- tokens: bfloat16 [2048, 1024], P('tok'), may hold values from -6 to 6
- class_ids: int32 [3], replicated, may hold values from 0 to 999
- slot_item: int32 [2048], replicated, may hold values from -1 to 2, as said below
- slot_scale: int32 [2048], replicated, may hold values from 0 to 9, as said below
- class_table: bfloat16 [1000, 1024], replicated, may hold values from -6 to 6
- w_ada: bfloat16 [6, 1024, 1024], replicated, may hold values from -0.1875 to 0.1875
- w_qkv: bfloat16 [1024, 3, 1024], P(None, None, 'head'), may hold values from -0.1875 to 0.1875
- w_out: bfloat16 [1024, 1024], P('head'), may hold values from -2 to 2
- w_fc1: bfloat16 [1024, 4096], P(None, 'head'), may hold values from -0.1875 to 0.1875
- w_fc2: bfloat16 [4096, 1024], P('head'), may hold values from -0.09375 to 0.09375
- cotangent: bfloat16 [2048, 1024], P('tok'), may hold values from -6 to 6
Outputs:
- output: bfloat16 [2048, 1024], P('tok')
- d_tokens: bfloat16 [2048, 1024], P('tok')
- d_class_table: float32 [1000, 1024], P(None, 'head')
- d_w_ada: float32 [6, 1024, 1024], P(None, None, 'head')
- d_w_qkv: float32 [1024, 3, 1024], P(None, None, 'head')
- d_w_out: float32 [1024, 1024], P('head')
- d_w_fc1: float32 [1024, 4096], P(None, 'head')
- d_w_fc2: float32 [4096, 1024], P('head')
The draws below stay inside these ranges and needn't reach their ends.
Inputs may be any that keep to these rules, and one draw needn't show every extreme that they name: `slot_item`: empty slots hold -1, the others an image. All tokens of scale s of all images precede those of scale s + 1; scale s of an image holds p * p tokens in a row, p = 1, 2, 3, 4, 5, 6, 8, 10, 13, 16 for s = 0 to 9; every image has all its 680 tokens; empty slots lie anywhere. `slot_scale`: the scale of the slot's token; an empty slot repeats the scale of the nearest earlier token (0 before the first), so the values never fall along the slots.
All inputs are finite; a program needn't handle non-finite values.
Results may differ from the reference program's by a relative error of at most 0.018.
Values may be sent and summed in bfloat16 or wider, within the bound.
A program may use at most 192 MiB of HBM per device.

```python
import math
import jax
import jax.numpy as jnp
from jax import lax

D = 1024
HEADS = 16
HEAD_DIM = 64
FF = 4096
NCLASS = 1000
ITEM_LEN = 680
TOKENS = 2048
ITEMS = 3


PATCHES = (1, 2, 3, 4, 5, 6, 8, 10, 13, 16)


def layout_of(key):
    item_parts = []
    scale_parts = []
    for level, side in enumerate(PATCHES):
        order = jax.random.permutation(jax.random.fold_in(key, 100 + level), ITEMS).astype(jnp.int32)
        item_parts.append(jnp.repeat(order, side * side, total_repeat_length=ITEMS * side * side))
        scale_parts.append(jnp.full((ITEMS * side * side,), level, jnp.int32))
    item_list = jnp.concatenate(item_parts).astype(jnp.int32)
    scale_list = jnp.concatenate(scale_parts).astype(jnp.int32)
    spare = TOKENS - ITEM_LEN * ITEMS
    ranking = jax.random.permutation(jax.random.fold_in(key, 200), TOKENS).astype(jnp.int32)
    vacant = ranking < spare
    position = (jnp.cumsum(jnp.where(vacant, 0, 1).astype(jnp.int32)) - 1).astype(jnp.int32)
    position = jnp.clip(position, 0, ITEM_LEN * ITEMS - 1).astype(jnp.int32)
    slot_item = jnp.where(vacant, -1, item_list[position]).astype(jnp.int32)
    slot_scale = scale_list[position].astype(jnp.int32)
    return (slot_item, slot_scale)


def draw_slot_item(key, part):
    return layout_of(key)[0]


def draw_slot_scale(key, part):
    return layout_of(key)[1]


def level_of(key, shape, cuts, smallest, largest):
    level = 1.0
    for dim, shards_of in cuts:
        heights = jax.random.uniform(jax.random.fold_in(jax.random.fold_in(key, 6), dim), (shards_of,), jnp.float32, smallest / len(cuts), largest / len(cuts))
        level = level * jnp.repeat(jnp.exp(heights), shape[dim] // shards_of).reshape((-1,) + (1,) * (len(shape) - 1 - dim))
    return level


def centred(own_key, extent, scale, limit, shards=(), dtype=jnp.bfloat16):
    factor_of = level_of(own_key, extent, shards, -0.22, 0.18) if shards else 1.0
    array = jax.random.normal(own_key, extent, jnp.float32) * scale * factor_of
    return jnp.minimum(jnp.maximum(array, -limit), limit).astype(dtype)


def setup_inputs(seed: int = 0) -> dict:
    arg_keys = jax.random.split(jax.random.key(seed), 12)
    return {
        "tokens": centred(arg_keys[0], (TOKENS, D), 1.0, 6.0, ((0, 8),)),
        "class_ids": jax.random.randint(arg_keys[1], (ITEMS,), 0, NCLASS).astype(jnp.int32),
        "slot_item": draw_slot_item(jax.random.fold_in(arg_keys[11], 71), 0),
        "slot_scale": draw_slot_scale(jax.random.fold_in(arg_keys[11], 71), 0),
        "class_table": centred(arg_keys[4], (NCLASS, D), 1.0, 6.0),
        "w_ada": centred(arg_keys[5], (6, D, D), D ** -0.5, 0.1875),
        "w_qkv": centred(arg_keys[6], (D, 3, D), D ** -0.5, 0.1875, ((2, 4),)),
        "w_out": centred(arg_keys[7], (D, D), (max(D // 128, 1)) ** -0.5, 2.0, ((0, 4),)),
        "w_fc1": centred(arg_keys[8], (D, FF), D ** -0.5, 0.1875, ((1, 4),)),
        "w_fc2": centred(arg_keys[9], (FF, D), FF ** -0.5, 0.09375, ((0, 4),)),
        "cotangent": centred(arg_keys[10], (TOKENS, D), 1.0, 6.0, ((0, 8),)),
    }


@jax.custom_vjp
def low(v):
    return lax.optimization_barrier(v.astype(jnp.bfloat16)).astype(jnp.float32)

@jax.custom_vjp
def low_back(v):
    return v

def low_keep(v):
    return (low(v), None)

def low_pass(kept, grad):
    return (grad,)

def back_keep(v):
    return (v, None)

def back_low(kept, grad):
    return (low(grad),)
low.defvjp(low_keep, low_pass)
low_back.defvjp(back_keep, back_low)
EPS = 1e-06
HIGH = lax.Precision.HIGHEST

def layer_norm(values):
    centre = lax.optimization_barrier(jnp.mean(values, axis=-1, keepdims=True))
    shifted = values - centre
    spread = lax.optimization_barrier(jnp.mean(shifted * shifted, axis=-1, keepdims=True))
    return shifted * lax.rsqrt(spread + EPS)

def attend(query_block, item_block, scale_block, keys, values, slot_item, slot_scale):
    scores = jnp.einsum('qhd,khd->hqk', query_block, keys, precision=HIGH) * 0.125
    scores = low_back(scores)
    allowed = ((item_block[:, None] == slot_item[None, :]) & (slot_scale[None, :] <= scale_block[:, None]))[None]
    scores = jnp.where(allowed, scores, -1e+30)
    rounded = low(jax.nn.softmax(scores, axis=-1))
    return jnp.einsum('hqk,khd->qhd', rounded, values, precision=HIGH)

def forward(tokens, class_table, w_ada, w_qkv, w_out, w_fc1, w_fc2, class_ids, slot_item, slot_scale):
    cond = class_table[class_ids]
    cond_low = low(jax.nn.silu(cond))
    modes = jnp.einsum('id,cde->ice', cond_low, w_ada, precision=HIGH)
    present = slot_item >= 0
    safe_item = jnp.where(present, slot_item, 0).astype(jnp.int32)
    per_token = jnp.where(present[:, None, None], modes[safe_item], 0.0)
    gamma_one = per_token[:, 0]
    gamma_two = per_token[:, 1]
    scale_one = per_token[:, 2]
    scale_two = per_token[:, 3]
    shift_one = per_token[:, 4]
    shift_two = per_token[:, 5]
    a_low = low(layer_norm(tokens) * (1.0 + scale_one) + shift_one)
    qkv = low(low_back(jnp.einsum('td,dce->tce', a_low, w_qkv, precision=HIGH)))
    split = qkv.reshape(TOKENS, 3, HEADS, HEAD_DIM)
    queries = split[:, 0]
    keys = split[:, 1]
    values = split[:, 2]
    block_rows = math.gcd(TOKENS, 256)
    blocks = TOKENS // block_rows

    def one_block(pieces):
        return attend(pieces[0], pieces[1], pieces[2], keys, values, slot_item, slot_scale)
    mapped = lax.map(jax.checkpoint(one_block), (queries.reshape(blocks, block_rows, HEADS, HEAD_DIM), slot_item.reshape(blocks, block_rows), slot_scale.reshape(blocks, block_rows)))
    heads_low = low(low_back(mapped.reshape(TOKENS, HEADS * HEAD_DIM)))
    attn_out = low_back(jnp.dot(heads_low, w_out, precision=HIGH))
    hidden = tokens + gamma_one * attn_out
    b_low = low(layer_norm(hidden) * (1.0 + scale_two) + shift_two)
    up_proj = low_back(jnp.dot(b_low, w_fc1, precision=HIGH))
    act_low = low(jax.nn.gelu(up_proj, approximate=True))
    mlp_out = low_back(jnp.dot(act_low, w_fc2, precision=HIGH))
    return hidden + gamma_two * mlp_out

def reference(tokens, class_ids, slot_item, slot_scale, class_table, w_ada, w_qkv, w_out, w_fc1, w_fc2, cotangent):

    def wrapped(tok_in, table_in, ada_in, qkv_in, out_in, fc_one, fc_two):
        return forward(tok_in, table_in, ada_in, qkv_in, out_in, fc_one, fc_two, class_ids, slot_item, slot_scale)
    result, pullback = jax.vjp(wrapped, tokens.astype(jnp.float32), class_table.astype(jnp.float32), w_ada.astype(jnp.float32), w_qkv.astype(jnp.float32), w_out.astype(jnp.float32), w_fc1.astype(jnp.float32), w_fc2.astype(jnp.float32))
    grads = pullback(cotangent.astype(jnp.float32))
    return (result.astype(jnp.bfloat16), grads[0].astype(jnp.bfloat16), grads[1], grads[2], grads[3], grads[4], grads[5], grads[6])
```

```python
import functools
import math
import types

import jax
import jax.numpy as jnp
from jax import lax
from jax.experimental import pallas as pl
from jax.experimental.pallas import tpu as pltpu
from jax.sharding import PartitionSpec as P

HEAD_DIM = 64
COMPONENTS = 6


EPS = 1e-06
HIGH = lax.Precision.HIGHEST
BF = jnp.bfloat16
F32 = jnp.float32
MESH = pl.DeviceIdType.MESH
BARRED = -1e30
EIGHTH_LOG2 = 0.125 * math.log2(math.e)
GELU_A = math.sqrt(2.0 / math.pi)
GELU_B = 0.044715
COPIES = 160
VMEM_BYTES = 62 * 1024 * 1024
ITEM_ROWS = 16


def dot(left, right):
    return lax.dot_general(left, right, (((1,), (0,)), ((), ())), preferred_element_type=F32)


def dot_nt(left, right):
    return lax.dot_general(left, right, (((1,), (1,)), ((), ())), preferred_element_type=F32)


def dot_tn(left, right):
    return lax.dot_general(left, right, (((0,), (0,)), ((), ())), preferred_element_type=F32)


def turned(block):
    return block.astype(F32).T


def norm_rows(values):
    shifted = values - jnp.mean(values, axis=-1, keepdims=True)
    inverse = lax.rsqrt(jnp.mean(shifted * shifted, axis=-1, keepdims=True) + EPS)
    return shifted * inverse, inverse


def norm_back(grad, normed, inverse):
    along = jnp.mean(grad * normed, axis=-1, keepdims=True)
    return (grad - jnp.mean(grad, axis=-1, keepdims=True) - normed * along) * inverse


class Net:
    def __init__(self, send, arrive):
        self.send, self.arrive = send, arrive
        self.made, self.waited = [], []

    def copy(self, source, target, device, when=None, gets=None):
        k = len(self.made)
        one = pltpu.make_async_remote_copy(
            src_ref=source,
            dst_ref=target,
            send_sem=self.send.at[k],
            recv_sem=self.arrive.at[k],
            device_id=device,
            device_id_type=MESH,
        )
        self.made.append((one, when, gets))
        on_some(when, one.start)
        return k

    def arrived(self, k):
        one, _, gets = self.made[k]
        on_some(gets, one.wait_recv)
        self.waited.append(k)

    def finish(self):
        for k, (one, when, _) in enumerate(self.made):
            on_some(when, one.wait_send)
            if k not in self.waited:
                self.arrived(k)


def on_some(when, act):
    if when is None:
        act()
    else:
        pl.when(when)(act)


def block_kernel(dims, *refs):
    rows, width, part, hidden, items, classes = dims
    names = list(buffers(dims))
    (
        tok_h, cls_s, item_v, scale_v, table_h, ada_h, wq_h, wo_h, f1_h, f2_h, cot_h,
        out_o, dtok_o, gqkv_o, gout_o, gf1_o, gf2_o, mode_o, cond_o,
        send_sem, arrive_sem, load_sem, *scratch,
    ) = refs
    b = types.SimpleNamespace(**dict(zip(names, scratch, strict=True)))
    own = rows // 4
    half = width // 2
    net = Net(send_sem, arrive_sem)
    loads = []

    def load(source, target):
        one = pltpu.make_async_copy(source, target, load_sem.at[len(loads)])
        one.start()
        loads.append(one)
        return one

    group = lax.axis_index("tok")
    plane = lax.axis_index("head")
    core = lax.rem(group, 2)
    chip = lax.div(group, 2)
    col, line = lax.rem(chip, 2), lax.div(chip, 2)
    chips = [chip, line * 2 + 1 - col, (1 - line) * 2 + col, 3 - chip]
    planes = [
        plane,
        lax.div(plane, 2) * 2 + 1 - lax.rem(plane, 2),
        lax.rem(plane + 2, 4),
        3 - plane,
    ]
    other = 1 - core
    inner = (plane == 1) | (plane == 2)
    outer = (plane == 0) | (plane == 3)
    offsets = [(dp, dz) for dz in range(4) for dp in range(4) if dp or dz]

    def at(dp, dz):
        return (chips[dp] * 2 + core, planes[dz])

    mate = (chip * 2 + other, plane)
    mine = pl.ds(pl.multiple_of(plane * own, own), own)

    l_table = load(table_h, b.table)
    l_ada = {k: load(ada_h.at[k], b.ada.at[k]) for k in (2, 4)}
    l_tok = load(tok_h, b.tok)
    l_wq = load(wq_h, b.wq)
    barrier = pltpu.get_barrier_semaphore()
    for dp, dz in offsets:
        pl.semaphore_signal(barrier, inc=1, device_id=at(dp, dz), device_id_type=MESH)
    pl.semaphore_signal(barrier, inc=1, device_id=mate, device_id_type=MESH)

    spot = lax.rem(lax.broadcasted_iota(jnp.int32, (3 * ITEM_ROWS, rows), 0), ITEM_ROWS)
    picks = jnp.where(spot == item_v[group], 1.0, 0.0)
    b.pick[...] = picks.T.astype(BF)

    spot = lax.broadcasted_iota(jnp.int32, (ITEM_ROWS, classes), 0)
    label = lax.broadcasted_iota(jnp.int32, (ITEM_ROWS, classes), 1)
    hot = jnp.zeros((ITEM_ROWS, classes), F32)
    for i in range(items):
        hot = jnp.where((spot == i) & (label == cls_s[i]), 1.0, hot)
    l_table.wait()
    cond = dot(hot.astype(BF), b.table[...])
    b.cond[...] = cond
    cond_low = (cond / (1.0 + jnp.exp(-cond))).astype(BF)

    def make_mode(k):
        l_ada[k].wait()
        value = dot(cond_low, b.ada[k])
        high = value.astype(BF)
        rest = value - high.astype(F32)
        middle = rest.astype(BF)
        b.modes[k, 0:ITEM_ROWS] = high
        b.modes[k, ITEM_ROWS : 2 * ITEM_ROWS] = middle
        b.modes[k, 2 * ITEM_ROWS : 3 * ITEM_ROWS] = (rest - middle.astype(F32)).astype(BF)

    def per_token(k, which):
        return dot(b.pick[which], b.modes[k])

    def chunks(body):
        def step(i, carry):
            body(pl.ds(pl.multiple_of(i * 64, 64), 64))
            return carry

        lax.fori_loop(0, rows // 64, step, 0)

    make_mode(2)
    make_mode(4)

    l_tok.wait()

    def first_norm(which):
        normed, _ = norm_rows(b.tok[which].astype(F32))
        value = (normed * (1.0 + per_token(2, which)) + per_token(4, which)).astype(BF)
        b.a[0, which] = value[:, :half]
        b.a[1, which] = value[:, half:]

    chunks(first_norm)
    l_wq.wait()
    l_wo = load(wo_h, b.wo.at[plane])
    l_ada.update({k: load(ada_h.at[k], b.ada.at[k]) for k in (0, 3, 5, 1)})
    l_cot = load(cot_h, b.cot)
    l_f2 = load(f2_h, b.f2)
    l_f1 = load(f1_h, b.f1)
    first_store = len(loads)
    for k in range(3):
        value = dot(b.a[0], b.wq[k, :half]) + dot(b.a[1], b.wq[k, half:])
        value = value.T.astype(BF)
        for h in range(4):
            b.q_out[h, k * 64 : (k + 1) * 64] = value[h * 64 : (h + 1) * 64]
    pl.semaphore_wait(barrier, len(offsets) + 1)
    sent_q = [
        net.copy(b.q_out.at[chips[dp]], b.q_in.at[chip], at(dp, 0)) for dp in (3, 1, 2)
    ]
    b.q_in[chip] = b.q_out[chip]
    sent_k = [net.copy(b.q_in.at[chip, 64:192], b.k_in.at[chip], mate)]
    b.a_all[chip, core] = b.a[core]
    sent_a = net.copy(b.a.at[other], b.a_all.at[chip, core], mate)
    sent_wo = [
        net.copy(wo_h.at[chip, core], b.wo.at[plane, chip, core], at(0, dz)) for dz in (3, 2, 1)
    ]

    spot = lax.broadcasted_iota(jnp.int32, (64, rows), 0)
    for s in range(4):
        for k, parity in enumerate((core, other)):
            item, scale = item_v[s * 2 + parity], scale_v[s * 2 + parity]
            by_item = jnp.where(item != spot - 1, BARRED, 0.0)
            by_scale = jnp.where((spot < 32) & (scale > spot - 16), BARRED, 0.0)
            b.kt[k * 4 + s, 64:128] = jnp.where(spot < 16, by_item, by_scale).astype(BF)
        item, scale = item_v[s * 2 + core], scale_v[s * 2 + core]
        by_item = jnp.where(item == spot - 1, 1.0, 0.0)
        by_scale = jnp.where((spot < 32) & (scale == spot - 16), 1.0, 0.0)
        b.qt[s, 64:128] = jnp.where(spot < 16, by_item, by_scale).astype(BF)
    make_mode(0)
    make_mode(3)
    for one, dp in zip(sent_q, (3, 1, 2), strict=True):
        net.arrived(one)
        sent_k.append(net.copy(b.q_in.at[chips[dp], 64:192], b.k_in.at[chips[dp]], mate))
    sent_all = [
        net.copy(b.a_all.at[chip, core], b.a_all.at[chip, core], at(dp, 0)) for dp in (3, 1, 2)
    ]
    for one in sent_wo:
        net.arrived(one)
    sent_wo2 = {
        (dp, dz): net.copy(
            b.wo.at[planes[dz], chip, core], b.wo.at[planes[dz], chip, core], at(dp, 0)
        )
        for dz in (1, 2, 3)
        for dp in (3, 1, 2)
    }
    make_mode(5)
    make_mode(1)
    l_cot.wait()

    def mlp_grad(which):
        b.mg[which] = (per_token(1, which) * b.cot[which].astype(F32)).astype(BF)

    chunks(mlp_grad)
    sent_mg = net.copy(b.mg, b.mg_in, mate)

    for s in range(4):
        b.qt[s, 0:64] = b.q_in[s, 0:64]
        b.kt[s, 0:64] = b.q_in[s, 64:128]
        b.vt[s] = b.q_in[s, 128:192]
    for one in sent_k:
        net.arrived(one)
    for s in range(4):
        b.kt[4 + s, 0:64] = b.k_in[s, 0:64]
        b.vt[4 + s] = b.k_in[s, 64:128]
    for s in range(8):
        b.ka[s] = turned(b.kt[s]).astype(BF)

    sent_h = {}
    for dp in (3, 1, 2, 0):
        q = chips[dp]
        queries = b.qt[q]
        peak = None
        for s in range(8):
            scores = dot(b.ka[s], queries)
            b.scores[s] = scores
            top = jnp.max(scores, axis=0, keepdims=True)
            peak = top if peak is None else jnp.maximum(peak, top)
        total = jnp.zeros((1, rows), F32)
        result = jnp.zeros((64, rows), F32)
        for s in range(8):
            terms = jnp.exp2((b.scores[s] - peak) * EIGHTH_LOG2)
            total = total + jnp.sum(terms, axis=0, keepdims=True)
            low = terms.astype(BF)
            b.terms[q, s] = low
            result = result + dot(b.vt[s], low)
        share = 1.0 / total
        b.share[q] = share
        result = result * share
        b.heads[q] = result
        b.h_out[q] = result.astype(BF)
        for dz in (3, 2, 1, 0):
            if dp or dz:
                sent_h[dp, dz] = net.copy(
                    b.h_out.at[q], b.h_in.at[plane, chip], at(dp, dz)
                )
    b.h_in[plane, chip] = b.h_out[chip]

    for s in range(8):
        b.vn[s] = turned(b.vt[s]).astype(BF)
    for s in range(4):
        b.qn[s] = turned(b.qt[s])[:, 0:64].astype(BF)
    l_f2.wait()
    for n in range(4):
        cols = slice(n * 256, (n + 1) * 256)
        b.dact[:, cols] = dot_nt(b.mg[...], b.f2[cols])
    l_wo.wait()
    for one in sent_wo2.values():
        net.arrived(one)
    sent_wo3 = [
        net.copy(b.wo.at[planes[dz], :, core], b.wo.at[planes[dz], :, core], mate)
        for dz in (1, 2, 3)
    ]

    for dz in range(4):
        for dp in range(4):
            if dp or dz:
                net.arrived(sent_h[dp, dz])
        if dz:
            net.arrived(sent_wo3[dz - 1])
        left = turned(b.h_in[planes[dz]].reshape(256, rows)).astype(BF)
        right = b.wo[planes[dz]].reshape(256, width)
        if dz:
            b.attn[...] += dot(left, right)
        else:
            b.attn[...] = dot(left, right)
    sent_hx = net.copy(b.h_in.at[plane, pl.ds(2 * other, 2)], b.h_mate, mate)

    net.arrived(sent_a)
    sent_all += [
        net.copy(b.a_all.at[chip, other], b.a_all.at[chip, other], at(dp, 0)) for dp in (3, 1, 2)
    ]

    def second_norm(which):
        value = b.tok[which].astype(F32) + per_token(0, which) * b.attn[which]
        b.hid[which] = value
        normed, _ = norm_rows(value)
        value = (normed * (1.0 + per_token(3, which)) + per_token(5, which)).astype(BF)
        b.b[0, which] = value[:, :half]
        b.b[1, which] = value[:, half:]

    chunks(second_norm)
    l_f1.wait()
    for n in range(4):
        cols = slice(n * 256, (n + 1) * 256)
        up = dot(b.b[0], b.f1[:half, cols]) + dot(b.b[1], b.f1[half:, cols])
        square = up * up
        bent = jnp.tanh(GELU_A * up * (1.0 + GELU_B * square))
        gate = 0.5 * (1.0 + bent)
        slope = gate + 0.5 * up * (1.0 - bent * bent) * (GELU_A * (1.0 + 3.0 * GELU_B * square))
        b.act[n // 2, :, (n % 2) * 256 : (n % 2 + 1) * 256] = (up * gate).astype(BF)
        b.ug[:, cols] = (b.dact[:, cols] * slope).astype(BF)
    for n in range(4):
        cols = slice(n * 256, (n + 1) * 256)
        value = dot_nt(b.ug[...], b.f1[cols])
        b.bg_out[:, :, cols] = value.astype(BF).reshape(4, own, 256)
    sent_bg = [
        net.copy(b.bg_out.at[planes[dz]], b.bg_in.at[dz - 1], at(0, dz)) for dz in (3, 2, 1)
    ]

    ways = ((0, 1, 2), (1, 2, 1))

    def scatter(blocks, arrived):
        return [
            net.copy(blocks.at[chips[which], way], arrived.at[way, n], at(first, 0))
            for n, pick in ((1, 3), (0, None))
            for way, first, _ in ways
            for which in (pick or first,)
        ]

    def scatter_on(sent, blocks, arrived):
        for one in sent:
            net.arrived(one)
        for way, _, then in ways:
            total = blocks[chips[then], way].astype(F32) + arrived[way, 1].astype(F32)
            blocks[chips[then], way] = total.astype(BF)
        return [
            net.copy(blocks.at[chips[then], way], arrived.at[way, 2], at(then, 0))
            for way, _, then in ways
        ]

    def gather(sent, blocks, arrived, total, target):
        for one in sent:
            net.arrived(one)
        for way, _, _ in ways:
            total[way] = (
                blocks[chip, way].astype(F32)
                + arrived[way, 0].astype(F32)
                + arrived[way, 2].astype(F32)
            ).astype(BF)
        load(total, target.at[core, chip])
        net.copy(total, target.at[core, chip], mate)
        return [
            net.copy(total.at[way], target.at[core, chip, way], at(dp, 0))
            for way, dp in ((0, 2), (1, 1), (0, 1), (1, 2))
        ]

    def gather_on(sent, target):
        for one in sent[:2]:
            net.arrived(one)
        return [
            net.copy(
                target.at[core, chips[then], way], target.at[core, chips[then], way], at(first, 0)
            )
            for way, first, then in ways
        ]

    sent_x = [
        net.copy(b.act.at[other], b.act_in, mate),
        net.copy(b.b.at[other], b.b_in, mate),
        net.copy(b.ug, b.ug_in, mate),
    ]
    b.left[0] = turned(b.act[core]).astype(BF)
    net.arrived(sent_mg)
    net.arrived(sent_x[0])
    b.left[1] = turned(b.act_in[...]).astype(BF)
    for n in range(4):
        some = slice(n * 128, (n + 1) * 128)
        value = dot(b.left[0, some], b.mg[...]) + dot(b.left[1, some], b.mg_in[...])
        b.g2_out[n] = value.astype(BF).reshape(2, 64, width)
    sent_g2 = scatter(b.g2_out, b.g2_in)
    b.left[0] = turned(b.b[core]).astype(BF)
    net.arrived(sent_x[1])
    b.left[1] = turned(b.b_in[...]).astype(BF)
    net.arrived(sent_x[2])
    for n in range(4):
        some = slice(n * 128, (n + 1) * 128)
        value = dot(b.left[0, some], b.ug[...]) + dot(b.left[1, some], b.ug_in[...])
        b.g1_out[n] = value.astype(BF).reshape(2, 64, width)
    sent_g1 = scatter(b.g1_out, b.g1_in)
    for n in range(4):
        cols = slice(n * 256, (n + 1) * 256)
        value = dot(b.act[0], b.f2[:half, cols]) + dot(b.act[1], b.f2[half:, cols])
        b.mo_out[:, :, cols] = value.astype(BF).reshape(4, own, 256)

    def summed(sent, kept, arrived):
        for one in sent:
            net.arrived(one)
        total = kept.astype(F32)
        for k in range(3):
            total = total + arrived[k].astype(F32)
        return total

    def mode_sums(k, value):
        high = value.astype(BF)
        low = (value - high.astype(F32)).astype(BF)
        picked = turned(b.pick[mine])[0:ITEM_ROWS].astype(BF)
        value = (dot(picked, high) + dot(picked, low))[0:8]
        b.ms[0, k * 8 : (k + 1) * 8] = value[:, :half]
        b.ms[1, k * 8 : (k + 1) * 8] = value[:, half:]

    def plane_scatter(blocks, arrived, far):
        far_sent = net.copy(blocks.at[planes[3]], far, at(0, 1), outer, inner)
        sent = [
            net.copy(blocks.at[planes[2]], arrived.at[1], at(0, 2), outer, inner),
            net.copy(blocks.at[planes[3]], arrived.at[2], at(0, 3), inner, inner),
            net.copy(blocks.at[planes[1]], arrived.at[0], at(0, 1)),
        ]

        @pl.when(outer)
        def _():
            arrived[2] = jnp.zeros(arrived.shape[1:], BF)

        return sent, far_sent

    def plane_scatter_on(far_sent, blocks, arrived, far):
        net.arrived(far_sent)

        @pl.when(inner)
        def _():
            total = blocks[planes[2]].astype(F32) + far[...].astype(F32)
            blocks[planes[2]] = total.astype(BF)

        return net.copy(blocks.at[planes[2]], arrived.at[1], at(0, 2), inner, outer)

    def plane_gather(source, target):
        return [
            net.copy(source, target.at[plane], at(0, 2)),
            net.copy(source, target.at[plane], at(0, 3), inner, inner),
            net.copy(source, target.at[plane], at(0, 1)),
        ]

    def plane_gather_on(sent, target):
        net.arrived(sent[0])
        return net.copy(target.at[planes[2]], target.at[planes[2]], at(0, 1), inner, outer)

    b_grad = summed(sent_bg, b.bg_out[plane], b.bg_in)
    normed, inverse = norm_rows(b.hid[mine])
    h_grad = b.cot[mine].astype(F32) + norm_back(
        b_grad * (1.0 + per_token(3, mine)), normed, inverse
    )
    b.hg[...] = h_grad
    attn_grad = (per_token(0, mine) * h_grad).astype(BF)
    b.ag[plane] = attn_grad
    for n in range(4):
        value = dot_nt(attn_grad, b.wo[n].reshape(256, width)).astype(BF)
        for h in range(4):
            some = value[:, h * 64 : (h + 1) * 64]
            b.do_out[n, h] = jnp.concatenate([some[: own // 2], some[own // 2 :]], axis=1)
    sent_do = {
        (dp, dz): net.copy(
            b.do_out.at[planes[dz], chips[dp]], b.do_in.at[chip, plane], at(dp, dz)
        )
        for dp, dz in reversed(offsets)
    }
    b.do_in[chip, plane] = b.do_out[plane, chip]
    mode_sums(0, h_grad * b.attn[mine])
    mode_sums(3, b_grad * normed)
    mode_sums(5, b_grad)
    sent_g2 = scatter_on(sent_g2, b.g2_out, b.g2_in)
    sent_g1 = scatter_on(sent_g1, b.g1_out, b.g1_in)

    for one in sent_do.values():
        net.arrived(one)
    sent_mo, far_mo = plane_scatter(b.mo_out, b.mo_in, b.mo_far)
    sent_ag = plane_gather(b.ag.at[plane], b.ag)
    for s in range(4):
        for n in range(4):
            both = b.do_in[s, n]
            b.dn[s, n * own : n * own + own // 2] = both[:, 0:64]
            b.dn[s, n * own + own // 2 : (n + 1) * own] = both[:, 64:128]
        value = turned(b.dn[s])
        b.dt[s] = value.astype(BF)
        b.delta[s] = jnp.sum(value * b.heads[s], axis=0, keepdims=True)
        b.dn[s] = (value * b.share[s]).T.astype(BF)
        b.dq[s] = jnp.zeros((64, rows), F32)

    def attend_back(s, carry):
        keys, values = b.kt[s, 0:64], b.vn[s]
        key_grad = jnp.zeros((rows, 64), F32)
        value_grad = jnp.zeros((rows, 64), F32)
        for q in range(4):
            terms = b.terms[q, s]
            pull = (dot(values, b.dt[q]) - b.delta[q]) * b.share[q]
            low = (pull * terms.astype(F32)).astype(BF)
            b.dq[q] += dot(keys, low)
            key_grad = key_grad + dot(low, b.qn[q])
            value_grad = value_grad + dot(terms, b.dn[q])
        b.dkv[s] = jnp.concatenate([key_grad * 0.125, value_grad], axis=1).T
        return carry

    lax.fori_loop(4, 8, attend_back, 0)
    sent_dkv = net.copy(b.dkv.at[4:8], b.dkv_in, mate)
    sent_mo.append(plane_scatter_on(far_mo, b.mo_out, b.mo_in, b.mo_far))
    sent_g2b = gather(sent_g2, b.g2_out, b.g2_in, b.g2, gf2_o)
    sent_g1b = gather(sent_g1, b.g1_out, b.g1_in, b.g1, gf1_o)
    lax.fori_loop(0, 4, attend_back, 0)
    net.arrived(sent_dkv)
    for s in range(4):
        b.dx_out[s, 0:64] = (b.dq[s] * 0.125).astype(BF)
        b.dx_out[s, 64:192] = (b.dkv[s] + b.dkv_in[s]).astype(BF)
    sent_dx = [
        net.copy(b.dx_out.at[chips[dp]], b.dx_in.at[chip], at(dp, 0)) for dp in (3, 1, 2)
    ]
    sent_dxm = net.copy(b.dx_out, b.dx_mate, mate)
    b.dx_in[chip] = b.dx_out[chip]

    sent_ag.append(plane_gather_on(sent_ag, b.ag))

    for one in sent_all:
        net.arrived(one)
    value = jnp.zeros((192, half), F32)
    for s in range(4):
        value = value + dot(b.dx_out[s], b.a_all[s, core])
    net.arrived(sent_dxm)
    for s in range(4):
        value = value + dot(b.dx_mate[s], b.a_all[s, other])
    b.gq[...] = value.astype(BF)
    for one in sent_dx:
        net.arrived(one)
    for k in range(3):
        value = b.dx_in[:, k * 64 : (k + 1) * 64].reshape(256, rows)
        b.dx[k] = turned(value).astype(BF)
    for n in range(4):
        cols = slice(n * 256, (n + 1) * 256)
        value = dot_nt(b.dx[0], b.wq[0, cols])
        value = value + dot_nt(b.dx[1], b.wq[1, cols])
        value = value + dot_nt(b.dx[2], b.wq[2, cols])
        b.xg_out[:, :, cols] = value.astype(BF).reshape(4, own, 256)
    sent_xg = [
        net.copy(b.xg_out.at[planes[dz]], b.xg_in.at[dz - 1], at(0, dz)) for dz in (3, 2, 1)
    ]
    sent_gq = [net.copy(b.gq, gqkv_o.at[chip, core], at(dp, 0)) for dp in (3, 1, 2)]
    load(b.gq, gqkv_o.at[chip, core])
    net.copy(b.gq, gqkv_o.at[chip, core], mate)

    sent_g2b += gather_on(sent_g2b, gf2_o)
    sent_g1b += gather_on(sent_g1b, gf1_o)

    mlp_out = summed(sent_mo, b.mo_out[plane], b.mo_in)
    b.out[...] = (b.hid[mine] + per_token(1, mine) * mlp_out).astype(BF)
    sent_out = plane_gather(b.out, out_o)
    load(b.out, out_o.at[plane])
    mode_sums(1, b.cot[mine].astype(F32) * mlp_out)

    for one in sent_ag[1:]:
        net.arrived(one)
    sent_agm = net.copy(b.ag, b.ag_in, mate)
    value = dot(
        b.h_in[plane, pl.ds(2 * core, 2)].reshape(128, rows), b.ag[...].reshape(rows, width)
    )
    net.arrived(sent_hx)
    net.arrived(sent_agm)
    value = value + dot(b.h_mate[...].reshape(128, rows), b.ag_in[...].reshape(rows, width))
    b.go_out[...] = value.astype(BF).reshape(4, 32, width)
    sent_go = [
        net.copy(b.go_out.at[chips[dp]], b.go_in.at[dp - 1], at(dp, 0)) for dp in (3, 1, 2)
    ]

    plane_gather_on(sent_out, out_o)

    a_grad = summed(sent_xg, b.xg_out[plane], b.xg_in)
    normed, inverse = norm_rows(b.tok[mine].astype(F32))
    mode_sums(2, a_grad * normed)
    mode_sums(4, a_grad)
    sent_ms = net.copy(b.ms.at[other], b.ms_in, mate)
    value = b.hg[...] + norm_back(a_grad * (1.0 + per_token(2, mine)), normed, inverse)
    b.dtok[...] = value.astype(BF)
    net.arrived(sent_ms)
    b.m1[...] = (b.ms[core] + b.ms_in[...]).astype(BF)
    sent_m1 = [net.copy(b.m1, b.m1_in.at[dz - 1], at(0, dz)) for dz in (3, 2, 1)]
    sent_dt = plane_gather(b.dtok, dtok_o)
    load(b.dtok, dtok_o.at[plane])

    b.go[...] = summed(sent_go, b.go_out[chip], b.go_in).astype(BF)
    sent_gob = [net.copy(b.go, gout_o.at[core, chip], at(dp, 0)) for dp in (3, 1, 2)]
    load(b.go, gout_o.at[core, chip])
    net.copy(b.go, gout_o.at[core, chip], mate)
    b.m2[...] = summed(sent_m1, b.m1[...], b.m1_in).astype(BF)
    sent_m2 = [net.copy(b.m2, b.m2_in.at[dp - 1], at(dp, 0)) for dp in (3, 1, 2)]
    b.m3[...] = summed(sent_m2, b.m2[...], b.m2_in)
    net.copy(b.m3, mode_o.at[core], mate)
    load(b.m3, mode_o.at[core])
    load(b.cond, cond_o)
    plane_gather_on(sent_dt, dtok_o)

    for sent, array in ((sent_g2b, gf2_o), (sent_g1b, gf1_o)):
        for one in sent[2:]:
            net.arrived(one)
        for dp in (1, 2, 3):
            where = (core, chips[dp])
            net.copy(array.at[where], array.at[where], mate)
    for sent, array in ((sent_gq, gqkv_o), (sent_gob, gout_o)):
        for one, dp in zip(sent, (3, 1, 2), strict=True):
            net.arrived(one)
            where = (chips[dp], core) if array is gqkv_o else (core, chips[dp])
            net.copy(array.at[where], array.at[where], mate)
    net.finish()
    for one in loads[first_store:]:
        one.wait()


def buffers(dims):
    rows, width, part, hidden, items, classes = dims
    own, half = rows // 4, width // 2
    return dict(
        tok=((rows, width), BF),
        cot=((rows, width), BF),
        table=((classes, width), BF),
        ada=((COMPONENTS, width, width), BF),
        wq=((3, width, part), BF),
        wo=((4, 4, 2, 32, width), BF),
        f1=((width, hidden), BF),
        f2=((hidden, width), BF),
        modes=((COMPONENTS, 3 * ITEM_ROWS, width), BF),
        pick=((rows, 3 * ITEM_ROWS), BF),
        cond=((ITEM_ROWS, width), F32),
        a=((2, rows, half), BF),
        a_all=((4, 2, rows, half), BF),
        q_out=((4, 192, rows), BF),
        q_in=((4, 192, rows), BF),
        k_in=((4, 128, rows), BF),
        kt=((8, 128, rows), BF),
        ka=((8, rows, 128), BF),
        vt=((8, 64, rows), BF),
        vn=((8, rows, 64), BF),
        qt=((4, 128, rows), BF),
        qn=((4, rows, 64), BF),
        scores=((8, rows, rows), F32),
        terms=((4, 8, rows, rows), BF),
        share=((4, 1, rows), F32),
        heads=((4, 64, rows), F32),
        h_out=((4, 64, rows), BF),
        h_in=((4, 4, 64, rows), BF),
        h_mate=((2, 64, rows), BF),
        attn=((rows, width), F32),
        hid=((rows, width), F32),
        b=((2, rows, half), BF),
        b_in=((rows, half), BF),
        act=((2, rows, half), BF),
        act_in=((rows, half), BF),
        mg=((rows, width), BF),
        mg_in=((rows, width), BF),
        ug=((rows, hidden), BF),
        ug_in=((rows, hidden), BF),
        dact=((rows, hidden), F32),
        left=((2, half, rows), BF),
        bg_out=((4, own, width), BF),
        bg_in=((3, own, width), BF),
        mo_out=((4, own, width), BF),
        mo_in=((3, own, width), BF),
        mo_far=((own, width), BF),
        xg_out=((4, own, width), BF),
        xg_in=((3, own, width), BF),
        g1_out=((4, 2, 64, width), BF),
        g1_in=((2, 3, 64, width), BF),
        g1=((2, 64, width), BF),
        g2_out=((4, 2, 64, width), BF),
        g2_in=((2, 3, 64, width), BF),
        g2=((2, 64, width), BF),
        hg=((own, width), F32),
        ag=((4, own, width), BF),
        ag_in=((4, own, width), BF),
        do_out=((4, 4, own // 2, 128), BF),
        do_in=((4, 4, own // 2, 128), BF),
        dn=((4, rows, 64), BF),
        dt=((4, 64, rows), BF),
        delta=((4, 1, rows), F32),
        dq=((4, 64, rows), F32),
        dkv=((8, 128, rows), F32),
        dkv_in=((4, 128, rows), F32),
        dx_out=((4, 192, rows), BF),
        dx_mate=((4, 192, rows), BF),
        dx_in=((4, 192, rows), BF),
        dx=((3, rows, part), BF),
        gq=((192, half), BF),
        out=((own, width), BF),
        dtok=((own, width), BF),
        go_out=((4, 32, width), BF),
        go_in=((3, 32, width), BF),
        go=((32, width), BF),
        ms=((2, 48, half), F32),
        ms_in=((48, half), F32),
        m1=((48, half), BF),
        m1_in=((3, 48, half), BF),
        m2=((48, half), BF),
        m2_in=((3, 48, half), BF),
        m3=((48, half), F32),
    )


def finish_kernel(
    cls_s, ada_h, out_i, dtok_i, gqkv_i, gout_i, gf1_i, gf2_i, mode_i, cond_i,
    out_o, dtok_o, table_o, ada_o, qkv_o, wout_o, f1_o, f2_o, ada_v, sems,
):
    step, last = pl.program_id(0), pl.num_programs(0) - 1
    plane = lax.axis_index("head")
    part = table_o.shape[1]
    mine = pl.ds(pl.multiple_of(plane * part, part), part)
    fetch = [
        pltpu.make_async_copy(ada_h.at[k, mine], ada_v.at[k], sems.at[k]) for k in range(COMPONENTS)
    ]

    @pl.when(step == 0)
    def _():
        for one in fetch:
            one.start()

    out_o[...] = out_i[0]
    dtok_o[...] = dtok_i[0]
    wout_o[...] = gout_i[0, 0].astype(F32)
    f1_o[...] = gf1_i[0, 0].astype(F32).reshape(f1_o.shape)
    f2_o[...] = gf2_i[0, 0].astype(F32).reshape(f2_o.shape)
    for k in range(3):
        value = gqkv_i[:, 0, k * 64 : (k + 1) * 64].astype(F32).reshape(part, 128)
        qkv_o[k] = value.T
    cond = cond_i[:, pl.ds(pl.multiple_of(step * 128, 128), 128)]
    cond_low = (cond / (1.0 + jnp.exp(-cond)))[0:8]
    low = jnp.concatenate([cond_low, cond_low], axis=0).astype(BF)
    side = pl.ds(pl.multiple_of(lax.rem(plane, 2) * part, part), part)
    for k in range(COMPONENTS):
        value = mode_i[lax.div(plane, 2), k * 8 : (k + 1) * 8, side]
        high = value.astype(BF).astype(F32)
        both = jnp.concatenate([high, value - high], axis=0).astype(BF)
        ada_o[k] = dot_tn(low, both)

    @pl.when(step == last)
    def _():
        cond_grad = jnp.zeros((16, part), F32)
        half = mode_i.shape[2]
        for k in range(COMPONENTS):
            fetch[k].wait()
            for n in range(2):
                value = mode_i[n, k * 8 : (k + 1) * 8]
                high = value.astype(BF).astype(F32)
                both = jnp.concatenate([high, value - high], axis=0).astype(BF)
                cond_grad = cond_grad + dot_nt(both, ada_v[k, :, n * half : (n + 1) * half])
        own = cond_i[0:8, mine]
        gate = 1.0 / (1.0 + jnp.exp(-own))
        grad = (cond_grad[0:8] + cond_grad[8:16]) * gate * (1.0 + own * (1.0 - gate))
        spot = lax.broadcasted_iota(jnp.int32, table_o.shape, 0)
        total = jnp.zeros(table_o.shape, F32)
        for i in range(cls_s.shape[0]):
            total = total + jnp.where(spot == cls_s[i], grad[i : i + 1], 0.0)
        table_o[...] = total


def finish(
    class_ids, w_ada, output, d_tokens, qkv_sum, out_sum, fc1_sum, fc2_sum, mode_grad, cond, classes
):
    steps = 8
    own, width = output.shape[1:]
    half, part, hidden = width // 2, width // 4, steps * 128
    rows = own * 4
    anywhere = pl.BlockSpec(memory_space=pl.ANY)
    smem = pl.BlockSpec(memory_space=pltpu.SMEM)
    few = pl.BlockSpec((1, own // 2, width), lambda i: (i // 2, i % 2, 0))
    table, ada, qkv, out, fc1, fc2 = (
        (classes, part),
        (COMPONENTS, width, part),
        (3, width, part),
        (part, width),
        (width, hidden),
        (hidden, width),
    )
    output, d_tokens, table, ada, qkv, out, fc1, fc2 = pl.pallas_call(
        finish_kernel,
        grid=(steps,),
        out_shape=[
            jax.ShapeDtypeStruct((rows, width), BF),
            jax.ShapeDtypeStruct((rows, width), BF),
        ]
        + [jax.ShapeDtypeStruct(shape, F32) for shape in (table, ada, qkv, out, fc1, fc2)],
        in_specs=[
            smem,
            anywhere,
            few,
            few,
            pl.BlockSpec((4, 1, 192, half // 4), lambda i: (0, i // 4, 0, i % 4)),
            pl.BlockSpec((1, 1, 32, width), lambda i: (i // 4, i % 4, 0, 0)),
            pl.BlockSpec((1, 1, 2, 64, hidden), lambda i: (i // 4, i % 4, 0, 0, 0)),
            pl.BlockSpec((1, 1, 2, 64, width), lambda i: (i // 4, i % 4, 0, 0, 0)),
            pl.BlockSpec((2, 48, half), lambda i: (0, 0, 0)),
            pl.BlockSpec((ITEM_ROWS, width), lambda i: (0, 0)),
        ],
        out_specs=[
            pl.BlockSpec((rows // steps, width), lambda i: (i, 0)),
            pl.BlockSpec((rows // steps, width), lambda i: (i, 0)),
            pl.BlockSpec((classes, part), lambda i: (0, 0)),
            pl.BlockSpec((COMPONENTS, 128, part), lambda i: (0, i, 0)),
            pl.BlockSpec((3, 128, part), lambda i: (0, i, 0)),
            pl.BlockSpec((32, width), lambda i: (i, 0)),
            pl.BlockSpec((128, hidden), lambda i: (i, 0)),
            pl.BlockSpec((128, width), lambda i: (i, 0)),
        ],
        scratch_shapes=[
            pltpu.VMEM((COMPONENTS, part, width), BF),
            pltpu.SemaphoreType.DMA((COMPONENTS,)),
        ],
        compiler_params=pltpu.CompilerParams(vmem_limit_bytes=VMEM_BYTES),
    )(
        class_ids, w_ada, output, d_tokens, qkv_sum, out_sum, fc1_sum, fc2_sum, mode_grad, cond
    )
    return output, d_tokens, table, ada, qkv.transpose(1, 0, 2), out, fc1, fc2


def on_block(
    tokens,
    class_ids,
    slot_item,
    slot_scale,
    class_table,
    w_ada,
    w_qkv,
    w_out,
    w_fc1,
    w_fc2,
    cotangent,
):
    rows, width = tokens.shape
    part, hidden = w_qkv.shape[2], w_fc1.shape[1]
    items, classes = class_ids.shape[0], class_table.shape[0]
    own, half = rows // 4, width // 2
    dims = (rows, width, part, hidden, items, classes)
    scratch = [pltpu.VMEM(shape, dtype) for shape, dtype in buffers(dims).values()]
    anywhere = pl.BlockSpec(memory_space=pl.ANY)
    vmem = pl.BlockSpec(memory_space=pltpu.VMEM)
    smem = pl.BlockSpec(memory_space=pltpu.SMEM)
    output, d_tokens, qkv_sum, out_sum, fc1_sum, fc2_sum, mode_grad, cond = pl.pallas_call(
        functools.partial(block_kernel, dims),
        out_shape=[
            jax.ShapeDtypeStruct((4, own, width), BF),
            jax.ShapeDtypeStruct((4, own, width), BF),
            jax.ShapeDtypeStruct((4, 2, 192, half), BF),
            jax.ShapeDtypeStruct((2, 4, 32, width), BF),
            jax.ShapeDtypeStruct((2, 4, 2, 64, width), BF),
            jax.ShapeDtypeStruct((2, 4, 2, 64, width), BF),
            jax.ShapeDtypeStruct((2, 48, half), F32),
            jax.ShapeDtypeStruct((ITEM_ROWS, width), F32),
        ],
        in_specs=[anywhere, smem, vmem, vmem] + [anywhere] * 7,
        out_specs=[anywhere] * 8,
        scratch_shapes=[
            pltpu.SemaphoreType.DMA((COPIES,)),
            pltpu.SemaphoreType.DMA((COPIES,)),
            pltpu.SemaphoreType.DMA((32,)),
            *scratch,
        ],
        compiler_params=pltpu.CompilerParams(
            collective_id=0, has_side_effects=True, vmem_limit_bytes=VMEM_BYTES
        ),
        cost_estimate=pl.CostEstimate(
            flops=10_000_000_000, bytes_accessed=40_000_000, transcendentals=3_000_000
        ),
    )(
        tokens,
        class_ids,
        slot_item.reshape(8, 1, rows),
        slot_scale.reshape(8, 1, rows),
        class_table,
        w_ada,
        w_qkv.transpose(1, 0, 2),
        w_out.reshape(4, 2, 32, width),
        w_fc1,
        w_fc2,
        cotangent,
    )
    return finish(
        class_ids, w_ada, output, d_tokens, qkv_sum, out_sum, fc1_sum, fc2_sum, mode_grad, cond,
        classes,
    )


def fits(mesh):
    return mesh.shape["tok"] == 8 and mesh.shape["head"] == 4


def layer_norm(values):
    centre = jnp.mean(values, axis=-1, keepdims=True)
    shifted = values - centre
    spread = jnp.mean(shifted * shifted, axis=-1, keepdims=True)
    return shifted * lax.rsqrt(spread + EPS)


def modulate(values, scale_in, shift_in):
    return layer_norm(values) * (1.0 + scale_in) + shift_in


def pair_scores(queries, key_block, query_item, key_item, query_scale, key_scale):
    scores = (
        jnp.einsum("qhd,khd->hqk", queries, key_block, preferred_element_type=jnp.float32) * 0.125
    )
    allowed = (
        (query_item[:, None] == key_item[None, :]) & (key_scale[None, :] <= query_scale[:, None])
    )[None]
    return (jnp.where(allowed, scores, -1e30), allowed)


def on_device(
    tokens,
    class_ids,
    slot_item,
    slot_scale,
    class_table,
    w_ada,
    w_qkv,
    w_out,
    w_fc1,
    w_fc2,
    cotangent,
):
    tok_rows, full_width = tokens.shape
    slot_count = slot_item.shape[0]
    item_count = class_ids.shape[0]
    class_count = class_table.shape[0]
    local_width = w_qkv.shape[2]
    local_heads = local_width // HEAD_DIM
    anchor = lax.axis_index("tok") * tok_rows
    first_col = lax.axis_index("head") * local_width
    my_item = lax.dynamic_slice_in_dim(slot_item, anchor, tok_rows)
    my_scale = lax.dynamic_slice_in_dim(slot_scale, anchor, tok_rows)
    class_pick = (class_ids[:, None] == jnp.arange(class_count, dtype=jnp.int32)[None, :]).astype(
        jnp.bfloat16
    )
    cond = jnp.dot(class_pick, class_table, preferred_element_type=jnp.float32)
    silu_cond, silu_back = jax.vjp(jax.nn.silu, cond)
    cond_low = silu_cond.astype(jnp.bfloat16)
    modes = jnp.einsum("id,cde->ice", cond_low, w_ada, preferred_element_type=jnp.float32)
    item_pick = (my_item[:, None] == jnp.arange(item_count, dtype=jnp.int32)[None, :]).astype(
        jnp.float32
    )
    per_token = jnp.dot(
        item_pick, modes.reshape(item_count, 6 * full_width), precision=HIGH
    ).reshape(tok_rows, 6, full_width)
    gamma_one = per_token[:, 0]
    gamma_two = per_token[:, 1]
    scale_one = per_token[:, 2]
    scale_two = per_token[:, 3]
    shift_one = per_token[:, 4]
    shift_two = per_token[:, 5]
    tok_float = tokens.astype(jnp.float32)
    a_pre, a_back = jax.vjp(modulate, tok_float, scale_one, shift_one)
    a_low = a_pre.astype(jnp.bfloat16)
    qkv_low = jnp.einsum("td,dce->tce", a_low, w_qkv, preferred_element_type=jnp.float32).astype(
        jnp.bfloat16
    )
    queries = qkv_low[:, 0]
    key_own = qkv_low[:, 1]
    value_own = qkv_low[:, 2]
    query_heads = queries.reshape(tok_rows, local_heads, HEAD_DIM)
    key_all, value_all = (
        lax.all_gather(key_own, "tok", axis=0, tiled=True),
        lax.all_gather(value_own, "tok", axis=0, tiled=True),
    )
    block_rows = math.gcd(slot_count, 2048)
    blocks = slot_count // block_rows
    key_blocks = key_all.reshape(blocks, block_rows, local_heads, HEAD_DIM)
    value_blocks = value_all.reshape(blocks, block_rows, local_heads, HEAD_DIM)
    item_blocks = slot_item.reshape(blocks, block_rows)
    scale_blocks = slot_scale.reshape(blocks, block_rows)
    key_wanted = jnp.min(scale_blocks, axis=1) <= jnp.max(my_scale)

    def first_pass(running, inputs):
        key_block, item_block, scale_block, wanted = inputs

        def first_compute_block(state_now):
            scores, allowed = pair_scores(
                query_heads, key_block, my_item, item_block, my_scale, scale_block
            )
            new_peak = jnp.maximum(state_now[0], jnp.max(scores, axis=2))
            terms = jnp.where(allowed, jnp.exp(scores - new_peak[:, :, None]), 0.0)
            return (
                new_peak,
                state_now[1] * jnp.exp(state_now[0] - new_peak) + jnp.sum(terms, axis=2),
            )

        return (lax.cond(wanted, first_compute_block, lambda state_now: state_now, running), None)

    initial = (
        jnp.full((local_heads, tok_rows), -1e30, jnp.float32),
        jnp.zeros((local_heads, tok_rows), jnp.float32),
    )
    (row_peak, summed), _ = lax.scan(
        first_pass, initial, (key_blocks, item_blocks, scale_blocks, key_wanted)
    )
    log_total = row_peak + jnp.log(summed)

    def second_pass(running, inputs):
        key_block, value_block, item_block, scale_block, wanted = inputs

        def second_compute_block(total_now):
            scores, allowed = pair_scores(
                query_heads, key_block, my_item, item_block, my_scale, scale_block
            )
            rounded = jnp.where(allowed, jnp.exp(scores - log_total[:, :, None]), 0.0).astype(
                jnp.bfloat16
            )
            return total_now + jnp.einsum(
                "hqk,khd->qhd", rounded, value_block, preferred_element_type=jnp.float32
            )

        return (lax.cond(wanted, second_compute_block, lambda total_now: total_now, running), None)

    heads_out, _ = lax.scan(
        second_pass,
        jnp.zeros((tok_rows, local_heads, HEAD_DIM), jnp.float32),
        (key_blocks, value_blocks, item_blocks, scale_blocks, key_wanted),
    )
    heads_low = heads_out.reshape(tok_rows, local_width).astype(jnp.bfloat16)
    attn_out = lax.psum(
        jnp.dot(heads_low, w_out, preferred_element_type=jnp.float32).astype(jnp.bfloat16), "head"
    ).astype(jnp.float32)
    hidden = tok_float + gamma_one * attn_out
    b_pre, b_back = jax.vjp(modulate, hidden, scale_two, shift_two)
    b_low = b_pre.astype(jnp.bfloat16)
    up_proj = jnp.dot(b_low, w_fc1, preferred_element_type=jnp.float32)
    act_pre, act_back = jax.vjp(lambda values: jax.nn.gelu(values, approximate=True), up_proj)
    act_low = act_pre.astype(jnp.bfloat16)
    mlp_out = lax.psum(
        jnp.dot(act_low, w_fc2, preferred_element_type=jnp.float32).astype(jnp.bfloat16), "head"
    ).astype(jnp.float32)
    output = (hidden + gamma_two * mlp_out).astype(jnp.bfloat16)
    out_grad = cotangent.astype(jnp.float32)
    mlp_grad = (gamma_two * out_grad).astype(jnp.bfloat16)
    fc2_weight_grad = jnp.einsum("tf,td->fd", act_low, mlp_grad, preferred_element_type=jnp.float32)
    act_grad = jnp.einsum("td,fd->tf", mlp_grad, w_fc2, preferred_element_type=jnp.float32)
    up_grad = act_back(act_grad)[0].astype(jnp.bfloat16)
    fc1_weight_grad = jnp.einsum("td,tf->df", b_low, up_grad, preferred_element_type=jnp.float32)
    b_grad = lax.psum(
        jnp.einsum("tf,df->td", up_grad, w_fc1, preferred_element_type=jnp.float32).astype(
            jnp.bfloat16
        ),
        "head",
    ).astype(jnp.float32)
    hidden_part, scale_two_grad, shift_two_grad = b_back(b_grad)
    hidden_grad = out_grad + hidden_part
    attn_grad = (gamma_one * hidden_grad).astype(jnp.bfloat16)
    out_weight_grad = jnp.einsum(
        "tf,te->fe", heads_low, attn_grad, preferred_element_type=jnp.float32
    )
    grad_low = jnp.einsum("te,fe->tf", attn_grad, w_out, preferred_element_type=jnp.float32).astype(
        jnp.bfloat16
    )
    grad_heads = grad_low.reshape(tok_rows, local_heads, HEAD_DIM)
    delta = jnp.einsum("qhd,qhd->hq", grad_heads.astype(jnp.float32), heads_out)

    def step_block(running, inputs):
        key_block, value_block, item_block, scale_block, wanted = inputs

        def step_compute_block(total_now):
            scores, allowed = pair_scores(
                query_heads, key_block, my_item, item_block, my_scale, scale_block
            )
            weights = jnp.where(allowed, jnp.exp(scores - log_total[:, :, None]), 0.0)
            weight_grad = jnp.einsum(
                "qhd,khd->hqk", grad_heads, value_block, preferred_element_type=jnp.float32
            )
            score_grad = (weights * (weight_grad - delta[:, :, None])).astype(jnp.bfloat16)
            total_now = (
                total_now
                + jnp.einsum(
                    "hqk,khd->qhd", score_grad, key_block, preferred_element_type=jnp.float32
                )
                * 0.125
            )
            key_term = (
                jnp.einsum(
                    "hqk,qhd->khd", score_grad, query_heads, preferred_element_type=jnp.float32
                )
                * 0.125
            )
            value_term = jnp.einsum(
                "hqk,qhd->khd",
                weights.astype(jnp.bfloat16),
                grad_heads,
                preferred_element_type=jnp.float32,
            )
            return (total_now, (key_term, value_term))

        def skip_block(total_now):
            nothing = jnp.zeros((block_rows, local_heads, HEAD_DIM), jnp.float32)
            return (total_now, (nothing, nothing))

        return lax.cond(wanted, step_compute_block, skip_block, running)

    query_grad, (key_terms, value_terms) = lax.scan(
        step_block,
        jnp.zeros((tok_rows, local_heads, HEAD_DIM), jnp.float32),
        (key_blocks, value_blocks, item_blocks, scale_blocks, key_wanted),
    )
    key_grad, value_grad = (
        lax.psum_scatter(
            key_terms.reshape(slot_count, local_width), "tok", scatter_dimension=0, tiled=True
        ),
        lax.psum_scatter(
            value_terms.reshape(slot_count, local_width), "tok", scatter_dimension=0, tiled=True
        ),
    )
    qkv_grad = jnp.stack(
        [query_grad.reshape(tok_rows, local_width), key_grad, value_grad], axis=1
    ).astype(jnp.bfloat16)
    qkv_weight_grad = jnp.einsum("td,tce->dce", a_low, qkv_grad, preferred_element_type=jnp.float32)
    a_grad = lax.psum(
        jnp.einsum("tce,dce->td", qkv_grad, w_qkv, preferred_element_type=jnp.float32).astype(
            jnp.bfloat16
        ),
        "head",
    ).astype(jnp.float32)
    tok_part, scale_one_grad, shift_one_grad = a_back(a_grad)
    d_tokens = (hidden_grad + tok_part).astype(jnp.bfloat16)
    token_modes = jnp.stack(
        [
            hidden_grad * attn_out,
            out_grad * mlp_out,
            scale_one_grad,
            scale_two_grad,
            shift_one_grad,
            shift_two_grad,
        ],
        axis=1,
    )
    mode_part = jnp.einsum(
        "ti,tf->if", item_pick, token_modes.reshape(tok_rows, 6 * full_width), precision=HIGH
    ).reshape(item_count, 6, full_width)
    qkv_sum, out_sum, fc1_sum, fc2_sum, mode_grad = lax.psum(
        (qkv_weight_grad, out_weight_grad, fc1_weight_grad, fc2_weight_grad, mode_part), "tok"
    )
    cond_grad = jnp.zeros((item_count, full_width), jnp.float32)
    for component in range(6):
        cond_grad = cond_grad + jnp.dot(
            mode_grad[:, component], w_ada[component].astype(jnp.float32).T, precision=HIGH
        )
    pre_grad = silu_back(cond_grad)[0]
    own_pre = lax.dynamic_slice_in_dim(pre_grad, first_col, local_width, 1)
    table_grad = jnp.einsum("ic,id->cd", class_pick.astype(jnp.float32), own_pre, precision=HIGH)
    own_modes = lax.dynamic_slice_in_dim(mode_grad, first_col, local_width, 2)
    ada_grad = jnp.einsum("id,ice->cde", cond_low.astype(jnp.float32), own_modes, precision=HIGH)
    return (output, d_tokens, table_grad, ada_grad, qkv_sum, out_sum, fc1_sum, fc2_sum)


def solution(mesh):
    placed = (
        P("tok", None),
        P(),
        P(),
        P(),
        P(),
        P(),
        P(None, None, "head"),
        P("head", None),
        P(None, "head"),
        P("head", None),
        P("tok", None),
    )
    return jax.shard_map(
        on_block if fits(mesh) else on_device,
        mesh=mesh,
        in_specs=placed,
        out_specs=(
            P("tok", None),
            P("tok", None),
            P(None, "head"),
            P(None, None, "head"),
            P(None, None, "head"),
            P("head", None),
            P(None, "head"),
            P("head", None),
        ),
        check_vma=False,
    )
```

```python
import functools
import math
import types

import jax
import jax.numpy as jnp
from jax import lax
from jax.experimental import pallas as pl
from jax.experimental.pallas import tpu as pltpu
from jax.sharding import PartitionSpec as P

HEAD_DIM = 64
COMPONENTS = 6


EPS = 1e-06
HIGH = lax.Precision.HIGHEST
BF = jnp.bfloat16
F32 = jnp.float32
MESH = pl.DeviceIdType.MESH
BARRED = -1e30
EIGHTH_LOG2 = 0.125 * math.log2(math.e)
GELU_A = math.sqrt(2.0 / math.pi)
GELU_B = 0.044715
COPIES = 160
VMEM_BYTES = 62 * 1024 * 1024
ITEM_ROWS = 16


def dot(left, right):
    return lax.dot_general(left, right, (((1,), (0,)), ((), ())), preferred_element_type=F32)


def dot_nt(left, right):
    return lax.dot_general(left, right, (((1,), (1,)), ((), ())), preferred_element_type=F32)


def dot_tn(left, right):
    return lax.dot_general(left, right, (((0,), (0,)), ((), ())), preferred_element_type=F32)


def turned(block):
    return block.astype(F32).T


def norm_rows(values):
    shifted = values - jnp.mean(values, axis=-1, keepdims=True)
    inverse = lax.rsqrt(jnp.mean(shifted * shifted, axis=-1, keepdims=True) + EPS)
    return shifted * inverse, inverse


def norm_back(grad, normed, inverse):
    along = jnp.mean(grad * normed, axis=-1, keepdims=True)
    return (grad - jnp.mean(grad, axis=-1, keepdims=True) - normed * along) * inverse


class Net:
    def __init__(self, send, arrive):
        self.send, self.arrive = send, arrive
        self.made, self.waited = [], []

    def copy(self, source, target, device, when=None, gets=None):
        k = len(self.made)
        one = pltpu.make_async_remote_copy(
            src_ref=source,
            dst_ref=target,
            send_sem=self.send.at[k],
            recv_sem=self.arrive.at[k],
            device_id=device,
            device_id_type=MESH,
        )
        self.made.append((one, when, gets))
        on_some(when, one.start)
        return k

    def arrived(self, k):
        one, _, gets = self.made[k]
        on_some(gets, one.wait_recv)
        self.waited.append(k)

    def finish(self):
        for k, (one, when, _) in enumerate(self.made):
            on_some(when, one.wait_send)
            if k not in self.waited:
                self.arrived(k)


def on_some(when, act):
    if when is None:
        act()
    else:
        pl.when(when)(act)


def block_kernel(dims, *refs):
    rows, width, part, hidden, items, classes = dims
    names = list(buffers(dims))
    (
        tok_h, cls_s, item_v, scale_v, table_h, ada_h, wq_h, wo_h, f1_h, f2_h, cot_h,
        out_o, dtok_o, gqkv_o, gout_o, gf1_o, gf2_o, mode_o, cond_o,
        send_sem, arrive_sem, load_sem, *scratch,
    ) = refs
    b = types.SimpleNamespace(**dict(zip(names, scratch, strict=True)))
    own = rows // 4
    half = width // 2
    net = Net(send_sem, arrive_sem)
    loads = []

    def load(source, target):
        one = pltpu.make_async_copy(source, target, load_sem.at[len(loads)])
        one.start()
        loads.append(one)
        return one

    group = lax.axis_index("tok")
    plane = lax.axis_index("head")
    core = lax.rem(group, 2)
    chip = lax.div(group, 2)
    col, line = lax.rem(chip, 2), lax.div(chip, 2)
    chips = [chip, line * 2 + 1 - col, (1 - line) * 2 + col, 3 - chip]
    planes = [
        plane,
        lax.div(plane, 2) * 2 + 1 - lax.rem(plane, 2),
        lax.rem(plane + 2, 4),
        3 - plane,
    ]
    other = 1 - core
    inner = (plane == 1) | (plane == 2)
    outer = (plane == 0) | (plane == 3)
    offsets = [(dp, dz) for dz in range(4) for dp in range(4) if dp or dz]

    def at(dp, dz):
        return (chips[dp] * 2 + core, planes[dz])

    mate = (chip * 2 + other, plane)
    mine = pl.ds(pl.multiple_of(plane * own, own), own)

    l_table = load(table_h, b.table)
    l_ada = {k: load(ada_h.at[k], b.ada.at[k]) for k in (2, 4)}
    l_tok = load(tok_h, b.tok)
    l_wq = load(wq_h, b.wq)
    barrier = pltpu.get_barrier_semaphore()
    for dp, dz in offsets:
        pl.semaphore_signal(barrier, inc=1, device_id=at(dp, dz), device_id_type=MESH)
    pl.semaphore_signal(barrier, inc=1, device_id=mate, device_id_type=MESH)

    spot = lax.rem(lax.broadcasted_iota(jnp.int32, (3 * ITEM_ROWS, rows), 0), ITEM_ROWS)
    picks = jnp.where(spot == item_v[group], 1.0, 0.0)
    b.pick[...] = picks.T.astype(BF)

    spot = lax.broadcasted_iota(jnp.int32, (ITEM_ROWS, classes), 0)
    label = lax.broadcasted_iota(jnp.int32, (ITEM_ROWS, classes), 1)
    hot = jnp.zeros((ITEM_ROWS, classes), F32)
    for i in range(items):
        hot = jnp.where((spot == i) & (label == cls_s[i]), 1.0, hot)
    l_table.wait()
    cond = dot(hot.astype(BF), b.table[...])
    b.cond[...] = cond
    cond_low = (cond / (1.0 + jnp.exp(-cond))).astype(BF)

    def make_mode(k):
        l_ada[k].wait()
        value = dot(cond_low, b.ada[k])
        high = value.astype(BF)
        rest = value - high.astype(F32)
        middle = rest.astype(BF)
        b.modes[k, 0:ITEM_ROWS] = high
        b.modes[k, ITEM_ROWS : 2 * ITEM_ROWS] = middle
        b.modes[k, 2 * ITEM_ROWS : 3 * ITEM_ROWS] = (rest - middle.astype(F32)).astype(BF)

    def per_token(k, which):
        return dot(b.pick[which], b.modes[k])

    def chunks(body):
        def step(i, carry):
            body(pl.ds(pl.multiple_of(i * 64, 64), 64))
            return carry

        lax.fori_loop(0, rows // 64, step, 0)

    make_mode(2)
    make_mode(4)

    l_tok.wait()

    def first_norm(which):
        normed, _ = norm_rows(b.tok[which].astype(F32))
        value = (normed * (1.0 + per_token(2, which)) + per_token(4, which)).astype(BF)
        b.a[0, which] = value[:, :half]
        b.a[1, which] = value[:, half:]

    chunks(first_norm)
    l_wq.wait()
    l_wo = load(wo_h, b.wo.at[plane])
    l_ada.update({k: load(ada_h.at[k], b.ada.at[k]) for k in (0, 3, 5, 1)})
    l_cot = load(cot_h, b.cot)
    l_f2 = load(f2_h, b.f2)
    l_f1 = load(f1_h, b.f1)
    first_store = len(loads)
    for k in range(3):
        value = dot(b.a[0], b.wq[k, :half]) + dot(b.a[1], b.wq[k, half:])
        value = value.T.astype(BF)
        for h in range(4):
            b.q_out[h, k * 64 : (k + 1) * 64] = value[h * 64 : (h + 1) * 64]
    pl.semaphore_wait(barrier, len(offsets) + 1)
    sent_q = [
        net.copy(b.q_out.at[chips[dp]], b.q_in.at[chip], at(dp, 0)) for dp in (3, 1, 2)
    ]
    b.q_in[chip] = b.q_out[chip]
    sent_k = [net.copy(b.q_in.at[chip, 64:192], b.k_in.at[chip], mate)]
    sent_a = net.copy(b.a.at[other], b.a_in, mate)
    sent_wo = [
        net.copy(wo_h.at[chip, core], b.wo.at[plane, chip, core], at(0, dz)) for dz in (3, 2, 1)
    ]

    spot = lax.broadcasted_iota(jnp.int32, (64, rows), 0)
    for s in range(4):
        for k, parity in enumerate((core, other)):
            item, scale = item_v[s * 2 + parity], scale_v[s * 2 + parity]
            by_item = jnp.where(item != spot - 1, BARRED, 0.0)
            by_scale = jnp.where((spot < 32) & (scale > spot - 16), BARRED, 0.0)
            b.kt[k * 4 + s, 64:128] = jnp.where(spot < 16, by_item, by_scale).astype(BF)
        item, scale = item_v[s * 2 + core], scale_v[s * 2 + core]
        by_item = jnp.where(item == spot - 1, 1.0, 0.0)
        by_scale = jnp.where((spot < 32) & (scale == spot - 16), 1.0, 0.0)
        b.qt[s, 64:128] = jnp.where(spot < 16, by_item, by_scale).astype(BF)
    make_mode(0)
    make_mode(3)
    for one, dp in zip(sent_q, (3, 1, 2), strict=True):
        net.arrived(one)
        sent_k.append(net.copy(b.q_in.at[chips[dp], 64:192], b.k_in.at[chips[dp]], mate))
    for one in sent_wo:
        net.arrived(one)
    sent_wo2 = {
        (dp, dz): net.copy(
            b.wo.at[planes[dz], chip, core], b.wo.at[planes[dz], chip, core], at(dp, 0)
        )
        for dz in (1, 2, 3)
        for dp in (3, 1, 2)
    }
    make_mode(5)
    make_mode(1)
    l_cot.wait()

    def mlp_grad(which):
        b.mg[which] = (per_token(1, which) * b.cot[which].astype(F32)).astype(BF)

    chunks(mlp_grad)
    sent_mg = net.copy(b.mg, b.mg_in, mate)

    for s in range(4):
        b.qt[s, 0:64] = b.q_in[s, 0:64]
        b.kt[s, 0:64] = b.q_in[s, 64:128]
        b.vt[s] = b.q_in[s, 128:192]
    for one in sent_k:
        net.arrived(one)
    for s in range(4):
        b.kt[4 + s, 0:64] = b.k_in[s, 0:64]
        b.vt[4 + s] = b.k_in[s, 64:128]
    for s in range(8):
        b.ka[s] = turned(b.kt[s]).astype(BF)

    sent_h = {}
    for dp in (3, 1, 2, 0):
        q = chips[dp]
        queries = b.qt[q]
        peak = None
        for s in range(8):
            scores = dot(b.ka[s], queries)
            b.scores[s] = scores
            top = jnp.max(scores, axis=0, keepdims=True)
            peak = top if peak is None else jnp.maximum(peak, top)
        total = jnp.zeros((1, rows), F32)
        result = jnp.zeros((64, rows), F32)
        for s in range(8):
            terms = jnp.exp2((b.scores[s] - peak) * EIGHTH_LOG2)
            total = total + jnp.sum(terms, axis=0, keepdims=True)
            low = terms.astype(BF)
            b.terms[q, s] = low
            result = result + dot(b.vt[s], low)
        share = 1.0 / total
        b.share[q] = share
        result = result * share
        b.heads[q] = result
        b.h_out[q] = result.astype(BF)
        for dz in (3, 2, 1, 0):
            if dp or dz:
                sent_h[dp, dz] = net.copy(
                    b.h_out.at[q], b.h_in.at[plane, chip], at(dp, dz)
                )
    b.h_in[plane, chip] = b.h_out[chip]

    for s in range(8):
        b.vn[s] = turned(b.vt[s]).astype(BF)
    for s in range(4):
        b.qn[s] = turned(b.qt[s])[:, 0:64].astype(BF)
    l_f2.wait()
    for n in range(4):
        cols = slice(n * 256, (n + 1) * 256)
        b.dact[:, cols] = dot_nt(b.mg[...], b.f2[cols])
    l_wo.wait()
    for one in sent_wo2.values():
        net.arrived(one)
    sent_wo3 = [
        net.copy(b.wo.at[planes[dz], :, core], b.wo.at[planes[dz], :, core], mate)
        for dz in (1, 2, 3)
    ]

    for dz in range(4):
        for dp in range(4):
            if dp or dz:
                net.arrived(sent_h[dp, dz])
        if dz:
            net.arrived(sent_wo3[dz - 1])
        left = turned(b.h_in[planes[dz]].reshape(256, rows)).astype(BF)
        right = b.wo[planes[dz]].reshape(256, width)
        if dz:
            b.attn[...] += dot(left, right)
        else:
            b.attn[...] = dot(left, right)
    sent_hx = net.copy(b.h_in.at[plane, pl.ds(2 * other, 2)], b.h_mate, mate)


    def second_norm(which):
        value = b.tok[which].astype(F32) + per_token(0, which) * b.attn[which]
        b.hid[which] = value
        normed, _ = norm_rows(value)
        value = (normed * (1.0 + per_token(3, which)) + per_token(5, which)).astype(BF)
        b.b[0, which] = value[:, :half]
        b.b[1, which] = value[:, half:]

    chunks(second_norm)
    l_f1.wait()
    for n in range(4):
        cols = slice(n * 256, (n + 1) * 256)
        up = dot(b.b[0], b.f1[:half, cols]) + dot(b.b[1], b.f1[half:, cols])
        square = up * up
        bent = jnp.tanh(GELU_A * up * (1.0 + GELU_B * square))
        gate = 0.5 * (1.0 + bent)
        slope = gate + 0.5 * up * (1.0 - bent * bent) * (GELU_A * (1.0 + 3.0 * GELU_B * square))
        b.act[n // 2, :, (n % 2) * 256 : (n % 2 + 1) * 256] = (up * gate).astype(BF)
        b.ug[:, cols] = (b.dact[:, cols] * slope).astype(BF)
    for n in range(4):
        cols = slice(n * 256, (n + 1) * 256)
        value = dot_nt(b.ug[...], b.f1[cols])
        b.bg_out[:, :, cols] = value.astype(BF).reshape(4, own, 256)
    sent_bg = [
        net.copy(b.bg_out.at[planes[dz]], b.bg_in.at[dz - 1], at(0, dz)) for dz in (3, 2, 1)
    ]

    ways = ((0, 1, 2), (1, 2, 1))

    def scatter(blocks, arrived):
        return [
            net.copy(blocks.at[chips[which], way], arrived.at[way, n], at(first, 0))
            for n, pick in ((1, 3), (0, None))
            for way, first, _ in ways
            for which in (pick or first,)
        ]

    def scatter_on(sent, blocks, arrived):
        for one in sent:
            net.arrived(one)
        for way, _, then in ways:
            total = blocks[chips[then], way].astype(F32) + arrived[way, 1].astype(F32)
            blocks[chips[then], way] = total.astype(BF)
        return [
            net.copy(blocks.at[chips[then], way], arrived.at[way, 2], at(then, 0))
            for way, _, then in ways
        ]

    def gather(sent, blocks, arrived, total, target):
        for one in sent:
            net.arrived(one)
        for way, _, _ in ways:
            total[way] = (
                blocks[chip, way].astype(F32)
                + arrived[way, 0].astype(F32)
                + arrived[way, 2].astype(F32)
            ).astype(BF)
        load(total, target.at[core, chip])
        net.copy(total, target.at[core, chip], mate)
        return [
            net.copy(total.at[way], target.at[core, chip, way], at(dp, 0))
            for way, dp in ((0, 2), (1, 1), (0, 1), (1, 2))
        ]

    def gather_on(sent, target):
        for one in sent[:2]:
            net.arrived(one)
        return [
            net.copy(
                target.at[core, chips[then], way], target.at[core, chips[then], way], at(first, 0)
            )
            for way, first, then in ways
        ]

    sent_x = [
        net.copy(b.act.at[other], b.act_in, mate),
        net.copy(b.b.at[other], b.b_in, mate),
        net.copy(b.ug, b.ug_in, mate),
    ]
    b.left[0] = turned(b.act[core]).astype(BF)
    net.arrived(sent_mg)
    net.arrived(sent_x[0])
    b.left[1] = turned(b.act_in[...]).astype(BF)
    for n in range(4):
        some = slice(n * 128, (n + 1) * 128)
        value = dot(b.left[0, some], b.mg[...]) + dot(b.left[1, some], b.mg_in[...])
        b.g2_out[n] = value.astype(BF).reshape(2, 64, width)
    sent_g2 = scatter(b.g2_out, b.g2_in)
    b.left[0] = turned(b.b[core]).astype(BF)
    net.arrived(sent_x[1])
    b.left[1] = turned(b.b_in[...]).astype(BF)
    net.arrived(sent_x[2])
    for n in range(4):
        some = slice(n * 128, (n + 1) * 128)
        value = dot(b.left[0, some], b.ug[...]) + dot(b.left[1, some], b.ug_in[...])
        b.g1_out[n] = value.astype(BF).reshape(2, 64, width)
    sent_g1 = scatter(b.g1_out, b.g1_in)
    for n in range(4):
        cols = slice(n * 256, (n + 1) * 256)
        value = dot(b.act[0], b.f2[:half, cols]) + dot(b.act[1], b.f2[half:, cols])
        b.mo_out[:, :, cols] = value.astype(BF).reshape(4, own, 256)

    def summed(sent, kept, arrived):
        for one in sent:
            net.arrived(one)
        total = kept.astype(F32)
        for k in range(3):
            total = total + arrived[k].astype(F32)
        return total

    def mode_sums(k, value):
        high = value.astype(BF)
        low = (value - high.astype(F32)).astype(BF)
        picked = turned(b.pick[mine])[0:ITEM_ROWS].astype(BF)
        value = (dot(picked, high) + dot(picked, low))[0:8]
        b.ms[0, k * 8 : (k + 1) * 8] = value[:, :half]
        b.ms[1, k * 8 : (k + 1) * 8] = value[:, half:]

    def plane_scatter(blocks, arrived, far):
        far_sent = net.copy(blocks.at[planes[3]], far, at(0, 1), outer, inner)
        sent = [
            net.copy(blocks.at[planes[2]], arrived.at[1], at(0, 2), outer, inner),
            net.copy(blocks.at[planes[3]], arrived.at[2], at(0, 3), inner, inner),
            net.copy(blocks.at[planes[1]], arrived.at[0], at(0, 1)),
        ]

        @pl.when(outer)
        def _():
            arrived[2] = jnp.zeros(arrived.shape[1:], BF)

        return sent, far_sent

    def plane_scatter_on(far_sent, blocks, arrived, far):
        net.arrived(far_sent)

        @pl.when(inner)
        def _():
            total = blocks[planes[2]].astype(F32) + far[...].astype(F32)
            blocks[planes[2]] = total.astype(BF)

        return net.copy(blocks.at[planes[2]], arrived.at[1], at(0, 2), inner, outer)

    def plane_gather(source, target):
        return [
            net.copy(source, target.at[plane], at(0, 2)),
            net.copy(source, target.at[plane], at(0, 3), inner, inner),
            net.copy(source, target.at[plane], at(0, 1)),
        ]

    def plane_gather_on(sent, target):
        net.arrived(sent[0])
        return net.copy(target.at[planes[2]], target.at[planes[2]], at(0, 1), inner, outer)

    b_grad = summed(sent_bg, b.bg_out[plane], b.bg_in)
    normed, inverse = norm_rows(b.hid[mine])
    h_grad = b.cot[mine].astype(F32) + norm_back(
        b_grad * (1.0 + per_token(3, mine)), normed, inverse
    )
    b.hg[...] = h_grad
    attn_grad = (per_token(0, mine) * h_grad).astype(BF)
    b.ag[plane] = attn_grad
    for n in range(4):
        value = dot_nt(attn_grad, b.wo[n].reshape(256, width)).astype(BF)
        for h in range(4):
            some = value[:, h * 64 : (h + 1) * 64]
            b.do_out[n, h] = jnp.concatenate([some[: own // 2], some[own // 2 :]], axis=1)
    sent_do = {
        (dp, dz): net.copy(
            b.do_out.at[planes[dz], chips[dp]], b.do_in.at[chip, plane], at(dp, dz)
        )
        for dp, dz in reversed(offsets)
    }
    b.do_in[chip, plane] = b.do_out[plane, chip]
    mode_sums(0, h_grad * b.attn[mine])
    mode_sums(3, b_grad * normed)
    mode_sums(5, b_grad)
    sent_g2 = scatter_on(sent_g2, b.g2_out, b.g2_in)
    sent_g1 = scatter_on(sent_g1, b.g1_out, b.g1_in)

    for one in sent_do.values():
        net.arrived(one)
    sent_mo, far_mo = plane_scatter(b.mo_out, b.mo_in, b.mo_far)
    sent_ag = plane_gather(b.ag.at[plane], b.ag)
    for s in range(4):
        for n in range(4):
            both = b.do_in[s, n]
            b.dn[s, n * own : n * own + own // 2] = both[:, 0:64]
            b.dn[s, n * own + own // 2 : (n + 1) * own] = both[:, 64:128]
        value = turned(b.dn[s])
        b.dt[s] = value.astype(BF)
        b.delta[s] = jnp.sum(value * b.heads[s], axis=0, keepdims=True)
        b.dn[s] = (value * b.share[s]).T.astype(BF)
        b.dq[s] = jnp.zeros((64, rows), F32)

    def attend_back(s, carry):
        keys, values = b.kt[s, 0:64], b.vn[s]
        key_grad = jnp.zeros((rows, 64), F32)
        value_grad = jnp.zeros((rows, 64), F32)
        for q in range(4):
            terms = b.terms[q, s]
            pull = (dot(values, b.dt[q]) - b.delta[q]) * b.share[q]
            low = (pull * terms.astype(F32)).astype(BF)
            b.dq[q] += dot(keys, low)
            key_grad = key_grad + dot(low, b.qn[q])
            value_grad = value_grad + dot(terms, b.dn[q])
        b.dkv[s] = jnp.concatenate([key_grad * 0.125, value_grad], axis=1).T
        return carry

    lax.fori_loop(4, 8, attend_back, 0)
    sent_dkv = net.copy(b.dkv.at[4:8], b.dkv_in, mate)
    sent_mo.append(plane_scatter_on(far_mo, b.mo_out, b.mo_in, b.mo_far))
    sent_g2b = gather(sent_g2, b.g2_out, b.g2_in, b.g2, gf2_o)
    sent_g1b = gather(sent_g1, b.g1_out, b.g1_in, b.g1, gf1_o)
    lax.fori_loop(0, 4, attend_back, 0)
    net.arrived(sent_dkv)
    for s in range(4):
        b.dx_out[s, 0:64] = (b.dq[s] * 0.125).astype(BF)
        b.dx_out[s, 64:192] = (b.dkv[s] + b.dkv_in[s]).astype(BF)
    sent_dx = [
        net.copy(b.dx_out.at[chips[dp]], b.dx_in.at[chip], at(dp, 0)) for dp in (3, 1, 2)
    ]
    b.dx_in[chip] = b.dx_out[chip]
    sent_ag.append(plane_gather_on(sent_ag, b.ag))

    for one in sent_dx:
        net.arrived(one)
    sent_dxm = net.copy(b.dx_in, b.dx_mate, mate)
    for k in range(3):
        value = b.dx_in[:, k * 64 : (k + 1) * 64].reshape(256, rows)
        b.dx[k] = turned(value).astype(BF)
    for n in range(4):
        cols = slice(n * 256, (n + 1) * 256)
        value = dot_nt(b.dx[0], b.wq[0, cols])
        value = value + dot_nt(b.dx[1], b.wq[1, cols])
        value = value + dot_nt(b.dx[2], b.wq[2, cols])
        b.xg_out[:, :, cols] = value.astype(BF).reshape(4, own, 256)
    sent_xg = [
        net.copy(b.xg_out.at[planes[dz]], b.xg_in.at[dz - 1], at(0, dz)) for dz in (3, 2, 1)
    ]

    net.arrived(sent_a)
    net.arrived(sent_dxm)
    for h in range(4):
        value = dot(b.dx_in[h], b.a[core]) + dot(b.dx_mate[h], b.a_in[...])
        b.gq_out[h] = value.astype(BF).reshape(2, 96, half)
    sent_gq = scatter(b.gq_out, b.gq_in)

    sent_g2b += gather_on(sent_g2b, gf2_o)
    sent_g1b += gather_on(sent_g1b, gf1_o)

    mlp_out = summed(sent_mo, b.mo_out[plane], b.mo_in)
    b.out[...] = (b.hid[mine] + per_token(1, mine) * mlp_out).astype(BF)
    sent_out = plane_gather(b.out, out_o)
    load(b.out, out_o.at[plane])
    mode_sums(1, b.cot[mine].astype(F32) * mlp_out)

    for one in sent_ag[1:]:
        net.arrived(one)
    sent_agm = net.copy(b.ag, b.ag_in, mate)
    value = dot(
        b.h_in[plane, pl.ds(2 * core, 2)].reshape(128, rows), b.ag[...].reshape(rows, width)
    )
    net.arrived(sent_hx)
    net.arrived(sent_agm)
    value = value + dot(b.h_mate[...].reshape(128, rows), b.ag_in[...].reshape(rows, width))
    b.go_out[...] = value.astype(BF).reshape(4, 32, width)
    sent_go = [
        net.copy(b.go_out.at[chips[dp]], b.go_in.at[dp - 1], at(dp, 0)) for dp in (3, 1, 2)
    ]

    plane_gather_on(sent_out, out_o)
    sent_gq = scatter_on(sent_gq, b.gq_out, b.gq_in)

    a_grad = summed(sent_xg, b.xg_out[plane], b.xg_in)
    normed, inverse = norm_rows(b.tok[mine].astype(F32))
    mode_sums(2, a_grad * normed)
    mode_sums(4, a_grad)
    sent_ms = net.copy(b.ms.at[other], b.ms_in, mate)
    value = b.hg[...] + norm_back(a_grad * (1.0 + per_token(2, mine)), normed, inverse)
    b.dtok[...] = value.astype(BF)
    net.arrived(sent_ms)
    b.m1[...] = (b.ms[core] + b.ms_in[...]).astype(BF)
    sent_m1 = [net.copy(b.m1, b.m1_in.at[dz - 1], at(0, dz)) for dz in (3, 2, 1)]
    sent_dt = plane_gather(b.dtok, dtok_o)
    load(b.dtok, dtok_o.at[plane])

    sent_gqb = gather(sent_gq, b.gq_out, b.gq_in, b.gq, gqkv_o)
    b.go[...] = summed(sent_go, b.go_out[chip], b.go_in).astype(BF)
    sent_gob = [net.copy(b.go, gout_o.at[core, chip], at(dp, 0)) for dp in (3, 1, 2)]
    load(b.go, gout_o.at[core, chip])
    net.copy(b.go, gout_o.at[core, chip], mate)
    b.m2[...] = summed(sent_m1, b.m1[...], b.m1_in).astype(BF)
    sent_m2 = [net.copy(b.m2, b.m2_in.at[dp - 1], at(dp, 0)) for dp in (3, 1, 2)]
    b.m3[...] = summed(sent_m2, b.m2[...], b.m2_in)
    net.copy(b.m3, mode_o.at[core], mate)
    load(b.m3, mode_o.at[core])
    load(b.cond, cond_o)
    sent_gqb += gather_on(sent_gqb, gqkv_o)
    plane_gather_on(sent_dt, dtok_o)

    for sent, array in ((sent_g2b, gf2_o), (sent_g1b, gf1_o), (sent_gqb, gqkv_o)):
        for one in sent[2:]:
            net.arrived(one)
        for dp in (1, 2, 3):
            where = (core, chips[dp])
            net.copy(array.at[where], array.at[where], mate)
    for one, dp in zip(sent_gob, (3, 1, 2), strict=True):
        net.arrived(one)
        where = (core, chips[dp])
        net.copy(gout_o.at[where], gout_o.at[where], mate)
    net.finish()
    for one in loads[first_store:]:
        one.wait()


def buffers(dims):
    rows, width, part, hidden, items, classes = dims
    own, half = rows // 4, width // 2
    return dict(
        tok=((rows, width), BF),
        cot=((rows, width), BF),
        table=((classes, width), BF),
        ada=((COMPONENTS, width, width), BF),
        wq=((3, width, part), BF),
        wo=((4, 4, 2, 32, width), BF),
        f1=((width, hidden), BF),
        f2=((hidden, width), BF),
        modes=((COMPONENTS, 3 * ITEM_ROWS, width), BF),
        pick=((rows, 3 * ITEM_ROWS), BF),
        cond=((ITEM_ROWS, width), F32),
        a=((2, rows, half), BF),
        a_in=((rows, half), BF),
        q_out=((4, 192, rows), BF),
        q_in=((4, 192, rows), BF),
        k_in=((4, 128, rows), BF),
        kt=((8, 128, rows), BF),
        ka=((8, rows, 128), BF),
        vt=((8, 64, rows), BF),
        vn=((8, rows, 64), BF),
        qt=((4, 128, rows), BF),
        qn=((4, rows, 64), BF),
        scores=((8, rows, rows), F32),
        terms=((4, 8, rows, rows), BF),
        share=((4, 1, rows), F32),
        heads=((4, 64, rows), F32),
        h_out=((4, 64, rows), BF),
        h_in=((4, 4, 64, rows), BF),
        h_mate=((2, 64, rows), BF),
        attn=((rows, width), F32),
        hid=((rows, width), F32),
        b=((2, rows, half), BF),
        b_in=((rows, half), BF),
        act=((2, rows, half), BF),
        act_in=((rows, half), BF),
        mg=((rows, width), BF),
        mg_in=((rows, width), BF),
        ug=((rows, hidden), BF),
        ug_in=((rows, hidden), BF),
        dact=((rows, hidden), F32),
        left=((2, half, rows), BF),
        bg_out=((4, own, width), BF),
        bg_in=((3, own, width), BF),
        mo_out=((4, own, width), BF),
        mo_in=((3, own, width), BF),
        mo_far=((own, width), BF),
        xg_out=((4, own, width), BF),
        xg_in=((3, own, width), BF),
        g1_out=((4, 2, 64, width), BF),
        g1_in=((2, 3, 64, width), BF),
        g1=((2, 64, width), BF),
        g2_out=((4, 2, 64, width), BF),
        g2_in=((2, 3, 64, width), BF),
        g2=((2, 64, width), BF),
        hg=((own, width), F32),
        ag=((4, own, width), BF),
        ag_in=((4, own, width), BF),
        do_out=((4, 4, own // 2, 128), BF),
        do_in=((4, 4, own // 2, 128), BF),
        dn=((4, rows, 64), BF),
        dt=((4, 64, rows), BF),
        delta=((4, 1, rows), F32),
        dq=((4, 64, rows), F32),
        dkv=((8, 128, rows), F32),
        dkv_in=((4, 128, rows), F32),
        dx_out=((4, 192, rows), BF),
        dx_mate=((4, 192, rows), BF),
        dx_in=((4, 192, rows), BF),
        dx=((3, rows, part), BF),
        gq_out=((4, 2, 96, half), BF),
        gq_in=((2, 3, 96, half), BF),
        gq=((2, 96, half), BF),
        out=((own, width), BF),
        dtok=((own, width), BF),
        go_out=((4, 32, width), BF),
        go_in=((3, 32, width), BF),
        go=((32, width), BF),
        ms=((2, 48, half), F32),
        ms_in=((48, half), F32),
        m1=((48, half), BF),
        m1_in=((3, 48, half), BF),
        m2=((48, half), BF),
        m2_in=((3, 48, half), BF),
        m3=((48, half), F32),
    )


def finish_kernel(
    cls_s, ada_h, out_i, dtok_i, gqkv_i, gout_i, gf1_i, gf2_i, mode_i, cond_i,
    out_o, dtok_o, table_o, ada_o, qkv_o, wout_o, f1_o, f2_o, ada_v, sems,
):
    step, last = pl.program_id(0), pl.num_programs(0) - 1
    plane = lax.axis_index("head")
    part = table_o.shape[1]
    mine = pl.ds(pl.multiple_of(plane * part, part), part)
    fetch = [
        pltpu.make_async_copy(ada_h.at[k, mine], ada_v.at[k], sems.at[k]) for k in range(COMPONENTS)
    ]

    @pl.when(step == 0)
    def _():
        for one in fetch:
            one.start()

    out_o[...] = out_i[0]
    dtok_o[...] = dtok_i[0]
    wout_o[...] = gout_i[0, 0].astype(F32)
    f1_o[...] = gf1_i[0, 0].astype(F32).reshape(f1_o.shape)
    f2_o[...] = gf2_i[0, 0].astype(F32).reshape(f2_o.shape)
    sums = gqkv_i[0].astype(F32).reshape(4, 192, 128)
    for k in range(3):
        qkv_o[k] = sums[:, k * 64 : (k + 1) * 64].reshape(part, 128).T
    cond = cond_i[:, pl.ds(pl.multiple_of(step * 128, 128), 128)]
    cond_low = (cond / (1.0 + jnp.exp(-cond)))[0:8]
    low = jnp.concatenate([cond_low, cond_low], axis=0).astype(BF)
    side = pl.ds(pl.multiple_of(lax.rem(plane, 2) * part, part), part)
    for k in range(COMPONENTS):
        value = mode_i[lax.div(plane, 2), k * 8 : (k + 1) * 8, side]
        high = value.astype(BF).astype(F32)
        both = jnp.concatenate([high, value - high], axis=0).astype(BF)
        ada_o[k] = dot_tn(low, both)

    @pl.when(step == last)
    def _():
        cond_grad = jnp.zeros((16, part), F32)
        half = mode_i.shape[2]
        for k in range(COMPONENTS):
            fetch[k].wait()
            for n in range(2):
                value = mode_i[n, k * 8 : (k + 1) * 8]
                high = value.astype(BF).astype(F32)
                both = jnp.concatenate([high, value - high], axis=0).astype(BF)
                cond_grad = cond_grad + dot_nt(both, ada_v[k, :, n * half : (n + 1) * half])
        own = cond_i[0:8, mine]
        gate = 1.0 / (1.0 + jnp.exp(-own))
        grad = (cond_grad[0:8] + cond_grad[8:16]) * gate * (1.0 + own * (1.0 - gate))
        spot = lax.broadcasted_iota(jnp.int32, table_o.shape, 0)
        total = jnp.zeros(table_o.shape, F32)
        for i in range(cls_s.shape[0]):
            total = total + jnp.where(spot == cls_s[i], grad[i : i + 1], 0.0)
        table_o[...] = total


def finish(
    class_ids, w_ada, output, d_tokens, qkv_sum, out_sum, fc1_sum, fc2_sum, mode_grad, cond, classes
):
    steps = 8
    own, width = output.shape[1:]
    half, part, hidden = width // 2, width // 4, steps * 128
    rows = own * 4
    anywhere = pl.BlockSpec(memory_space=pl.ANY)
    smem = pl.BlockSpec(memory_space=pltpu.SMEM)
    few = pl.BlockSpec((1, own // 2, width), lambda i: (i // 2, i % 2, 0))
    table, ada, qkv, out, fc1, fc2 = (
        (classes, part),
        (COMPONENTS, width, part),
        (3, width, part),
        (part, width),
        (width, hidden),
        (hidden, width),
    )
    output, d_tokens, table, ada, qkv, out, fc1, fc2 = pl.pallas_call(
        finish_kernel,
        grid=(steps,),
        out_shape=[
            jax.ShapeDtypeStruct((rows, width), BF),
            jax.ShapeDtypeStruct((rows, width), BF),
        ]
        + [jax.ShapeDtypeStruct(shape, F32) for shape in (table, ada, qkv, out, fc1, fc2)],
        in_specs=[
            smem,
            anywhere,
            few,
            few,
            pl.BlockSpec((1, 4, 2, 96, half // 4), lambda i: (i // 4, 0, 0, 0, i % 4)),
            pl.BlockSpec((1, 1, 32, width), lambda i: (i // 4, i % 4, 0, 0)),
            pl.BlockSpec((1, 1, 2, 64, hidden), lambda i: (i // 4, i % 4, 0, 0, 0)),
            pl.BlockSpec((1, 1, 2, 64, width), lambda i: (i // 4, i % 4, 0, 0, 0)),
            pl.BlockSpec((2, 48, half), lambda i: (0, 0, 0)),
            pl.BlockSpec((ITEM_ROWS, width), lambda i: (0, 0)),
        ],
        out_specs=[
            pl.BlockSpec((rows // steps, width), lambda i: (i, 0)),
            pl.BlockSpec((rows // steps, width), lambda i: (i, 0)),
            pl.BlockSpec((classes, part), lambda i: (0, 0)),
            pl.BlockSpec((COMPONENTS, 128, part), lambda i: (0, i, 0)),
            pl.BlockSpec((3, 128, part), lambda i: (0, i, 0)),
            pl.BlockSpec((32, width), lambda i: (i, 0)),
            pl.BlockSpec((128, hidden), lambda i: (i, 0)),
            pl.BlockSpec((128, width), lambda i: (i, 0)),
        ],
        scratch_shapes=[
            pltpu.VMEM((COMPONENTS, part, width), BF),
            pltpu.SemaphoreType.DMA((COMPONENTS,)),
        ],
        compiler_params=pltpu.CompilerParams(vmem_limit_bytes=VMEM_BYTES),
    )(
        class_ids, w_ada, output, d_tokens, qkv_sum, out_sum, fc1_sum, fc2_sum, mode_grad, cond
    )
    return output, d_tokens, table, ada, qkv.transpose(1, 0, 2), out, fc1, fc2


def on_block(
    tokens,
    class_ids,
    slot_item,
    slot_scale,
    class_table,
    w_ada,
    w_qkv,
    w_out,
    w_fc1,
    w_fc2,
    cotangent,
):
    rows, width = tokens.shape
    part, hidden = w_qkv.shape[2], w_fc1.shape[1]
    items, classes = class_ids.shape[0], class_table.shape[0]
    own, half = rows // 4, width // 2
    dims = (rows, width, part, hidden, items, classes)
    scratch = [pltpu.VMEM(shape, dtype) for shape, dtype in buffers(dims).values()]
    anywhere = pl.BlockSpec(memory_space=pl.ANY)
    vmem = pl.BlockSpec(memory_space=pltpu.VMEM)
    smem = pl.BlockSpec(memory_space=pltpu.SMEM)
    output, d_tokens, qkv_sum, out_sum, fc1_sum, fc2_sum, mode_grad, cond = pl.pallas_call(
        functools.partial(block_kernel, dims),
        out_shape=[
            jax.ShapeDtypeStruct((4, own, width), BF),
            jax.ShapeDtypeStruct((4, own, width), BF),
            jax.ShapeDtypeStruct((2, 4, 2, 96, half), BF),
            jax.ShapeDtypeStruct((2, 4, 32, width), BF),
            jax.ShapeDtypeStruct((2, 4, 2, 64, width), BF),
            jax.ShapeDtypeStruct((2, 4, 2, 64, width), BF),
            jax.ShapeDtypeStruct((2, 48, half), F32),
            jax.ShapeDtypeStruct((ITEM_ROWS, width), F32),
        ],
        in_specs=[anywhere, smem, vmem, vmem] + [anywhere] * 7,
        out_specs=[anywhere] * 8,
        scratch_shapes=[
            pltpu.SemaphoreType.DMA((COPIES,)),
            pltpu.SemaphoreType.DMA((COPIES,)),
            pltpu.SemaphoreType.DMA((32,)),
            *scratch,
        ],
        compiler_params=pltpu.CompilerParams(
            collective_id=0, has_side_effects=True, vmem_limit_bytes=VMEM_BYTES
        ),
        cost_estimate=pl.CostEstimate(
            flops=10_000_000_000, bytes_accessed=40_000_000, transcendentals=3_000_000
        ),
    )(
        tokens,
        class_ids,
        slot_item.reshape(8, 1, rows),
        slot_scale.reshape(8, 1, rows),
        class_table,
        w_ada,
        w_qkv.transpose(1, 0, 2),
        w_out.reshape(4, 2, 32, width),
        w_fc1,
        w_fc2,
        cotangent,
    )
    return finish(
        class_ids, w_ada, output, d_tokens, qkv_sum, out_sum, fc1_sum, fc2_sum, mode_grad, cond,
        classes,
    )


def fits(mesh):
    return mesh.shape["tok"] == 8 and mesh.shape["head"] == 4


def layer_norm(values):
    centre = jnp.mean(values, axis=-1, keepdims=True)
    shifted = values - centre
    spread = jnp.mean(shifted * shifted, axis=-1, keepdims=True)
    return shifted * lax.rsqrt(spread + EPS)


def modulate(values, scale_in, shift_in):
    return layer_norm(values) * (1.0 + scale_in) + shift_in


def pair_scores(queries, key_block, query_item, key_item, query_scale, key_scale):
    scores = (
        jnp.einsum("qhd,khd->hqk", queries, key_block, preferred_element_type=jnp.float32) * 0.125
    )
    allowed = (
        (query_item[:, None] == key_item[None, :]) & (key_scale[None, :] <= query_scale[:, None])
    )[None]
    return (jnp.where(allowed, scores, -1e30), allowed)


def on_device(
    tokens,
    class_ids,
    slot_item,
    slot_scale,
    class_table,
    w_ada,
    w_qkv,
    w_out,
    w_fc1,
    w_fc2,
    cotangent,
):
    tok_rows, full_width = tokens.shape
    slot_count = slot_item.shape[0]
    item_count = class_ids.shape[0]
    class_count = class_table.shape[0]
    local_width = w_qkv.shape[2]
    local_heads = local_width // HEAD_DIM
    anchor = lax.axis_index("tok") * tok_rows
    first_col = lax.axis_index("head") * local_width
    my_item = lax.dynamic_slice_in_dim(slot_item, anchor, tok_rows)
    my_scale = lax.dynamic_slice_in_dim(slot_scale, anchor, tok_rows)
    class_pick = (class_ids[:, None] == jnp.arange(class_count, dtype=jnp.int32)[None, :]).astype(
        jnp.bfloat16
    )
    cond = jnp.dot(class_pick, class_table, preferred_element_type=jnp.float32)
    silu_cond, silu_back = jax.vjp(jax.nn.silu, cond)
    cond_low = silu_cond.astype(jnp.bfloat16)
    modes = jnp.einsum("id,cde->ice", cond_low, w_ada, preferred_element_type=jnp.float32)
    item_pick = (my_item[:, None] == jnp.arange(item_count, dtype=jnp.int32)[None, :]).astype(
        jnp.float32
    )
    per_token = jnp.dot(
        item_pick, modes.reshape(item_count, 6 * full_width), precision=HIGH
    ).reshape(tok_rows, 6, full_width)
    gamma_one = per_token[:, 0]
    gamma_two = per_token[:, 1]
    scale_one = per_token[:, 2]
    scale_two = per_token[:, 3]
    shift_one = per_token[:, 4]
    shift_two = per_token[:, 5]
    tok_float = tokens.astype(jnp.float32)
    a_pre, a_back = jax.vjp(modulate, tok_float, scale_one, shift_one)
    a_low = a_pre.astype(jnp.bfloat16)
    qkv_low = jnp.einsum("td,dce->tce", a_low, w_qkv, preferred_element_type=jnp.float32).astype(
        jnp.bfloat16
    )
    queries = qkv_low[:, 0]
    key_own = qkv_low[:, 1]
    value_own = qkv_low[:, 2]
    query_heads = queries.reshape(tok_rows, local_heads, HEAD_DIM)
    key_all, value_all = (
        lax.all_gather(key_own, "tok", axis=0, tiled=True),
        lax.all_gather(value_own, "tok", axis=0, tiled=True),
    )
    block_rows = math.gcd(slot_count, 2048)
    blocks = slot_count // block_rows
    key_blocks = key_all.reshape(blocks, block_rows, local_heads, HEAD_DIM)
    value_blocks = value_all.reshape(blocks, block_rows, local_heads, HEAD_DIM)
    item_blocks = slot_item.reshape(blocks, block_rows)
    scale_blocks = slot_scale.reshape(blocks, block_rows)
    key_wanted = jnp.min(scale_blocks, axis=1) <= jnp.max(my_scale)

    def first_pass(running, inputs):
        key_block, item_block, scale_block, wanted = inputs

        def first_compute_block(state_now):
            scores, allowed = pair_scores(
                query_heads, key_block, my_item, item_block, my_scale, scale_block
            )
            new_peak = jnp.maximum(state_now[0], jnp.max(scores, axis=2))
            terms = jnp.where(allowed, jnp.exp(scores - new_peak[:, :, None]), 0.0)
            return (
                new_peak,
                state_now[1] * jnp.exp(state_now[0] - new_peak) + jnp.sum(terms, axis=2),
            )

        return (lax.cond(wanted, first_compute_block, lambda state_now: state_now, running), None)

    initial = (
        jnp.full((local_heads, tok_rows), -1e30, jnp.float32),
        jnp.zeros((local_heads, tok_rows), jnp.float32),
    )
    (row_peak, summed), _ = lax.scan(
        first_pass, initial, (key_blocks, item_blocks, scale_blocks, key_wanted)
    )
    log_total = row_peak + jnp.log(summed)

    def second_pass(running, inputs):
        key_block, value_block, item_block, scale_block, wanted = inputs

        def second_compute_block(total_now):
            scores, allowed = pair_scores(
                query_heads, key_block, my_item, item_block, my_scale, scale_block
            )
            rounded = jnp.where(allowed, jnp.exp(scores - log_total[:, :, None]), 0.0).astype(
                jnp.bfloat16
            )
            return total_now + jnp.einsum(
                "hqk,khd->qhd", rounded, value_block, preferred_element_type=jnp.float32
            )

        return (lax.cond(wanted, second_compute_block, lambda total_now: total_now, running), None)

    heads_out, _ = lax.scan(
        second_pass,
        jnp.zeros((tok_rows, local_heads, HEAD_DIM), jnp.float32),
        (key_blocks, value_blocks, item_blocks, scale_blocks, key_wanted),
    )
    heads_low = heads_out.reshape(tok_rows, local_width).astype(jnp.bfloat16)
    attn_out = lax.psum(
        jnp.dot(heads_low, w_out, preferred_element_type=jnp.float32).astype(jnp.bfloat16), "head"
    ).astype(jnp.float32)
    hidden = tok_float + gamma_one * attn_out
    b_pre, b_back = jax.vjp(modulate, hidden, scale_two, shift_two)
    b_low = b_pre.astype(jnp.bfloat16)
    up_proj = jnp.dot(b_low, w_fc1, preferred_element_type=jnp.float32)
    act_pre, act_back = jax.vjp(lambda values: jax.nn.gelu(values, approximate=True), up_proj)
    act_low = act_pre.astype(jnp.bfloat16)
    mlp_out = lax.psum(
        jnp.dot(act_low, w_fc2, preferred_element_type=jnp.float32).astype(jnp.bfloat16), "head"
    ).astype(jnp.float32)
    output = (hidden + gamma_two * mlp_out).astype(jnp.bfloat16)
    out_grad = cotangent.astype(jnp.float32)
    mlp_grad = (gamma_two * out_grad).astype(jnp.bfloat16)
    fc2_weight_grad = jnp.einsum("tf,td->fd", act_low, mlp_grad, preferred_element_type=jnp.float32)
    act_grad = jnp.einsum("td,fd->tf", mlp_grad, w_fc2, preferred_element_type=jnp.float32)
    up_grad = act_back(act_grad)[0].astype(jnp.bfloat16)
    fc1_weight_grad = jnp.einsum("td,tf->df", b_low, up_grad, preferred_element_type=jnp.float32)
    b_grad = lax.psum(
        jnp.einsum("tf,df->td", up_grad, w_fc1, preferred_element_type=jnp.float32).astype(
            jnp.bfloat16
        ),
        "head",
    ).astype(jnp.float32)
    hidden_part, scale_two_grad, shift_two_grad = b_back(b_grad)
    hidden_grad = out_grad + hidden_part
    attn_grad = (gamma_one * hidden_grad).astype(jnp.bfloat16)
    out_weight_grad = jnp.einsum(
        "tf,te->fe", heads_low, attn_grad, preferred_element_type=jnp.float32
    )
    grad_low = jnp.einsum("te,fe->tf", attn_grad, w_out, preferred_element_type=jnp.float32).astype(
        jnp.bfloat16
    )
    grad_heads = grad_low.reshape(tok_rows, local_heads, HEAD_DIM)
    delta = jnp.einsum("qhd,qhd->hq", grad_heads.astype(jnp.float32), heads_out)

    def step_block(running, inputs):
        key_block, value_block, item_block, scale_block, wanted = inputs

        def step_compute_block(total_now):
            scores, allowed = pair_scores(
                query_heads, key_block, my_item, item_block, my_scale, scale_block
            )
            weights = jnp.where(allowed, jnp.exp(scores - log_total[:, :, None]), 0.0)
            weight_grad = jnp.einsum(
                "qhd,khd->hqk", grad_heads, value_block, preferred_element_type=jnp.float32
            )
            score_grad = (weights * (weight_grad - delta[:, :, None])).astype(jnp.bfloat16)
            total_now = (
                total_now
                + jnp.einsum(
                    "hqk,khd->qhd", score_grad, key_block, preferred_element_type=jnp.float32
                )
                * 0.125
            )
            key_term = (
                jnp.einsum(
                    "hqk,qhd->khd", score_grad, query_heads, preferred_element_type=jnp.float32
                )
                * 0.125
            )
            value_term = jnp.einsum(
                "hqk,qhd->khd",
                weights.astype(jnp.bfloat16),
                grad_heads,
                preferred_element_type=jnp.float32,
            )
            return (total_now, (key_term, value_term))

        def skip_block(total_now):
            nothing = jnp.zeros((block_rows, local_heads, HEAD_DIM), jnp.float32)
            return (total_now, (nothing, nothing))

        return lax.cond(wanted, step_compute_block, skip_block, running)

    query_grad, (key_terms, value_terms) = lax.scan(
        step_block,
        jnp.zeros((tok_rows, local_heads, HEAD_DIM), jnp.float32),
        (key_blocks, value_blocks, item_blocks, scale_blocks, key_wanted),
    )
    key_grad, value_grad = (
        lax.psum_scatter(
            key_terms.reshape(slot_count, local_width), "tok", scatter_dimension=0, tiled=True
        ),
        lax.psum_scatter(
            value_terms.reshape(slot_count, local_width), "tok", scatter_dimension=0, tiled=True
        ),
    )
    qkv_grad = jnp.stack(
        [query_grad.reshape(tok_rows, local_width), key_grad, value_grad], axis=1
    ).astype(jnp.bfloat16)
    qkv_weight_grad = jnp.einsum("td,tce->dce", a_low, qkv_grad, preferred_element_type=jnp.float32)
    a_grad = lax.psum(
        jnp.einsum("tce,dce->td", qkv_grad, w_qkv, preferred_element_type=jnp.float32).astype(
            jnp.bfloat16
        ),
        "head",
    ).astype(jnp.float32)
    tok_part, scale_one_grad, shift_one_grad = a_back(a_grad)
    d_tokens = (hidden_grad + tok_part).astype(jnp.bfloat16)
    token_modes = jnp.stack(
        [
            hidden_grad * attn_out,
            out_grad * mlp_out,
            scale_one_grad,
            scale_two_grad,
            shift_one_grad,
            shift_two_grad,
        ],
        axis=1,
    )
    mode_part = jnp.einsum(
        "ti,tf->if", item_pick, token_modes.reshape(tok_rows, 6 * full_width), precision=HIGH
    ).reshape(item_count, 6, full_width)
    qkv_sum, out_sum, fc1_sum, fc2_sum, mode_grad = lax.psum(
        (qkv_weight_grad, out_weight_grad, fc1_weight_grad, fc2_weight_grad, mode_part), "tok"
    )
    cond_grad = jnp.zeros((item_count, full_width), jnp.float32)
    for component in range(6):
        cond_grad = cond_grad + jnp.dot(
            mode_grad[:, component], w_ada[component].astype(jnp.float32).T, precision=HIGH
        )
    pre_grad = silu_back(cond_grad)[0]
    own_pre = lax.dynamic_slice_in_dim(pre_grad, first_col, local_width, 1)
    table_grad = jnp.einsum("ic,id->cd", class_pick.astype(jnp.float32), own_pre, precision=HIGH)
    own_modes = lax.dynamic_slice_in_dim(mode_grad, first_col, local_width, 2)
    ada_grad = jnp.einsum("id,ice->cde", cond_low.astype(jnp.float32), own_modes, precision=HIGH)
    return (output, d_tokens, table_grad, ada_grad, qkv_sum, out_sum, fc1_sum, fc2_sum)


def solution(mesh):
    placed = (
        P("tok", None),
        P(),
        P(),
        P(),
        P(),
        P(),
        P(None, None, "head"),
        P("head", None),
        P(None, "head"),
        P("head", None),
        P("tok", None),
    )
    return jax.shard_map(
        on_block if fits(mesh) else on_device,
        mesh=mesh,
        in_specs=placed,
        out_specs=(
            P("tok", None),
            P("tok", None),
            P(None, "head"),
            P(None, None, "head"),
            P(None, None, "head"),
            P("head", None),
            P(None, "head"),
            P("head", None),
        ),
        check_vma=False,
    )
```

```python
import functools
import math
import types

import jax
import jax.numpy as jnp
from jax import lax
from jax.experimental import pallas as pl
from jax.experimental.pallas import tpu as pltpu
from jax.sharding import PartitionSpec as P

HEAD_DIM = 64
COMPONENTS = 6


EPS = 1e-06
HIGH = lax.Precision.HIGHEST
BF = jnp.bfloat16
F32 = jnp.float32
MESH = pl.DeviceIdType.MESH
BARRED = -1e30
EIGHTH_LOG2 = 0.125 * math.log2(math.e)
GELU_A = math.sqrt(2.0 / math.pi)
GELU_B = 0.044715
COPIES = 164
LOADS = 22
VMEM_BYTES = 62 * 1024 * 1024
ITEM_ROWS = 16


def dot(left, right):
    return lax.dot_general(left, right, (((1,), (0,)), ((), ())), preferred_element_type=F32)


def dot_nt(left, right):
    return lax.dot_general(left, right, (((1,), (1,)), ((), ())), preferred_element_type=F32)


def dot_tn(left, right):
    return lax.dot_general(left, right, (((0,), (0,)), ((), ())), preferred_element_type=F32)


def turned(block):
    return block.astype(F32).T


def norm_rows(values):
    shifted = values - jnp.mean(values, axis=-1, keepdims=True)
    inverse = lax.rsqrt(jnp.mean(shifted * shifted, axis=-1, keepdims=True) + EPS)
    return shifted * inverse, inverse


def norm_back(grad, normed, inverse):
    along = jnp.mean(grad * normed, axis=-1, keepdims=True)
    return (grad - jnp.mean(grad, axis=-1, keepdims=True) - normed * along) * inverse


class Net:
    def __init__(self, send, arrive):
        self.send, self.arrive = send, arrive
        self.made, self.waited = [], []

    def copy(self, source, target, device, when=None, gets=None):
        k = len(self.made)
        one = pltpu.make_async_remote_copy(
            src_ref=source,
            dst_ref=target,
            send_sem=self.send.at[k],
            recv_sem=self.arrive.at[k],
            device_id=device,
            device_id_type=MESH,
        )
        self.made.append((one, when, gets))
        on_some(when, one.start)
        return k

    def arrived(self, k):
        one, _, gets = self.made[k]
        on_some(gets, one.wait_recv)
        self.waited.append(k)

    def finish(self):
        for k, (one, when, _) in enumerate(self.made):
            on_some(when, one.wait_send)
            if k not in self.waited:
                self.arrived(k)


def on_some(when, act):
    if when is None:
        act()
    else:
        pl.when(when)(act)


def block_kernel(dims, *refs):
    rows, width, part, hidden, items, classes = dims
    names = list(buffers(dims))
    (
        tok_h, cls_s, item_v, scale_v, table_h, ada_h, wq_h, wo_h, f1_h, f2_h, cot_h,
        out_o, dtok_o, gqkv_o, gout_o, gf1_o, gf2_o, mode_o, cond_o, cg_o,
        send_sem, arrive_sem, load_sem, *scratch,
    ) = refs
    b = types.SimpleNamespace(**dict(zip(names, scratch, strict=True)))
    own = rows // 4
    half = width // 2
    net = Net(send_sem, arrive_sem)
    loads = []

    def load(source, target):
        one = pltpu.make_async_copy(source, target, load_sem.at[len(loads)])
        one.start()
        loads.append(one)
        return one

    group = lax.axis_index("tok")
    plane = lax.axis_index("head")
    core = lax.rem(group, 2)
    chip = lax.div(group, 2)
    col, line = lax.rem(chip, 2), lax.div(chip, 2)
    chips = [chip, line * 2 + 1 - col, (1 - line) * 2 + col, 3 - chip]
    planes = [
        plane,
        lax.div(plane, 2) * 2 + 1 - lax.rem(plane, 2),
        lax.rem(plane + 2, 4),
        3 - plane,
    ]
    other = 1 - core
    inner = (plane == 1) | (plane == 2)
    outer = (plane == 0) | (plane == 3)
    offsets = [(dp, dz) for dz in range(4) for dp in range(4) if dp or dz]

    def at(dp, dz):
        return (chips[dp] * 2 + core, planes[dz])

    mate = (chip * 2 + other, plane)
    mine = pl.ds(pl.multiple_of(plane * own, own), own)

    def summed(sent, kept, arrived):
        for one in sent:
            net.arrived(one)
        total = kept.astype(F32)
        for k in range(3):
            total = total + arrived[k].astype(F32)
        return total

    ways = ((0, 1, 2), (1, 2, 1))

    def scatter(blocks, arrived):
        return [
            net.copy(blocks.at[chips[which], way], arrived.at[way, n], at(first, 0))
            for n, pick in ((1, 3), (0, None))
            for way, first, _ in ways
            for which in (pick or first,)
        ]

    def scatter_on(sent, blocks, arrived):
        for one in sent:
            net.arrived(one)
        for way, _, then in ways:
            total = blocks[chips[then], way].astype(F32) + arrived[way, 1].astype(F32)
            blocks[chips[then], way] = total.astype(BF)
        return [
            net.copy(blocks.at[chips[then], way], arrived.at[way, 2], at(then, 0))
            for way, _, then in ways
        ]

    def gather(sent, blocks, arrived, total, target):
        for one in sent:
            net.arrived(one)
        for way, _, _ in ways:
            total[way] = (
                blocks[chip, way].astype(F32)
                + arrived[way, 0].astype(F32)
                + arrived[way, 2].astype(F32)
            ).astype(BF)
        load(total, target.at[core, chip])
        net.copy(total, target.at[core, chip], mate)
        return [
            net.copy(total.at[way], target.at[core, chip, way], at(dp, 0))
            for way, dp in ((0, 2), (1, 1), (0, 1), (1, 2))
        ]

    def gather_on(sent, target):
        for one in sent[:2]:
            net.arrived(one)
        return [
            net.copy(
                target.at[core, chips[then], way], target.at[core, chips[then], way], at(first, 0)
            )
            for way, first, then in ways
        ]

    def plane_scatter(blocks, arrived, far):
        far_sent = net.copy(blocks.at[planes[3]], far, at(0, 1), outer, inner)
        sent = [
            net.copy(blocks.at[planes[2]], arrived.at[1], at(0, 2), outer, inner),
            net.copy(blocks.at[planes[3]], arrived.at[2], at(0, 3), inner, inner),
            net.copy(blocks.at[planes[1]], arrived.at[0], at(0, 1)),
        ]

        @pl.when(outer)
        def _():
            arrived[2] = jnp.zeros(arrived.shape[1:], BF)

        return sent, far_sent

    def plane_scatter_on(far_sent, blocks, arrived, far):
        net.arrived(far_sent)

        @pl.when(inner)
        def _():
            total = blocks[planes[2]].astype(F32) + far[...].astype(F32)
            blocks[planes[2]] = total.astype(BF)

        return net.copy(blocks.at[planes[2]], arrived.at[1], at(0, 2), inner, outer)

    def plane_gather(source, target):
        return [
            net.copy(source, target.at[plane], at(0, 2)),
            net.copy(source, target.at[plane], at(0, 3), inner, inner),
            net.copy(source, target.at[plane], at(0, 1)),
        ]

    def plane_gather_on(sent, target):
        net.arrived(sent[0])
        return net.copy(target.at[planes[2]], target.at[planes[2]], at(0, 1), inner, outer)

    l_table = load(table_h, b.table)
    l_ada = {k: load(ada_h.at[k], b.ada.at[k]) for k in (2, 4)}
    l_tok = load(tok_h, b.tok)
    l_wq = load(wq_h, b.wq)
    barrier = pltpu.get_barrier_semaphore()
    for dp, dz in offsets:
        pl.semaphore_signal(barrier, inc=1, device_id=at(dp, dz), device_id_type=MESH)
    pl.semaphore_signal(barrier, inc=1, device_id=mate, device_id_type=MESH)

    spot = lax.rem(lax.broadcasted_iota(jnp.int32, (3 * ITEM_ROWS, rows), 0), ITEM_ROWS)
    picks = jnp.where(spot == item_v[group], 1.0, 0.0)
    b.pick[...] = picks.T.astype(BF)

    spot = lax.broadcasted_iota(jnp.int32, (ITEM_ROWS, classes), 0)
    label = lax.broadcasted_iota(jnp.int32, (ITEM_ROWS, classes), 1)
    hot = jnp.zeros((ITEM_ROWS, classes), F32)
    for i in range(items):
        hot = jnp.where((spot == i) & (label == cls_s[i]), 1.0, hot)
    l_table.wait()
    cond = dot(hot.astype(BF), b.table[...])
    b.cond[...] = cond
    cond_low = (cond / (1.0 + jnp.exp(-cond))).astype(BF)

    def make_mode(k):
        l_ada[k].wait()
        value = dot(cond_low, b.ada[k])
        high = value.astype(BF)
        rest = value - high.astype(F32)
        middle = rest.astype(BF)
        b.modes[k, 0:ITEM_ROWS] = high
        b.modes[k, ITEM_ROWS : 2 * ITEM_ROWS] = middle
        b.modes[k, 2 * ITEM_ROWS : 3 * ITEM_ROWS] = (rest - middle.astype(F32)).astype(BF)

    def per_token(k, which):
        return dot(b.pick[which], b.modes[k])

    def chunks(body):
        def step(i, carry):
            body(pl.ds(pl.multiple_of(i * 64, 64), 64))
            return carry

        lax.fori_loop(0, rows // 64, step, 0)

    make_mode(2)
    make_mode(4)

    l_tok.wait()

    def first_norm(which):
        normed, _ = norm_rows(b.tok[which].astype(F32))
        value = (normed * (1.0 + per_token(2, which)) + per_token(4, which)).astype(BF)
        b.a[0, which] = value[:, :half]
        b.a[1, which] = value[:, half:]

    for i in range(0, rows, 64):
        first_norm(slice(i, i + 64))
    l_wq.wait()
    l_wo = load(wo_h, b.wo.at[plane])
    l_ada.update({k: load(ada_h.at[k], b.ada.at[k]) for k in (0, 3, 5, 1)})
    l_cot = load(cot_h, b.cot)
    l_f2 = load(f2_h, b.f2)
    l_f1 = load(f1_h, b.f1)
    first_store = len(loads)
    for k in range(3):
        value = dot(b.a[0], b.wq[k, :half]) + dot(b.a[1], b.wq[k, half:])
        value = value.T.astype(BF)
        for h in range(4):
            b.q_out[h, k * 64 : (k + 1) * 64] = value[h * 64 : (h + 1) * 64]
    pl.semaphore_wait(barrier, len(offsets) + 1)
    sent_q = {
        (dp, n): net.copy(b.q_out.at[chips[dp], part_of], b.q_in.at[dp, part_of], at(dp, 0))
        for n, part_of in enumerate((slice(64, 192), slice(0, 64)))
        for dp in (3, 1, 2)
    }
    b.q_in[0] = b.q_out[chip]
    sent_k = [net.copy(b.q_in.at[0, 64:192], b.k_in.at[0], mate)]
    sent_a = net.copy(b.a.at[other], b.a_in, mate)
    sent_wo = [
        net.copy(wo_h.at[chip, core], b.wo.at[plane, chip, core], at(0, dz)) for dz in (3, 2, 1)
    ]

    spot = lax.broadcasted_iota(jnp.int32, (64, rows), 0)
    for s in range(4):
        for k, parity in enumerate((core, other)):
            item, scale = item_v[chips[s] * 2 + parity], scale_v[chips[s] * 2 + parity]
            by_item = jnp.where(item != spot - 1, BARRED, 0.0)
            by_scale = jnp.where((spot < 32) & (scale > spot - 16), BARRED, 0.0)
            b.kt[k * 4 + s, 64:128] = jnp.where(spot < 16, by_item, by_scale).astype(BF)
        item, scale = item_v[chips[s] * 2 + core], scale_v[chips[s] * 2 + core]
        by_item = jnp.where(item == spot - 1, 1.0, 0.0)
        by_scale = jnp.where((spot < 32) & (scale == spot - 16), 1.0, 0.0)
        b.qt[s, 64:128] = jnp.where(spot < 16, by_item, by_scale).astype(BF)
    make_mode(0)
    make_mode(3)
    make_mode(5)
    make_mode(1)
    l_cot.wait()

    def mlp_grad(which):
        b.mg[which] = (per_token(1, which) * b.cot[which].astype(F32)).astype(BF)

    chunks(mlp_grad)
    for dp in (3, 1, 2):
        net.arrived(sent_q[dp, 0])
        sent_k.append(net.copy(b.q_in.at[dp, 64:192], b.k_in.at[dp], mate))

    def take_keys(s, block):
        b.kt[s, 0:64] = block[0:64]
        b.ktw[:, s * 256 : (s + 1) * 256] = block[0:64]
        b.vt[s] = block[64:128]
        b.ka[s] = turned(b.kt[s]).astype(BF)

    for s in range(4):
        take_keys(s, b.q_in[s, 64:192])
    for dp in (3, 1, 2):
        net.arrived(sent_q[dp, 1])
    for s in range(4):
        b.qt[s, 0:64] = b.q_in[s, 0:64]
    for one in sent_k:
        net.arrived(one)
    for s in range(4):
        take_keys(4 + s, b.k_in[s])
    sent_mg = net.copy(b.mg, b.mg_in, mate)

    sent_h = {}
    for dp in (3, 1, 2, 0):
        queries = b.qt[dp]
        peak = None
        for s in range(8):
            scores = dot(b.ka[s], queries)
            b.scores[s] = scores
            top = jnp.max(scores, axis=0, keepdims=True)
            peak = top if peak is None else jnp.maximum(peak, top)
        total = jnp.zeros((1, rows), F32)
        result = jnp.zeros((64, rows), F32)
        cols = slice(dp * 256, (dp + 1) * 256)
        for s in range(8):
            terms = jnp.exp2((b.scores[s] - peak) * EIGHTH_LOG2)
            total = total + jnp.sum(terms, axis=0, keepdims=True)
            low = terms.astype(BF)
            b.pairs[s * 256 : (s + 1) * 256, 1024 + dp * 256 : 1280 + dp * 256] = low
            result = result + dot(b.vt[s], low)
        share = 1.0 / total
        b.share[:, cols] = share
        result = result * share
        b.heads[:, cols] = result
        b.h_out[dp] = result.astype(BF)
        for dz in (3, 2, 1, 0):
            if dp or dz:
                sent_h[dp, dz] = net.copy(b.h_out.at[dp], b.h_in.at[plane, chip], at(dp, dz))
        if dp == 3:
            for one in sent_wo:
                net.arrived(one)
            sent_wo2 = {
                (to, dz): net.copy(
                    b.wo.at[planes[dz], chip, core], b.wo.at[planes[dz], chip, core], at(to, 0)
                )
                for dz in (1, 2, 3)
                for to in (3, 1, 2)
            }
    b.h_in[plane, chip] = b.h_out[0]

    for s in range(8):
        b.vn[s] = turned(b.vt[s]).astype(BF)
    for s in range(4):
        some = turned(b.q_in[s, 0:64])
        b.wide[s * 256 : (s + 1) * 256] = jnp.concatenate(
            [some * 0.125, jnp.zeros((rows, 64), F32)], axis=1
        ).astype(BF)
    l_f2.wait()
    for n in range(4):
        cols = slice(n * 256, (n + 1) * 256)
        b.dact[:, cols] = dot_nt(b.mg[...], b.f2[cols])
    l_wo.wait()
    for one in sent_wo2.values():
        net.arrived(one)
    sent_wo3 = [
        net.copy(b.wo.at[planes[dz], :, core], b.wo.at[planes[dz], :, core], mate)
        for dz in (1, 2, 3)
    ]

    for dz in range(4):
        for dp in range(4):
            if dp or dz:
                net.arrived(sent_h[dp, dz])
        if dz:
            net.arrived(sent_wo3[dz - 1])
        left = turned(b.h_in[planes[dz]].reshape(256, rows)).astype(BF)
        right = b.wo[planes[dz]].reshape(256, width)
        if dz:
            b.attn[...] += dot(left, right)
        else:
            b.attn[...] = dot(left, right)
    sent_hx = net.copy(b.h_in.at[plane, pl.ds(2 * other, 2)], b.h_mate, mate)


    def second_norm(which):
        value = b.tok[which].astype(F32) + per_token(0, which) * b.attn[which]
        b.hid[which] = value
        normed, _ = norm_rows(value)
        value = (normed * (1.0 + per_token(3, which)) + per_token(5, which)).astype(BF)
        b.b[0, which] = value[:, :half]
        b.b[1, which] = value[:, half:]

    for i in range(0, rows, 64):
        second_norm(slice(i, i + 64))
    l_f1.wait()
    for n in range(4):
        cols = slice(n * 256, (n + 1) * 256)
        up = dot(b.b[0], b.f1[:half, cols]) + dot(b.b[1], b.f1[half:, cols])
        square = up * up
        bent = jnp.tanh(GELU_A * up * (1.0 + GELU_B * square))
        gate = 0.5 * (1.0 + bent)
        slope = gate + 0.5 * up * (1.0 - bent * bent) * (GELU_A * (1.0 + 3.0 * GELU_B * square))
        b.act[n // 2, :, (n % 2) * 256 : (n % 2 + 1) * 256] = (up * gate).astype(BF)
        b.ug[:, cols] = (b.dact[:, cols] * slope).astype(BF)
    for n in range(4):
        cols = slice(n * 256, (n + 1) * 256)
        value = dot_nt(b.ug[...], b.f1[cols])
        b.bg_out[:, :, cols] = value.astype(BF).reshape(4, own, 256)
    sent_bg, far_bg = plane_scatter(b.bg_out, b.bg_in, b.bg_far)

    sent_x = [
        net.copy(b.act.at[other], b.act_in, mate),
        net.copy(b.b.at[other], b.b_in, mate),
        net.copy(b.ug, b.ug_in, mate),
    ]
    b.left[0] = turned(b.act[core]).astype(BF)
    net.arrived(sent_mg)
    net.arrived(sent_x[0])
    b.left[1] = turned(b.act_in[...]).astype(BF)
    for n in range(4):
        some = slice(n * 128, (n + 1) * 128)
        value = dot(b.left[0, some], b.mg[...]) + dot(b.left[1, some], b.mg_in[...])
        b.g2_out[n] = value.astype(BF).reshape(2, 64, width)
    sent_g2 = scatter(b.g2_out, b.g2_in)
    sent_bg.append(plane_scatter_on(far_bg, b.bg_out, b.bg_in, b.bg_far))
    b.left[0] = turned(b.b[core]).astype(BF)
    net.arrived(sent_x[1])
    b.left[1] = turned(b.b_in[...]).astype(BF)
    net.arrived(sent_x[2])
    for n in range(4):
        some = slice(n * 128, (n + 1) * 128)
        value = dot(b.left[0, some], b.ug[...]) + dot(b.left[1, some], b.ug_in[...])
        b.g1_out[n] = value.astype(BF).reshape(2, 64, width)
    sent_g1 = scatter(b.g1_out, b.g1_in)
    for n in range(4):
        cols = slice(n * 256, (n + 1) * 256)
        value = dot(b.act[0], b.f2[:half, cols]) + dot(b.act[1], b.f2[half:, cols])
        b.mo_out[:, :, cols] = value.astype(BF).reshape(4, own, 256)

    def mode_sums(k, value):
        high = value.astype(BF)
        low = (value - high.astype(F32)).astype(BF)
        picked = turned(b.pick[mine])[0:ITEM_ROWS].astype(BF)
        value = (dot(picked, high) + dot(picked, low))[0:8]
        b.ms[0, k * 8 : (k + 1) * 8] = value[:, :half]
        b.ms[1, k * 8 : (k + 1) * 8] = value[:, half:]

    b_grad = summed(sent_bg, b.bg_out[plane], b.bg_in)
    normed, inverse = norm_rows(b.hid[mine])
    h_grad = b.cot[mine].astype(F32) + norm_back(
        b_grad * (1.0 + per_token(3, mine)), normed, inverse
    )
    b.hg[...] = h_grad
    attn_grad = (per_token(0, mine) * h_grad).astype(BF)
    b.ag[plane] = attn_grad
    for n in range(4):
        value = dot_nt(attn_grad, b.wo[n].reshape(256, width)).astype(BF)
        for h in range(4):
            some = value[:, h * 64 : (h + 1) * 64]
            b.do_out[n, h] = jnp.concatenate([some[: own // 2], some[own // 2 :]], axis=1)
    sent_do = {
        (dp, dz): net.copy(
            b.do_out.at[planes[dz], chips[dp]], b.do_in.at[dp, plane], at(dp, dz)
        )
        for dp, dz in reversed(offsets)
    }
    b.do_in[0, plane] = b.do_out[plane, chip]
    sent_mo, far_mo = plane_scatter(b.mo_out, b.mo_in, b.mo_far)
    sent_ag = plane_gather(b.ag.at[plane], b.ag)
    mode_sums(0, h_grad * b.attn[mine])
    mode_sums(3, b_grad * normed)
    mode_sums(5, b_grad)
    sent_g2 = scatter_on(sent_g2, b.g2_out, b.g2_in)
    sent_g1 = scatter_on(sent_g1, b.g1_out, b.g1_in)

    for one in sent_do.values():
        net.arrived(one)
    for s in range(4):
        cols = slice(s * 256, (s + 1) * 256)
        for n in range(4):
            both = b.do_in[s, n]
            b.dn[n * own : n * own + own // 2] = both[:, 0:64]
            b.dn[n * own + own // 2 : (n + 1) * own] = both[:, 64:128]
        value = turned(b.dn[...])
        b.dt[:, cols] = value.astype(BF)
        b.delta[:, cols] = jnp.sum(value * b.heads[:, cols], axis=0, keepdims=True)
        b.wide[1024 + s * 256 : 1280 + s * 256] = jnp.concatenate(
            [jnp.zeros((rows, 64), F32), (value * b.share[:, cols]).T], axis=1
        ).astype(BF)

    def attend_back(s):
        keys = slice(s * 256, (s + 1) * 256)
        for q in range(4):
            cols = slice(q * 256, (q + 1) * 256)
            pull = (dot(b.vn[s], b.dt[:, cols]) - b.delta[:, cols]) * b.share[:, cols]
            terms = b.pairs[keys, 1024 + q * 256 : 1280 + q * 256]
            b.pairs[keys, cols] = (pull * terms.astype(F32)).astype(BF)
        b.dkv[s] = dot(b.pairs[keys], b.wide[...]).T

    for s in range(4, 8):
        attend_back(s)
    sent_dkv = net.copy(b.dkv.at[4:8], b.dkv_in, mate)
    for s in range(4):
        attend_back(s)
    value = (dot(b.ktw[...], b.pairs[:, 0:1024]) * 0.125).astype(BF)
    for s in range(4):
        b.dx_out[s, 0:64] = value[:, s * 256 : (s + 1) * 256]
    b.dx_in[chip, 0:64] = b.dx_out[0, 0:64]
    sent_dx = [
        net.copy(b.dx_out.at[dp, 0:64], b.dx_in.at[chip, 0:64], at(dp, 0)) for dp in (3, 1, 2)
    ]
    net.arrived(sent_dkv)
    for s in range(4):
        b.dx_out[s, 64:192] = (b.dkv[s] + b.dkv_in[s]).astype(BF)
    b.dx_in[chip, 64:192] = b.dx_out[0, 64:192]
    sent_dx += [
        net.copy(b.dx_out.at[dp, 64:192], b.dx_in.at[chip, 64:192], at(dp, 0)) for dp in (3, 1, 2)
    ]
    sent_mo.append(plane_scatter_on(far_mo, b.mo_out, b.mo_in, b.mo_far))
    sent_g2b = gather(sent_g2, b.g2_out, b.g2_in, b.g2, gf2_o)
    sent_g1b = gather(sent_g1, b.g1_out, b.g1_in, b.g1, gf1_o)
    sent_ag.append(plane_gather_on(sent_ag, b.ag))

    for one in sent_dx:
        net.arrived(one)
    sent_dxm = net.copy(b.dx_in, b.dx_mate, mate)
    for k in range(3):
        value = b.dx_in[:, k * 64 : (k + 1) * 64].reshape(256, rows)
        b.dx[k] = turned(value).astype(BF)
    for n in range(4):
        cols = slice(n * 256, (n + 1) * 256)
        value = dot_nt(b.dx[0], b.wq[0, cols])
        value = value + dot_nt(b.dx[1], b.wq[1, cols])
        value = value + dot_nt(b.dx[2], b.wq[2, cols])
        b.xg_out[:, :, cols] = value.astype(BF).reshape(4, own, 256)
    sent_xg, far_xg = plane_scatter(b.xg_out, b.xg_in, b.xg_far)

    net.arrived(sent_a)
    net.arrived(sent_dxm)
    for h in range(4):
        value = dot(b.dx_in[h], b.a[core]) + dot(b.dx_mate[h], b.a_in[...])
        b.gq_out[h] = value.astype(BF).reshape(2, 96, half)
    sent_gq = scatter(b.gq_out, b.gq_in)
    sent_xg.append(plane_scatter_on(far_xg, b.xg_out, b.xg_in, b.xg_far))

    sent_g2b += gather_on(sent_g2b, gf2_o)
    sent_g1b += gather_on(sent_g1b, gf1_o)

    mlp_out = summed(sent_mo, b.mo_out[plane], b.mo_in)
    b.out[...] = (b.hid[mine] + per_token(1, mine) * mlp_out).astype(BF)
    sent_out = plane_gather(b.out, out_o)
    load(b.out, out_o.at[plane])
    mode_sums(1, b.cot[mine].astype(F32) * mlp_out)

    for one in sent_ag[1:]:
        net.arrived(one)
    sent_agm = net.copy(b.ag, b.ag_in, mate)
    value = dot(
        b.h_in[plane, pl.ds(2 * core, 2)].reshape(128, rows), b.ag[...].reshape(rows, width)
    )
    net.arrived(sent_hx)
    net.arrived(sent_agm)
    value = value + dot(b.h_mate[...].reshape(128, rows), b.ag_in[...].reshape(rows, width))
    b.go_out[...] = value.astype(BF).reshape(4, 32, width)
    sent_go = [
        net.copy(b.go_out.at[chips[dp]], b.go_in.at[dp - 1], at(dp, 0)) for dp in (3, 1, 2)
    ]

    sent_gq = scatter_on(sent_gq, b.gq_out, b.gq_in)
    plane_gather_on(sent_out, out_o)

    a_grad = summed(sent_xg, b.xg_out[plane], b.xg_in)
    normed, inverse = norm_rows(b.tok[mine].astype(F32))
    mode_sums(2, a_grad * normed)
    mode_sums(4, a_grad)
    sent_ms = net.copy(b.ms.at[other], b.ms_in, mate)
    value = b.hg[...] + norm_back(a_grad * (1.0 + per_token(2, mine)), normed, inverse)
    b.dtok[...] = value.astype(BF)
    net.arrived(sent_ms)
    b.m1[...] = (b.ms[core] + b.ms_in[...]).astype(BF)
    sent_m1 = [net.copy(b.m1, b.m1_in.at[dz - 1], at(0, dz)) for dz in (3, 2, 1)]
    sent_dt = plane_gather(b.dtok, dtok_o)
    load(b.dtok, dtok_o.at[plane])

    sent_gqb = gather(sent_gq, b.gq_out, b.gq_in, b.gq, gqkv_o)
    b.go[...] = summed(sent_go, b.go_out[chip], b.go_in).astype(BF)
    sent_gob = [net.copy(b.go, gout_o.at[core, chip], at(dp, 0)) for dp in (3, 1, 2)]
    load(b.go, gout_o.at[core, chip])
    net.copy(b.go, gout_o.at[core, chip], mate)
    b.m2[...] = summed(sent_m1, b.m1[...], b.m1_in).astype(BF)
    sent_m2 = [net.copy(b.m2, b.m2_in.at[dp - 1], at(dp, 0)) for dp in (3, 1, 2)]
    plane_gather_on(sent_dt, dtok_o)

    def pass_on(sent, array):
        for one in sent:
            net.arrived(one)
        for dp in (1, 2, 3):
            where = (core, chips[dp])
            net.copy(array.at[where], array.at[where], mate)

    pass_on(sent_g2b[2:], gf2_o)
    pass_on(sent_g1b[2:], gf1_o)
    sent_gqb += gather_on(sent_gqb, gqkv_o)
    b.m3[...] = summed(sent_m2, b.m2[...], b.m2_in)
    net.copy(b.m3, mode_o.at[core], mate)
    load(b.m3, mode_o.at[core])
    some = pl.ds(pl.multiple_of(plane * part, part), part)
    side = pl.ds(pl.multiple_of(core * half, half), half)
    value = jnp.zeros((16, part), F32)
    for k in range(COMPONENTS):
        sums = b.m3[k * 8 : (k + 1) * 8]
        high = sums.astype(BF).astype(F32)
        both = jnp.concatenate([high, sums - high], axis=0).astype(BF)
        value = value + dot_nt(both, b.ada[k, some, side])
    b.cg[...] = value[0:8] + value[8:16]
    net.copy(b.cg, cg_o.at[core], mate)
    load(b.cg, cg_o.at[core])
    load(b.cond, cond_o)
    pass_on(sent_gob, gout_o)
    pass_on(sent_gqb[2:], gqkv_o)
    assert len(net.made) == COPIES and len(loads) == LOADS
    net.finish()
    for one in loads[first_store:]:
        one.wait()


def buffers(dims):
    rows, width, part, hidden, items, classes = dims
    own, half = rows // 4, width // 2
    return dict(
        tok=((rows, width), BF),
        cot=((rows, width), BF),
        table=((classes, width), BF),
        ada=((COMPONENTS, width, width), BF),
        wq=((3, width, part), BF),
        wo=((4, 4, 2, 32, width), BF),
        f1=((width, hidden), BF),
        f2=((hidden, width), BF),
        modes=((COMPONENTS, 3 * ITEM_ROWS, width), BF),
        pick=((rows, 3 * ITEM_ROWS), BF),
        cond=((ITEM_ROWS, width), F32),
        a=((2, rows, half), BF),
        a_in=((rows, half), BF),
        q_out=((4, 192, rows), BF),
        q_in=((4, 192, rows), BF),
        k_in=((4, 128, rows), BF),
        kt=((8, 128, rows), BF),
        ka=((8, rows, 128), BF),
        vt=((8, 64, rows), BF),
        vn=((8, rows, 64), BF),
        qt=((4, 128, rows), BF),
        ktw=((64, 2048), BF),
        wide=((2048, 128), BF),
        scores=((8, rows, rows), F32),
        pairs=((2048, 2048), BF),
        share=((1, 1024), F32),
        heads=((64, 1024), F32),
        h_out=((4, 64, rows), BF),
        h_in=((4, 4, 64, rows), BF),
        h_mate=((2, 64, rows), BF),
        attn=((rows, width), F32),
        hid=((rows, width), F32),
        b=((2, rows, half), BF),
        b_in=((rows, half), BF),
        act=((2, rows, half), BF),
        act_in=((rows, half), BF),
        mg=((rows, width), BF),
        mg_in=((rows, width), BF),
        ug=((rows, hidden), BF),
        ug_in=((rows, hidden), BF),
        dact=((rows, hidden), F32),
        left=((2, half, rows), BF),
        bg_out=((4, own, width), BF),
        bg_in=((3, own, width), BF),
        mo_out=((4, own, width), BF),
        mo_in=((3, own, width), BF),
        mo_far=((own, width), BF),
        bg_far=((own, width), BF),
        xg_far=((own, width), BF),
        xg_out=((4, own, width), BF),
        xg_in=((3, own, width), BF),
        g1_out=((4, 2, 64, width), BF),
        g1_in=((2, 3, 64, width), BF),
        g1=((2, 64, width), BF),
        g2_out=((4, 2, 64, width), BF),
        g2_in=((2, 3, 64, width), BF),
        g2=((2, 64, width), BF),
        hg=((own, width), F32),
        ag=((4, own, width), BF),
        ag_in=((4, own, width), BF),
        do_out=((4, 4, own // 2, 128), BF),
        do_in=((4, 4, own // 2, 128), BF),
        dn=((rows, 64), BF),
        dt=((64, 1024), BF),
        delta=((1, 1024), F32),
        dkv=((8, 128, rows), F32),
        dkv_in=((4, 128, rows), F32),
        dx_out=((4, 192, rows), BF),
        dx_mate=((4, 192, rows), BF),
        dx_in=((4, 192, rows), BF),
        dx=((3, rows, part), BF),
        gq_out=((4, 2, 96, half), BF),
        gq_in=((2, 3, 96, half), BF),
        gq=((2, 96, half), BF),
        out=((own, width), BF),
        dtok=((own, width), BF),
        go_out=((4, 32, width), BF),
        go_in=((3, 32, width), BF),
        go=((32, width), BF),
        ms=((2, 48, half), F32),
        ms_in=((48, half), F32),
        m1=((48, half), BF),
        m1_in=((3, 48, half), BF),
        m2=((48, half), BF),
        m2_in=((3, 48, half), BF),
        m3=((48, half), F32),
        cg=((8, part), F32),
    )


def finish_kernel(
    cls_s, out_i, dtok_i, gqkv_i, gout_i, gf1_i, gf2_i, mode_i, cond_i, cg_i,
    out_o, dtok_o, table_o, ada_o, qkv_o, wout_o, f1_o, f2_o,
):
    step, last = pl.program_id(0), pl.num_programs(0) - 1
    plane = lax.axis_index("head")
    part = table_o.shape[1]
    mine = pl.ds(pl.multiple_of(plane * part, part), part)
    out_o[...] = out_i[0]
    dtok_o[...] = dtok_i[0]
    wout_o[...] = gout_i[0, 0].astype(F32)
    f1_o[...] = gf1_i[0, 0].astype(F32).reshape(f1_o.shape)
    f2_o[...] = gf2_i[0, 0].astype(F32).reshape(f2_o.shape)
    sums = gqkv_i[0].astype(F32).reshape(4, 192, 128)
    for k in range(3):
        qkv_o[k] = sums[:, k * 64 : (k + 1) * 64].reshape(part, 128).T
    cond = cond_i[:, pl.ds(pl.multiple_of(step * 128, 128), 128)]
    cond_low = (cond / (1.0 + jnp.exp(-cond)))[0:8]
    low = jnp.concatenate([cond_low, cond_low], axis=0).astype(BF)
    side = pl.ds(pl.multiple_of(lax.rem(plane, 2) * part, part), part)
    for k in range(COMPONENTS):
        value = mode_i[lax.div(plane, 2), k * 8 : (k + 1) * 8, side]
        high = value.astype(BF).astype(F32)
        both = jnp.concatenate([high, value - high], axis=0).astype(BF)
        ada_o[k] = dot_tn(low, both)

    @pl.when(step == last)
    def _():
        own = cond_i[0:8, mine]
        gate = 1.0 / (1.0 + jnp.exp(-own))
        grad = (cg_i[0] + cg_i[1]) * gate * (1.0 + own * (1.0 - gate))
        spot = lax.broadcasted_iota(jnp.int32, table_o.shape, 0)
        total = jnp.zeros(table_o.shape, F32)
        for i in range(cls_s.shape[0]):
            total = total + jnp.where(spot == cls_s[i], grad[i : i + 1], 0.0)
        table_o[...] = total


def finish(
    class_ids,
    output,
    d_tokens,
    qkv_sum,
    out_sum,
    fc1_sum,
    fc2_sum,
    mode_grad,
    cond,
    cond_grad,
    classes,
):
    steps = 8
    own, width = output.shape[1:]
    half, part, hidden = width // 2, width // 4, steps * 128
    rows = own * 4
    smem = pl.BlockSpec(memory_space=pltpu.SMEM)
    few = pl.BlockSpec((1, own // 2, width), lambda i: (i // 2, i % 2, 0))
    table, ada, qkv, out, fc1, fc2 = (
        (classes, part),
        (COMPONENTS, width, part),
        (3, width, part),
        (part, width),
        (width, hidden),
        (hidden, width),
    )
    output, d_tokens, table, ada, qkv, out, fc1, fc2 = pl.pallas_call(
        finish_kernel,
        grid=(steps,),
        out_shape=[
            jax.ShapeDtypeStruct((rows, width), BF),
            jax.ShapeDtypeStruct((rows, width), BF),
        ]
        + [jax.ShapeDtypeStruct(shape, F32) for shape in (table, ada, qkv, out, fc1, fc2)],
        in_specs=[
            smem,
            few,
            few,
            pl.BlockSpec((1, 4, 2, 96, half // 4), lambda i: (i // 4, 0, 0, 0, i % 4)),
            pl.BlockSpec((1, 1, 32, width), lambda i: (i // 4, i % 4, 0, 0)),
            pl.BlockSpec((1, 1, 2, 64, hidden), lambda i: (i // 4, i % 4, 0, 0, 0)),
            pl.BlockSpec((1, 1, 2, 64, width), lambda i: (i // 4, i % 4, 0, 0, 0)),
            pl.BlockSpec((2, 48, half), lambda i: (0, 0, 0)),
            pl.BlockSpec((ITEM_ROWS, width), lambda i: (0, 0)),
            pl.BlockSpec((2, 8, part), lambda i: (0, 0, 0)),
        ],
        out_specs=[
            pl.BlockSpec((rows // steps, width), lambda i: (i, 0)),
            pl.BlockSpec((rows // steps, width), lambda i: (i, 0)),
            pl.BlockSpec((classes, part), lambda i: (0, 0)),
            pl.BlockSpec((COMPONENTS, 128, part), lambda i: (0, i, 0)),
            pl.BlockSpec((3, 128, part), lambda i: (0, i, 0)),
            pl.BlockSpec((32, width), lambda i: (i, 0)),
            pl.BlockSpec((128, hidden), lambda i: (i, 0)),
            pl.BlockSpec((128, width), lambda i: (i, 0)),
        ],
        compiler_params=pltpu.CompilerParams(vmem_limit_bytes=VMEM_BYTES),
    )(
        class_ids, output, d_tokens, qkv_sum, out_sum, fc1_sum, fc2_sum, mode_grad, cond, cond_grad
    )
    return output, d_tokens, table, ada, qkv.transpose(1, 0, 2), out, fc1, fc2


def on_block(
    tokens,
    class_ids,
    slot_item,
    slot_scale,
    class_table,
    w_ada,
    w_qkv,
    w_out,
    w_fc1,
    w_fc2,
    cotangent,
):
    rows, width = tokens.shape
    part, hidden = w_qkv.shape[2], w_fc1.shape[1]
    items, classes = class_ids.shape[0], class_table.shape[0]
    own, half = rows // 4, width // 2
    dims = (rows, width, part, hidden, items, classes)
    scratch = [pltpu.VMEM(shape, dtype) for shape, dtype in buffers(dims).values()]
    anywhere = pl.BlockSpec(memory_space=pl.ANY)
    vmem = pl.BlockSpec(memory_space=pltpu.VMEM)
    smem = pl.BlockSpec(memory_space=pltpu.SMEM)
    output, d_tokens, qkv_sum, out_sum, fc1_sum, fc2_sum, mode_grad, cond, cond_grad = pl.pallas_call(
        functools.partial(block_kernel, dims),
        out_shape=[
            jax.ShapeDtypeStruct((4, own, width), BF),
            jax.ShapeDtypeStruct((4, own, width), BF),
            jax.ShapeDtypeStruct((2, 4, 2, 96, half), BF),
            jax.ShapeDtypeStruct((2, 4, 32, width), BF),
            jax.ShapeDtypeStruct((2, 4, 2, 64, width), BF),
            jax.ShapeDtypeStruct((2, 4, 2, 64, width), BF),
            jax.ShapeDtypeStruct((2, 48, half), F32),
            jax.ShapeDtypeStruct((ITEM_ROWS, width), F32),
            jax.ShapeDtypeStruct((2, 8, part), F32),
        ],
        in_specs=[anywhere, smem, vmem, vmem] + [anywhere] * 7,
        out_specs=[anywhere] * 9,
        scratch_shapes=[
            pltpu.SemaphoreType.DMA((COPIES,)),
            pltpu.SemaphoreType.DMA((COPIES,)),
            pltpu.SemaphoreType.DMA((LOADS,)),
            *scratch,
        ],
        compiler_params=pltpu.CompilerParams(
            collective_id=0, has_side_effects=True, vmem_limit_bytes=VMEM_BYTES
        ),
        cost_estimate=pl.CostEstimate(
            flops=10_000_000_000, bytes_accessed=40_000_000, transcendentals=3_000_000
        ),
    )(
        tokens,
        class_ids,
        slot_item.reshape(8, 1, rows),
        slot_scale.reshape(8, 1, rows),
        class_table,
        w_ada,
        w_qkv.transpose(1, 0, 2),
        w_out.reshape(4, 2, 32, width),
        w_fc1,
        w_fc2,
        cotangent,
    )
    return finish(
        class_ids, output, d_tokens, qkv_sum, out_sum, fc1_sum, fc2_sum, mode_grad, cond, cond_grad,
        classes,
    )


def fits(mesh):
    return mesh.shape["tok"] == 8 and mesh.shape["head"] == 4


def layer_norm(values):
    centre = jnp.mean(values, axis=-1, keepdims=True)
    shifted = values - centre
    spread = jnp.mean(shifted * shifted, axis=-1, keepdims=True)
    return shifted * lax.rsqrt(spread + EPS)


def modulate(values, scale_in, shift_in):
    return layer_norm(values) * (1.0 + scale_in) + shift_in


def pair_scores(queries, key_block, query_item, key_item, query_scale, key_scale):
    scores = (
        jnp.einsum("qhd,khd->hqk", queries, key_block, preferred_element_type=jnp.float32) * 0.125
    )
    allowed = (
        (query_item[:, None] == key_item[None, :]) & (key_scale[None, :] <= query_scale[:, None])
    )[None]
    return (jnp.where(allowed, scores, -1e30), allowed)


def on_device(
    tokens,
    class_ids,
    slot_item,
    slot_scale,
    class_table,
    w_ada,
    w_qkv,
    w_out,
    w_fc1,
    w_fc2,
    cotangent,
):
    tok_rows, full_width = tokens.shape
    slot_count = slot_item.shape[0]
    item_count = class_ids.shape[0]
    class_count = class_table.shape[0]
    local_width = w_qkv.shape[2]
    local_heads = local_width // HEAD_DIM
    anchor = lax.axis_index("tok") * tok_rows
    first_col = lax.axis_index("head") * local_width
    my_item = lax.dynamic_slice_in_dim(slot_item, anchor, tok_rows)
    my_scale = lax.dynamic_slice_in_dim(slot_scale, anchor, tok_rows)
    class_pick = (class_ids[:, None] == jnp.arange(class_count, dtype=jnp.int32)[None, :]).astype(
        jnp.bfloat16
    )
    cond = jnp.dot(class_pick, class_table, preferred_element_type=jnp.float32)
    silu_cond, silu_back = jax.vjp(jax.nn.silu, cond)
    cond_low = silu_cond.astype(jnp.bfloat16)
    modes = jnp.einsum("id,cde->ice", cond_low, w_ada, preferred_element_type=jnp.float32)
    item_pick = (my_item[:, None] == jnp.arange(item_count, dtype=jnp.int32)[None, :]).astype(
        jnp.float32
    )
    per_token = jnp.dot(
        item_pick, modes.reshape(item_count, 6 * full_width), precision=HIGH
    ).reshape(tok_rows, 6, full_width)
    gamma_one = per_token[:, 0]
    gamma_two = per_token[:, 1]
    scale_one = per_token[:, 2]
    scale_two = per_token[:, 3]
    shift_one = per_token[:, 4]
    shift_two = per_token[:, 5]
    tok_float = tokens.astype(jnp.float32)
    a_pre, a_back = jax.vjp(modulate, tok_float, scale_one, shift_one)
    a_low = a_pre.astype(jnp.bfloat16)
    qkv_low = jnp.einsum("td,dce->tce", a_low, w_qkv, preferred_element_type=jnp.float32).astype(
        jnp.bfloat16
    )
    queries = qkv_low[:, 0]
    key_own = qkv_low[:, 1]
    value_own = qkv_low[:, 2]
    query_heads = queries.reshape(tok_rows, local_heads, HEAD_DIM)
    key_all, value_all = (
        lax.all_gather(key_own, "tok", axis=0, tiled=True),
        lax.all_gather(value_own, "tok", axis=0, tiled=True),
    )
    block_rows = math.gcd(slot_count, 2048)
    blocks = slot_count // block_rows
    key_blocks = key_all.reshape(blocks, block_rows, local_heads, HEAD_DIM)
    value_blocks = value_all.reshape(blocks, block_rows, local_heads, HEAD_DIM)
    item_blocks = slot_item.reshape(blocks, block_rows)
    scale_blocks = slot_scale.reshape(blocks, block_rows)
    key_wanted = jnp.min(scale_blocks, axis=1) <= jnp.max(my_scale)

    def first_pass(running, inputs):
        key_block, item_block, scale_block, wanted = inputs

        def first_compute_block(state_now):
            scores, allowed = pair_scores(
                query_heads, key_block, my_item, item_block, my_scale, scale_block
            )
            new_peak = jnp.maximum(state_now[0], jnp.max(scores, axis=2))
            terms = jnp.where(allowed, jnp.exp(scores - new_peak[:, :, None]), 0.0)
            return (
                new_peak,
                state_now[1] * jnp.exp(state_now[0] - new_peak) + jnp.sum(terms, axis=2),
            )

        return (lax.cond(wanted, first_compute_block, lambda state_now: state_now, running), None)

    initial = (
        jnp.full((local_heads, tok_rows), -1e30, jnp.float32),
        jnp.zeros((local_heads, tok_rows), jnp.float32),
    )
    (row_peak, summed), _ = lax.scan(
        first_pass, initial, (key_blocks, item_blocks, scale_blocks, key_wanted)
    )
    log_total = row_peak + jnp.log(summed)

    def second_pass(running, inputs):
        key_block, value_block, item_block, scale_block, wanted = inputs

        def second_compute_block(total_now):
            scores, allowed = pair_scores(
                query_heads, key_block, my_item, item_block, my_scale, scale_block
            )
            rounded = jnp.where(allowed, jnp.exp(scores - log_total[:, :, None]), 0.0).astype(
                jnp.bfloat16
            )
            return total_now + jnp.einsum(
                "hqk,khd->qhd", rounded, value_block, preferred_element_type=jnp.float32
            )

        return (lax.cond(wanted, second_compute_block, lambda total_now: total_now, running), None)

    heads_out, _ = lax.scan(
        second_pass,
        jnp.zeros((tok_rows, local_heads, HEAD_DIM), jnp.float32),
        (key_blocks, value_blocks, item_blocks, scale_blocks, key_wanted),
    )
    heads_low = heads_out.reshape(tok_rows, local_width).astype(jnp.bfloat16)
    attn_out = lax.psum(
        jnp.dot(heads_low, w_out, preferred_element_type=jnp.float32).astype(jnp.bfloat16), "head"
    ).astype(jnp.float32)
    hidden = tok_float + gamma_one * attn_out
    b_pre, b_back = jax.vjp(modulate, hidden, scale_two, shift_two)
    b_low = b_pre.astype(jnp.bfloat16)
    up_proj = jnp.dot(b_low, w_fc1, preferred_element_type=jnp.float32)
    act_pre, act_back = jax.vjp(lambda values: jax.nn.gelu(values, approximate=True), up_proj)
    act_low = act_pre.astype(jnp.bfloat16)
    mlp_out = lax.psum(
        jnp.dot(act_low, w_fc2, preferred_element_type=jnp.float32).astype(jnp.bfloat16), "head"
    ).astype(jnp.float32)
    output = (hidden + gamma_two * mlp_out).astype(jnp.bfloat16)
    out_grad = cotangent.astype(jnp.float32)
    mlp_grad = (gamma_two * out_grad).astype(jnp.bfloat16)
    fc2_weight_grad = jnp.einsum("tf,td->fd", act_low, mlp_grad, preferred_element_type=jnp.float32)
    act_grad = jnp.einsum("td,fd->tf", mlp_grad, w_fc2, preferred_element_type=jnp.float32)
    up_grad = act_back(act_grad)[0].astype(jnp.bfloat16)
    fc1_weight_grad = jnp.einsum("td,tf->df", b_low, up_grad, preferred_element_type=jnp.float32)
    b_grad = lax.psum(
        jnp.einsum("tf,df->td", up_grad, w_fc1, preferred_element_type=jnp.float32).astype(
            jnp.bfloat16
        ),
        "head",
    ).astype(jnp.float32)
    hidden_part, scale_two_grad, shift_two_grad = b_back(b_grad)
    hidden_grad = out_grad + hidden_part
    attn_grad = (gamma_one * hidden_grad).astype(jnp.bfloat16)
    out_weight_grad = jnp.einsum(
        "tf,te->fe", heads_low, attn_grad, preferred_element_type=jnp.float32
    )
    grad_low = jnp.einsum("te,fe->tf", attn_grad, w_out, preferred_element_type=jnp.float32).astype(
        jnp.bfloat16
    )
    grad_heads = grad_low.reshape(tok_rows, local_heads, HEAD_DIM)
    delta = jnp.einsum("qhd,qhd->hq", grad_heads.astype(jnp.float32), heads_out)

    def step_block(running, inputs):
        key_block, value_block, item_block, scale_block, wanted = inputs

        def step_compute_block(total_now):
            scores, allowed = pair_scores(
                query_heads, key_block, my_item, item_block, my_scale, scale_block
            )
            weights = jnp.where(allowed, jnp.exp(scores - log_total[:, :, None]), 0.0)
            weight_grad = jnp.einsum(
                "qhd,khd->hqk", grad_heads, value_block, preferred_element_type=jnp.float32
            )
            score_grad = (weights * (weight_grad - delta[:, :, None])).astype(jnp.bfloat16)
            total_now = (
                total_now
                + jnp.einsum(
                    "hqk,khd->qhd", score_grad, key_block, preferred_element_type=jnp.float32
                )
                * 0.125
            )
            key_term = (
                jnp.einsum(
                    "hqk,qhd->khd", score_grad, query_heads, preferred_element_type=jnp.float32
                )
                * 0.125
            )
            value_term = jnp.einsum(
                "hqk,qhd->khd",
                weights.astype(jnp.bfloat16),
                grad_heads,
                preferred_element_type=jnp.float32,
            )
            return (total_now, (key_term, value_term))

        def skip_block(total_now):
            nothing = jnp.zeros((block_rows, local_heads, HEAD_DIM), jnp.float32)
            return (total_now, (nothing, nothing))

        return lax.cond(wanted, step_compute_block, skip_block, running)

    query_grad, (key_terms, value_terms) = lax.scan(
        step_block,
        jnp.zeros((tok_rows, local_heads, HEAD_DIM), jnp.float32),
        (key_blocks, value_blocks, item_blocks, scale_blocks, key_wanted),
    )
    key_grad, value_grad = (
        lax.psum_scatter(
            key_terms.reshape(slot_count, local_width), "tok", scatter_dimension=0, tiled=True
        ),
        lax.psum_scatter(
            value_terms.reshape(slot_count, local_width), "tok", scatter_dimension=0, tiled=True
        ),
    )
    qkv_grad = jnp.stack(
        [query_grad.reshape(tok_rows, local_width), key_grad, value_grad], axis=1
    ).astype(jnp.bfloat16)
    qkv_weight_grad = jnp.einsum("td,tce->dce", a_low, qkv_grad, preferred_element_type=jnp.float32)
    a_grad = lax.psum(
        jnp.einsum("tce,dce->td", qkv_grad, w_qkv, preferred_element_type=jnp.float32).astype(
            jnp.bfloat16
        ),
        "head",
    ).astype(jnp.float32)
    tok_part, scale_one_grad, shift_one_grad = a_back(a_grad)
    d_tokens = (hidden_grad + tok_part).astype(jnp.bfloat16)
    token_modes = jnp.stack(
        [
            hidden_grad * attn_out,
            out_grad * mlp_out,
            scale_one_grad,
            scale_two_grad,
            shift_one_grad,
            shift_two_grad,
        ],
        axis=1,
    )
    mode_part = jnp.einsum(
        "ti,tf->if", item_pick, token_modes.reshape(tok_rows, 6 * full_width), precision=HIGH
    ).reshape(item_count, 6, full_width)
    qkv_sum, out_sum, fc1_sum, fc2_sum, mode_grad = lax.psum(
        (qkv_weight_grad, out_weight_grad, fc1_weight_grad, fc2_weight_grad, mode_part), "tok"
    )
    cond_grad = jnp.zeros((item_count, full_width), jnp.float32)
    for component in range(6):
        cond_grad = cond_grad + jnp.dot(
            mode_grad[:, component], w_ada[component].astype(jnp.float32).T, precision=HIGH
        )
    pre_grad = silu_back(cond_grad)[0]
    own_pre = lax.dynamic_slice_in_dim(pre_grad, first_col, local_width, 1)
    table_grad = jnp.einsum("ic,id->cd", class_pick.astype(jnp.float32), own_pre, precision=HIGH)
    own_modes = lax.dynamic_slice_in_dim(mode_grad, first_col, local_width, 2)
    ada_grad = jnp.einsum("id,ice->cde", cond_low.astype(jnp.float32), own_modes, precision=HIGH)
    return (output, d_tokens, table_grad, ada_grad, qkv_sum, out_sum, fc1_sum, fc2_sum)


def solution(mesh):
    placed = (
        P("tok", None),
        P(),
        P(),
        P(),
        P(),
        P(),
        P(None, None, "head"),
        P("head", None),
        P(None, "head"),
        P("head", None),
        P("tok", None),
    )
    return jax.shard_map(
        on_block if fits(mesh) else on_device,
        mesh=mesh,
        in_specs=placed,
        out_specs=(
            P("tok", None),
            P("tok", None),
            P(None, "head"),
            P(None, None, "head"),
            P(None, None, "head"),
            P("head", None),
            P(None, "head"),
            P("head", None),
        ),
        check_vma=False,
    )
```

```python
import functools
import math
import types

import jax
import jax.numpy as jnp
from jax import lax
from jax.experimental import pallas as pl
from jax.experimental.pallas import tpu as pltpu
from jax.sharding import PartitionSpec as P

HEAD_DIM = 64
COMPONENTS = 6


EPS = 1e-06
HIGH = lax.Precision.HIGHEST
BF = jnp.bfloat16
F32 = jnp.float32
MESH = pl.DeviceIdType.MESH
BARRED = -1e30
EIGHTH_LOG2 = 0.125 * math.log2(math.e)
GELU_A = math.sqrt(2.0 / math.pi)
GELU_B = 0.044715
COPIES = 164
LOADS = 22
VMEM_BYTES = 62 * 1024 * 1024
ITEM_ROWS = 16


def dot(left, right):
    return lax.dot_general(left, right, (((1,), (0,)), ((), ())), preferred_element_type=F32)


def dot_nt(left, right):
    return lax.dot_general(left, right, (((1,), (1,)), ((), ())), preferred_element_type=F32)


def dot_tn(left, right):
    return lax.dot_general(left, right, (((0,), (0,)), ((), ())), preferred_element_type=F32)


def turned(block):
    return block.astype(F32).T


def norm_rows(values):
    shifted = values - jnp.mean(values, axis=-1, keepdims=True)
    inverse = lax.rsqrt(jnp.mean(shifted * shifted, axis=-1, keepdims=True) + EPS)
    return shifted * inverse, inverse


def norm_back(grad, normed, inverse):
    along = jnp.mean(grad * normed, axis=-1, keepdims=True)
    return (grad - jnp.mean(grad, axis=-1, keepdims=True) - normed * along) * inverse


class Net:
    def __init__(self, send, arrive):
        self.send, self.arrive = send, arrive
        self.made, self.waited = [], []

    def copy(self, source, target, device, when=None, gets=None):
        k = len(self.made)
        one = pltpu.make_async_remote_copy(
            src_ref=source,
            dst_ref=target,
            send_sem=self.send.at[k],
            recv_sem=self.arrive.at[k],
            device_id=device,
            device_id_type=MESH,
        )
        self.made.append((one, when, gets))
        on_some(when, one.start)
        return k

    def arrived(self, k):
        one, _, gets = self.made[k]
        on_some(gets, one.wait_recv)
        self.waited.append(k)

    def finish(self):
        for k, (one, when, _) in enumerate(self.made):
            on_some(when, one.wait_send)
            if k not in self.waited:
                self.arrived(k)


def on_some(when, act):
    if when is None:
        act()
    else:
        pl.when(when)(act)


def block_kernel(dims, *refs):
    rows, width, part, hidden, items, classes = dims
    names = list(buffers(dims))
    (
        tok_h, cls_s, item_v, scale_v, table_h, ada_h, wq_h, wo_h, f1_h, f2_h, cot_h,
        out_o, dtok_o, gqkv_o, gout_o, gf1_o, gf2_o, mode_o, cond_o, cg_o,
        send_sem, arrive_sem, load_sem, *scratch,
    ) = refs
    b = types.SimpleNamespace(**dict(zip(names, scratch, strict=True)))
    own = rows // 4
    half = width // 2
    net = Net(send_sem, arrive_sem)
    loads = []

    def load(source, target):
        one = pltpu.make_async_copy(source, target, load_sem.at[len(loads)])
        one.start()
        loads.append(one)
        return one

    group = lax.axis_index("tok")
    plane = lax.axis_index("head")
    core = lax.rem(group, 2)
    chip = lax.div(group, 2)
    col, line = lax.rem(chip, 2), lax.div(chip, 2)
    chips = [chip, line * 2 + 1 - col, (1 - line) * 2 + col, 3 - chip]
    planes = [
        plane,
        lax.div(plane, 2) * 2 + 1 - lax.rem(plane, 2),
        lax.rem(plane + 2, 4),
        3 - plane,
    ]
    other = 1 - core
    inner = (plane == 1) | (plane == 2)
    outer = (plane == 0) | (plane == 3)
    offsets = [(dp, dz) for dz in range(4) for dp in range(4) if dp or dz]

    def at(dp, dz):
        return (chips[dp] * 2 + core, planes[dz])

    mate = (chip * 2 + other, plane)
    mine = pl.ds(pl.multiple_of(plane * own, own), own)

    def summed(sent, kept, arrived):
        for one in sent:
            net.arrived(one)
        total = kept.astype(F32)
        for k in range(3):
            total = total + arrived[k].astype(F32)
        return total

    ways = ((0, 1, 2), (1, 2, 1))

    def scatter(blocks, arrived):
        return [
            net.copy(blocks.at[chips[which], way], arrived.at[way, n], at(first, 0))
            for n, pick in ((1, 3), (0, None))
            for way, first, _ in ways
            for which in (pick or first,)
        ]

    def scatter_on(sent, blocks, arrived):
        for one in sent:
            net.arrived(one)
        for way, _, then in ways:
            total = blocks[chips[then], way].astype(F32) + arrived[way, 1].astype(F32)
            blocks[chips[then], way] = total.astype(BF)
        return [
            net.copy(blocks.at[chips[then], way], arrived.at[way, 2], at(then, 0))
            for way, _, then in ways
        ]

    def gather(sent, blocks, arrived, total, target):
        for one in sent:
            net.arrived(one)
        for way, _, _ in ways:
            total[way] = (
                blocks[chip, way].astype(F32)
                + arrived[way, 0].astype(F32)
                + arrived[way, 2].astype(F32)
            ).astype(BF)
        load(total, target.at[core, chip])
        net.copy(total, target.at[core, chip], mate)
        return [
            net.copy(total.at[way], target.at[core, chip, way], at(dp, 0))
            for way, dp in ((0, 2), (1, 1), (0, 1), (1, 2))
        ]

    def gather_on(sent, target):
        for one in sent[:2]:
            net.arrived(one)
        return [
            net.copy(
                target.at[core, chips[then], way], target.at[core, chips[then], way], at(first, 0)
            )
            for way, first, then in ways
        ]

    def plane_scatter(blocks, arrived, far):
        far_sent = net.copy(blocks.at[planes[3]], far, at(0, 1), outer, inner)
        sent = [
            net.copy(blocks.at[planes[2]], arrived.at[1], at(0, 2), outer, inner),
            net.copy(blocks.at[planes[3]], arrived.at[2], at(0, 3), inner, inner),
            net.copy(blocks.at[planes[1]], arrived.at[0], at(0, 1)),
        ]

        @pl.when(outer)
        def _():
            arrived[2] = jnp.zeros(arrived.shape[1:], BF)

        return sent, far_sent

    def plane_scatter_on(far_sent, blocks, arrived, far):
        net.arrived(far_sent)

        @pl.when(inner)
        def _():
            total = blocks[planes[2]].astype(F32) + far[...].astype(F32)
            blocks[planes[2]] = total.astype(BF)

        return net.copy(blocks.at[planes[2]], arrived.at[1], at(0, 2), inner, outer)

    def plane_gather(source, target):
        return [
            net.copy(source, target.at[plane], at(0, 2)),
            net.copy(source, target.at[plane], at(0, 3), inner, inner),
            net.copy(source, target.at[plane], at(0, 1)),
        ]

    def plane_gather_on(sent, target):
        net.arrived(sent[0])
        return net.copy(target.at[planes[2]], target.at[planes[2]], at(0, 1), inner, outer)

    l_table = load(table_h, b.table)
    l_ada = {k: load(ada_h.at[k], b.ada.at[k]) for k in (2, 4)}
    l_tok = load(tok_h, b.tok)
    l_wq = load(wq_h, b.wq)
    barrier = pltpu.get_barrier_semaphore()
    for dp, dz in offsets:
        pl.semaphore_signal(barrier, inc=1, device_id=at(dp, dz), device_id_type=MESH)
    pl.semaphore_signal(barrier, inc=1, device_id=mate, device_id_type=MESH)

    spot = lax.rem(lax.broadcasted_iota(jnp.int32, (3 * ITEM_ROWS, rows), 0), ITEM_ROWS)
    picks = jnp.where(spot == item_v[group], 1.0, 0.0)
    b.pick[...] = picks.T.astype(BF)

    spot = lax.broadcasted_iota(jnp.int32, (ITEM_ROWS, classes), 0)
    label = lax.broadcasted_iota(jnp.int32, (ITEM_ROWS, classes), 1)
    hot = jnp.zeros((ITEM_ROWS, classes), F32)
    for i in range(items):
        hot = jnp.where((spot == i) & (label == cls_s[i]), 1.0, hot)
    l_table.wait()
    cond = dot(hot.astype(BF), b.table[...])
    b.cond[...] = cond
    cond_low = (cond / (1.0 + jnp.exp(-cond))).astype(BF)

    def make_mode(k):
        l_ada[k].wait()
        value = dot(cond_low, b.ada[k])
        high = value.astype(BF)
        rest = value - high.astype(F32)
        middle = rest.astype(BF)
        b.modes[k, 0:ITEM_ROWS] = high
        b.modes[k, ITEM_ROWS : 2 * ITEM_ROWS] = middle
        b.modes[k, 2 * ITEM_ROWS : 3 * ITEM_ROWS] = (rest - middle.astype(F32)).astype(BF)

    def per_token(k, which):
        return dot(b.pick[which], b.modes[k])

    def chunks(body):
        def step(i, carry):
            body(pl.ds(pl.multiple_of(i * 64, 64), 64))
            return carry

        lax.fori_loop(0, rows // 64, step, 0)

    make_mode(2)
    make_mode(4)

    l_tok.wait()

    def first_norm(which):
        normed, _ = norm_rows(b.tok[which].astype(F32))
        value = (normed * (1.0 + per_token(2, which)) + per_token(4, which)).astype(BF)
        b.a[0, which] = value[:, :half]
        b.a[1, which] = value[:, half:]

    for i in range(0, rows, 64):
        first_norm(slice(i, i + 64))
    l_wq.wait()
    l_wo = load(wo_h, b.wo.at[plane])
    l_ada.update({k: load(ada_h.at[k], b.ada.at[k]) for k in (0, 3, 5, 1)})
    l_cot = load(cot_h, b.cot)
    l_f2 = load(f2_h, b.f2)
    l_f1 = load(f1_h, b.f1)
    first_store = len(loads)
    for k in range(3):
        value = dot(b.a[0], b.wq[k, :half]) + dot(b.a[1], b.wq[k, half:])
        value = value.T.astype(BF)
        for h in range(4):
            b.q_out[h, k * 64 : (k + 1) * 64] = value[h * 64 : (h + 1) * 64]
    pl.semaphore_wait(barrier, len(offsets) + 1)
    sent_q = {
        (dp, n): net.copy(b.q_out.at[chips[dp], part_of], b.q_in.at[dp, part_of], at(dp, 0))
        for n, part_of in enumerate((slice(64, 192), slice(0, 64)))
        for dp in (3, 1, 2)
    }
    b.q_in[0] = b.q_out[chip]
    sent_k = [net.copy(b.q_in.at[0, 64:192], b.k_in.at[0], mate)]
    sent_a = net.copy(b.a.at[other], b.a_in, mate)
    sent_wo = [
        net.copy(wo_h.at[chip, core], b.wo.at[plane, chip, core], at(0, dz)) for dz in (3, 2, 1)
    ]

    spot = lax.broadcasted_iota(jnp.int32, (64, rows), 0)
    for s in range(4):
        for k, parity in enumerate((core, other)):
            item, scale = item_v[chips[s] * 2 + parity], scale_v[chips[s] * 2 + parity]
            by_item = jnp.where(item != spot - 1, BARRED, 0.0)
            by_scale = jnp.where((spot < 32) & (scale > spot - 16), BARRED, 0.0)
            b.kt[k * 4 + s, 64:128] = jnp.where(spot < 16, by_item, by_scale).astype(BF)
        item, scale = item_v[chips[s] * 2 + core], scale_v[chips[s] * 2 + core]
        by_item = jnp.where(item == spot - 1, 1.0, 0.0)
        by_scale = jnp.where((spot < 32) & (scale == spot - 16), 1.0, 0.0)
        b.qt[s, 64:128] = jnp.where(spot < 16, by_item, by_scale).astype(BF)
    make_mode(0)
    make_mode(3)
    make_mode(5)
    make_mode(1)
    l_cot.wait()

    def mlp_grad(which):
        b.mg[which] = (per_token(1, which) * b.cot[which].astype(F32)).astype(BF)

    chunks(mlp_grad)
    for dp in (3, 1, 2):
        net.arrived(sent_q[dp, 0])
        sent_k.append(net.copy(b.q_in.at[dp, 64:192], b.k_in.at[dp], mate))

    def take_keys(s, block):
        b.kt[s, 0:64] = block[0:64]
        b.ktw[:, s * 256 : (s + 1) * 256] = block[0:64]
        b.vt[s] = block[64:128]
        b.ka[s] = turned(b.kt[s]).astype(BF)

    for s in range(4):
        take_keys(s, b.q_in[s, 64:192])
    for dp in (3, 1, 2):
        net.arrived(sent_q[dp, 1])
    for s in range(4):
        b.qt[s, 0:64] = b.q_in[s, 0:64]
    for one in sent_k:
        net.arrived(one)
    for s in range(4):
        take_keys(4 + s, b.k_in[s])
    sent_mg = net.copy(b.mg, b.mg_in, mate)

    sent_h = {}
    for dp in (3, 1, 2, 0):
        queries = b.qt[dp]
        peak = None
        for s in range(8):
            scores = dot(b.ka[s], queries)
            b.scores[s] = scores
            top = jnp.max(scores, axis=0, keepdims=True)
            peak = top if peak is None else jnp.maximum(peak, top)
        total = jnp.zeros((1, rows), F32)
        result = jnp.zeros((64, rows), F32)
        cols = slice(dp * 256, (dp + 1) * 256)
        for s in range(8):
            terms = jnp.exp2((b.scores[s] - peak) * EIGHTH_LOG2)
            total = total + jnp.sum(terms, axis=0, keepdims=True)
            low = terms.astype(BF)
            b.pairs[s * 256 : (s + 1) * 256, 1024 + dp * 256 : 1280 + dp * 256] = low
            result = result + dot(b.vt[s], low)
        share = 1.0 / total
        b.share[:, cols] = share
        result = result * share
        b.heads[:, cols] = result
        b.h_out[dp] = result.astype(BF)
        for dz in (3, 2, 1, 0):
            if dp or dz:
                sent_h[dp, dz] = net.copy(b.h_out.at[dp], b.h_in.at[plane, chip], at(dp, dz))
        if dp == 3:
            for one in sent_wo:
                net.arrived(one)
            sent_wo2 = {
                (to, dz): net.copy(
                    b.wo.at[planes[dz], chip, core], b.wo.at[planes[dz], chip, core], at(to, 0)
                )
                for dz in (1, 2, 3)
                for to in (3, 1, 2)
            }
    b.h_in[plane, chip] = b.h_out[0]

    for s in range(8):
        b.vn[s] = turned(b.vt[s]).astype(BF)
    for s in range(4):
        some = turned(b.q_in[s, 0:64])
        b.wide[s * 256 : (s + 1) * 256] = jnp.concatenate(
            [some * 0.125, jnp.zeros((rows, 64), F32)], axis=1
        ).astype(BF)
    l_f2.wait()
    for n in range(4):
        cols = slice(n * 256, (n + 1) * 256)
        b.dact[:, cols] = dot_nt(b.mg[...], b.f2[cols])
    l_wo.wait()
    for one in sent_wo2.values():
        net.arrived(one)
    sent_wo3 = [
        net.copy(b.wo.at[planes[dz], :, core], b.wo.at[planes[dz], :, core], mate)
        for dz in (1, 2, 3)
    ]

    for dz in range(4):
        for dp in range(4):
            if dp or dz:
                net.arrived(sent_h[dp, dz])
        if dz:
            net.arrived(sent_wo3[dz - 1])
        left = turned(b.h_in[planes[dz]].reshape(256, rows)).astype(BF)
        right = b.wo[planes[dz]].reshape(256, width)
        if dz:
            b.attn[...] += dot(left, right)
        else:
            b.attn[...] = dot(left, right)
    sent_hx = net.copy(b.h_in.at[plane, pl.ds(2 * other, 2)], b.h_mate, mate)


    def second_norm(which):
        value = b.tok[which].astype(F32) + per_token(0, which) * b.attn[which]
        b.hid[which] = value
        normed, _ = norm_rows(value)
        value = (normed * (1.0 + per_token(3, which)) + per_token(5, which)).astype(BF)
        b.b[0, which] = value[:, :half]
        b.b[1, which] = value[:, half:]

    for i in range(0, rows, 64):
        second_norm(slice(i, i + 64))
    l_f1.wait()
    for n in range(4):
        cols = slice(n * 256, (n + 1) * 256)
        up = dot(b.b[0], b.f1[:half, cols]) + dot(b.b[1], b.f1[half:, cols])
        square = up * up
        bent = jnp.tanh(GELU_A * up * (1.0 + GELU_B * square))
        gate = 0.5 * (1.0 + bent)
        slope = gate + 0.5 * up * (1.0 - bent * bent) * (GELU_A * (1.0 + 3.0 * GELU_B * square))
        b.act[n // 2, :, (n % 2) * 256 : (n % 2 + 1) * 256] = (up * gate).astype(BF)
        b.ug[:, cols] = (b.dact[:, cols] * slope).astype(BF)
    for n in range(4):
        cols = slice(n * 256, (n + 1) * 256)
        value = dot_nt(b.ug[...], b.f1[cols])
        b.bg_out[:, :, cols] = value.astype(BF).reshape(4, own, 256)
    sent_bg, far_bg = plane_scatter(b.bg_out, b.bg_in, b.bg_far)

    sent_x = [
        net.copy(b.act.at[other], b.act_in, mate),
        net.copy(b.b.at[other], b.b_in, mate),
        net.copy(b.ug, b.ug_in, mate),
    ]
    b.left[0] = turned(b.act[core]).astype(BF)
    net.arrived(sent_mg)
    net.arrived(sent_x[0])
    b.left[1] = turned(b.act_in[...]).astype(BF)
    for n in range(4):
        some = slice(n * 128, (n + 1) * 128)
        value = dot(b.left[0, some], b.mg[...]) + dot(b.left[1, some], b.mg_in[...])
        b.g2_out[n] = value.astype(BF).reshape(2, 64, width)
    sent_g2 = scatter(b.g2_out, b.g2_in)
    sent_bg.append(plane_scatter_on(far_bg, b.bg_out, b.bg_in, b.bg_far))
    b.left[0] = turned(b.b[core]).astype(BF)
    net.arrived(sent_x[1])
    b.left[1] = turned(b.b_in[...]).astype(BF)
    net.arrived(sent_x[2])
    for n in range(4):
        some = slice(n * 128, (n + 1) * 128)
        value = dot(b.left[0, some], b.ug[...]) + dot(b.left[1, some], b.ug_in[...])
        b.g1_out[n] = value.astype(BF).reshape(2, 64, width)
    sent_g1 = scatter(b.g1_out, b.g1_in)
    for n in range(4):
        cols = slice(n * 256, (n + 1) * 256)
        value = dot(b.act[0], b.f2[:half, cols]) + dot(b.act[1], b.f2[half:, cols])
        b.mo_out[:, :, cols] = value.astype(BF).reshape(4, own, 256)

    def mode_sums(k, value):
        high = value.astype(BF)
        low = (value - high.astype(F32)).astype(BF)
        picked = turned(b.pick[mine])[0:ITEM_ROWS].astype(BF)
        value = (dot(picked, high) + dot(picked, low))[0:8]
        b.ms[0, k * 8 : (k + 1) * 8] = value[:, :half]
        b.ms[1, k * 8 : (k + 1) * 8] = value[:, half:]

    b_grad = summed(sent_bg, b.bg_out[plane], b.bg_in)
    normed, inverse = norm_rows(b.hid[mine])
    h_grad = b.cot[mine].astype(F32) + norm_back(
        b_grad * (1.0 + per_token(3, mine)), normed, inverse
    )
    b.hg[...] = h_grad
    attn_grad = (per_token(0, mine) * h_grad).astype(BF)
    b.ag[plane] = attn_grad
    for n in range(4):
        value = dot_nt(attn_grad, b.wo[n].reshape(256, width)).astype(BF)
        for h in range(4):
            some = value[:, h * 64 : (h + 1) * 64]
            b.do_out[n, h] = jnp.concatenate([some[: own // 2], some[own // 2 :]], axis=1)
    sent_do = {
        (dp, dz): net.copy(
            b.do_out.at[planes[dz], chips[dp]], b.do_in.at[dp, plane], at(dp, dz)
        )
        for dp, dz in reversed(offsets)
    }
    b.do_in[0, plane] = b.do_out[plane, chip]
    sent_mo, far_mo = plane_scatter(b.mo_out, b.mo_in, b.mo_far)
    sent_ag = plane_gather(b.ag.at[plane], b.ag)
    mode_sums(0, h_grad * b.attn[mine])
    mode_sums(3, b_grad * normed)
    mode_sums(5, b_grad)
    sent_g2 = scatter_on(sent_g2, b.g2_out, b.g2_in)
    sent_g1 = scatter_on(sent_g1, b.g1_out, b.g1_in)

    for one in sent_do.values():
        net.arrived(one)
    for s in range(4):
        cols = slice(s * 256, (s + 1) * 256)
        for n in range(4):
            both = b.do_in[s, n]
            b.dn[n * own : n * own + own // 2] = both[:, 0:64]
            b.dn[n * own + own // 2 : (n + 1) * own] = both[:, 64:128]
        value = turned(b.dn[...])
        b.dt[:, cols] = value.astype(BF)
        b.delta[:, cols] = jnp.sum(value * b.heads[:, cols], axis=0, keepdims=True)
        b.wide[1024 + s * 256 : 1280 + s * 256] = jnp.concatenate(
            [jnp.zeros((rows, 64), F32), (value * b.share[:, cols]).T], axis=1
        ).astype(BF)

    def attend_back(s):
        keys = slice(s * 256, (s + 1) * 256)
        for q in range(4):
            cols = slice(q * 256, (q + 1) * 256)
            pull = (dot(b.vn[s], b.dt[:, cols]) - b.delta[:, cols]) * b.share[:, cols]
            terms = b.pairs[keys, 1024 + q * 256 : 1280 + q * 256]
            b.pairs[keys, cols] = (pull * terms.astype(F32)).astype(BF)
        b.dkv[s] = dot(b.pairs[keys], b.wide[...]).T

    for s in range(4, 8):
        attend_back(s)
    sent_dkv = net.copy(b.dkv.at[4:8], b.dkv_in, mate)
    for s in range(4):
        attend_back(s)
    value = (dot(b.ktw[...], b.pairs[:, 0:1024]) * 0.125).astype(BF)
    for s in range(4):
        b.dx_out[s, 0:64] = value[:, s * 256 : (s + 1) * 256]
    b.dx_in[chip, 0:64] = b.dx_out[0, 0:64]
    sent_dx = [
        net.copy(b.dx_out.at[dp, 0:64], b.dx_in.at[chip, 0:64], at(dp, 0)) for dp in (3, 1, 2)
    ]
    net.arrived(sent_dkv)
    for s in range(4):
        b.dx_out[s, 64:192] = (b.dkv[s] + b.dkv_in[s]).astype(BF)
    b.dx_in[chip, 64:192] = b.dx_out[0, 64:192]
    sent_dx += [
        net.copy(b.dx_out.at[dp, 64:192], b.dx_in.at[chip, 64:192], at(dp, 0)) for dp in (3, 1, 2)
    ]
    sent_mo.append(plane_scatter_on(far_mo, b.mo_out, b.mo_in, b.mo_far))
    sent_g2b = gather(sent_g2, b.g2_out, b.g2_in, b.g2, gf2_o)
    sent_g1b = gather(sent_g1, b.g1_out, b.g1_in, b.g1, gf1_o)
    sent_ag.append(plane_gather_on(sent_ag, b.ag))

    for one in sent_dx:
        net.arrived(one)
    sent_dxm = net.copy(b.dx_in, b.dx_mate, mate)
    for k in range(3):
        value = b.dx_in[:, k * 64 : (k + 1) * 64].reshape(256, rows)
        b.dx[k] = turned(value).astype(BF)
    for n in range(4):
        cols = slice(n * 256, (n + 1) * 256)
        value = dot_nt(b.dx[0], b.wq[0, cols])
        value = value + dot_nt(b.dx[1], b.wq[1, cols])
        value = value + dot_nt(b.dx[2], b.wq[2, cols])
        b.xg_out[:, :, cols] = value.astype(BF).reshape(4, own, 256)
    sent_xg, far_xg = plane_scatter(b.xg_out, b.xg_in, b.xg_far)

    net.arrived(sent_a)
    net.arrived(sent_dxm)
    for h in range(4):
        value = dot(b.dx_in[h], b.a[core]) + dot(b.dx_mate[h], b.a_in[...])
        b.gq_out[h] = value.astype(BF).reshape(2, 96, half)
    sent_gq = scatter(b.gq_out, b.gq_in)
    sent_xg.append(plane_scatter_on(far_xg, b.xg_out, b.xg_in, b.xg_far))

    sent_g2b += gather_on(sent_g2b, gf2_o)
    sent_g1b += gather_on(sent_g1b, gf1_o)

    mlp_out = summed(sent_mo, b.mo_out[plane], b.mo_in)
    b.out[...] = (b.hid[mine] + per_token(1, mine) * mlp_out).astype(BF)
    sent_out = plane_gather(b.out, out_o)
    load(b.out, out_o.at[plane])
    mode_sums(1, b.cot[mine].astype(F32) * mlp_out)

    for one in sent_ag[1:]:
        net.arrived(one)
    sent_agm = net.copy(b.ag, b.ag_in, mate)
    value = dot(
        b.h_in[plane, pl.ds(2 * core, 2)].reshape(128, rows), b.ag[...].reshape(rows, width)
    )
    net.arrived(sent_hx)
    net.arrived(sent_agm)
    value = value + dot(b.h_mate[...].reshape(128, rows), b.ag_in[...].reshape(rows, width))
    b.go_out[...] = value.astype(BF).reshape(4, 32, width)
    sent_go = [
        net.copy(b.go_out.at[chips[dp]], b.go_in.at[dp - 1], at(dp, 0)) for dp in (3, 1, 2)
    ]

    sent_gq = scatter_on(sent_gq, b.gq_out, b.gq_in)
    plane_gather_on(sent_out, out_o)

    a_grad = summed(sent_xg, b.xg_out[plane], b.xg_in)
    normed, inverse = norm_rows(b.tok[mine].astype(F32))
    mode_sums(2, a_grad * normed)
    mode_sums(4, a_grad)
    sent_ms = net.copy(b.ms.at[other], b.ms_in, mate)
    value = b.hg[...] + norm_back(a_grad * (1.0 + per_token(2, mine)), normed, inverse)
    b.dtok[...] = value.astype(BF)
    net.arrived(sent_ms)
    b.m1[...] = (b.ms[core] + b.ms_in[...]).astype(BF)
    sent_m1 = [net.copy(b.m1, b.m1_in.at[dz - 1], at(0, dz)) for dz in (3, 2, 1)]
    sent_dt = plane_gather(b.dtok, dtok_o)
    load(b.dtok, dtok_o.at[plane])

    sent_gqb = gather(sent_gq, b.gq_out, b.gq_in, b.gq, gqkv_o)
    b.go[...] = summed(sent_go, b.go_out[chip], b.go_in).astype(BF)
    sent_gob = [net.copy(b.go, gout_o.at[core, chip], at(dp, 0)) for dp in (3, 1, 2)]
    load(b.go, gout_o.at[core, chip])
    net.copy(b.go, gout_o.at[core, chip], mate)
    b.m2[...] = summed(sent_m1, b.m1[...], b.m1_in).astype(BF)
    sent_m2 = [net.copy(b.m2, b.m2_in.at[dp - 1], at(dp, 0)) for dp in (3, 1, 2)]
    plane_gather_on(sent_dt, dtok_o)

    def pass_on(sent, array):
        for one in sent:
            net.arrived(one)
        for dp in (1, 2, 3):
            where = (core, chips[dp])
            net.copy(array.at[where], array.at[where], mate)

    pass_on(sent_g2b[2:], gf2_o)
    pass_on(sent_g1b[2:], gf1_o)
    sent_gqb += gather_on(sent_gqb, gqkv_o)
    b.m3[...] = summed(sent_m2, b.m2[...], b.m2_in)
    net.copy(b.m3, mode_o.at[core], mate)
    load(b.m3, mode_o.at[core])
    some = pl.ds(pl.multiple_of(plane * part, part), part)
    side = pl.ds(pl.multiple_of(core * half, half), half)
    value = jnp.zeros((16, part), F32)
    for k in range(COMPONENTS):
        sums = b.m3[k * 8 : (k + 1) * 8]
        high = sums.astype(BF).astype(F32)
        both = jnp.concatenate([high, sums - high], axis=0).astype(BF)
        value = value + dot_nt(both, b.ada[k, some, side])
    b.cg[...] = value[0:8] + value[8:16]
    net.copy(b.cg, cg_o.at[core], mate)
    load(b.cg, cg_o.at[core])
    load(b.cond, cond_o)
    pass_on(sent_gob, gout_o)
    pass_on(sent_gqb[2:], gqkv_o)
    assert len(net.made) == COPIES and len(loads) == LOADS
    net.finish()
    for one in loads[first_store:]:
        one.wait()


def buffers(dims):
    rows, width, part, hidden, items, classes = dims
    own, half = rows // 4, width // 2
    return dict(
        tok=((rows, width), BF),
        cot=((rows, width), BF),
        table=((classes, width), BF),
        ada=((COMPONENTS, width, width), BF),
        wq=((3, width, part), BF),
        wo=((4, 4, 2, 32, width), BF),
        f1=((width, hidden), BF),
        f2=((hidden, width), BF),
        modes=((COMPONENTS, 3 * ITEM_ROWS, width), BF),
        pick=((rows, 3 * ITEM_ROWS), BF),
        cond=((ITEM_ROWS, width), F32),
        a=((2, rows, half), BF),
        a_in=((rows, half), BF),
        q_out=((4, 192, rows), BF),
        q_in=((4, 192, rows), BF),
        k_in=((4, 128, rows), BF),
        kt=((8, 128, rows), BF),
        ka=((8, rows, 128), BF),
        vt=((8, 64, rows), BF),
        vn=((8, rows, 64), BF),
        qt=((4, 128, rows), BF),
        ktw=((64, 2048), BF),
        wide=((2048, 128), BF),
        scores=((8, rows, rows), F32),
        pairs=((2048, 2048), BF),
        share=((1, 1024), F32),
        heads=((64, 1024), F32),
        h_out=((4, 64, rows), BF),
        h_in=((4, 4, 64, rows), BF),
        h_mate=((2, 64, rows), BF),
        attn=((rows, width), F32),
        hid=((rows, width), F32),
        b=((2, rows, half), BF),
        b_in=((rows, half), BF),
        act=((2, rows, half), BF),
        act_in=((rows, half), BF),
        mg=((rows, width), BF),
        mg_in=((rows, width), BF),
        ug=((rows, hidden), BF),
        ug_in=((rows, hidden), BF),
        dact=((rows, hidden), F32),
        left=((2, half, rows), BF),
        bg_out=((4, own, width), BF),
        bg_in=((3, own, width), BF),
        mo_out=((4, own, width), BF),
        mo_in=((3, own, width), BF),
        mo_far=((own, width), BF),
        bg_far=((own, width), BF),
        xg_far=((own, width), BF),
        xg_out=((4, own, width), BF),
        xg_in=((3, own, width), BF),
        g1_out=((4, 2, 64, width), BF),
        g1_in=((2, 3, 64, width), BF),
        g1=((2, 64, width), BF),
        g2_out=((4, 2, 64, width), BF),
        g2_in=((2, 3, 64, width), BF),
        g2=((2, 64, width), BF),
        hg=((own, width), F32),
        ag=((4, own, width), BF),
        ag_in=((4, own, width), BF),
        do_out=((4, 4, own // 2, 128), BF),
        do_in=((4, 4, own // 2, 128), BF),
        dn=((rows, 64), BF),
        dt=((64, 1024), BF),
        delta=((1, 1024), F32),
        dkv=((8, 128, rows), F32),
        dkv_in=((4, 128, rows), F32),
        dx_out=((4, 192, rows), BF),
        dx_mate=((4, 192, rows), BF),
        dx_in=((4, 192, rows), BF),
        dx=((3, rows, part), BF),
        gq_out=((4, 2, 96, half), BF),
        gq_in=((2, 3, 96, half), BF),
        gq=((2, 96, half), BF),
        out=((own, width), BF),
        dtok=((own, width), BF),
        go_out=((4, 32, width), BF),
        go_in=((3, 32, width), BF),
        go=((32, width), BF),
        ms=((2, 48, half), F32),
        ms_in=((48, half), F32),
        m1=((48, half), BF),
        m1_in=((3, 48, half), BF),
        m2=((48, half), BF),
        m2_in=((3, 48, half), BF),
        m3=((48, half), F32),
        cg=((8, part), F32),
    )


def finish_kernel(
    cls_s, out_i, dtok_i, gqkv_i, gout_i, gf1_i, gf2_i, mode_i, cond_i, cg_i,
    out_o, dtok_o, table_o, ada_o, qkv_o, wout_o, f1_o, f2_o,
):
    step, last = pl.program_id(0), pl.num_programs(0) - 1
    plane = lax.axis_index("head")
    part = table_o.shape[1]
    mine = pl.ds(pl.multiple_of(plane * part, part), part)
    out_o[...] = out_i[0]
    dtok_o[...] = dtok_i[0]
    wout_o[...] = gout_i[0].astype(F32).reshape(wout_o.shape)
    f1_o[...] = gf1_i[0].astype(F32).reshape(f1_o.shape)
    f2_o[...] = gf2_i[0].astype(F32).reshape(f2_o.shape)
    sums = gqkv_i[0].astype(F32).reshape(4, 192, 256)
    for k in range(3):
        qkv_o[k] = sums[:, k * 64 : (k + 1) * 64].reshape(part, 256).T
    cond = cond_i[:, pl.ds(pl.multiple_of(step * 256, 256), 256)]
    cond_low = (cond / (1.0 + jnp.exp(-cond)))[0:8]
    low = jnp.concatenate([cond_low, cond_low], axis=0).astype(BF)
    side = pl.ds(pl.multiple_of(lax.rem(plane, 2) * part, part), part)
    for k in range(COMPONENTS):
        value = mode_i[lax.div(plane, 2), k * 8 : (k + 1) * 8, side]
        high = value.astype(BF).astype(F32)
        both = jnp.concatenate([high, value - high], axis=0).astype(BF)
        ada_o[k] = dot_tn(low, both)

    @pl.when(step == last)
    def _():
        own = cond_i[0:8, mine]
        gate = 1.0 / (1.0 + jnp.exp(-own))
        grad = (cg_i[0] + cg_i[1]) * gate * (1.0 + own * (1.0 - gate))
        spot = lax.broadcasted_iota(jnp.int32, table_o.shape, 0)
        total = jnp.zeros(table_o.shape, F32)
        for i in range(cls_s.shape[0]):
            total = total + jnp.where(spot == cls_s[i], grad[i : i + 1], 0.0)
        table_o[...] = total


def finish(
    class_ids,
    output,
    d_tokens,
    qkv_sum,
    out_sum,
    fc1_sum,
    fc2_sum,
    mode_grad,
    cond,
    cond_grad,
    classes,
):
    steps = 4
    own, width = output.shape[1:]
    half, part, hidden = width // 2, width // 4, 1024
    rows = own * 4
    smem = pl.BlockSpec(memory_space=pltpu.SMEM)
    few = pl.BlockSpec((1, own, width), lambda i: (i, 0, 0))
    table, ada, qkv, out, fc1, fc2 = (
        (classes, part),
        (COMPONENTS, width, part),
        (3, width, part),
        (part, width),
        (width, hidden),
        (hidden, width),
    )
    output, d_tokens, table, ada, qkv, out, fc1, fc2 = pl.pallas_call(
        finish_kernel,
        grid=(steps,),
        out_shape=[
            jax.ShapeDtypeStruct((rows, width), BF),
            jax.ShapeDtypeStruct((rows, width), BF),
        ]
        + [jax.ShapeDtypeStruct(shape, F32) for shape in (table, ada, qkv, out, fc1, fc2)],
        in_specs=[
            smem,
            few,
            few,
            pl.BlockSpec((1, 4, 2, 96, half // 2), lambda i: (i // 2, 0, 0, 0, i % 2)),
            pl.BlockSpec((1, 2, 32, width), lambda i: (i // 2, i % 2, 0, 0)),
            pl.BlockSpec((1, 2, 2, 64, hidden), lambda i: (i // 2, i % 2, 0, 0, 0)),
            pl.BlockSpec((1, 2, 2, 64, width), lambda i: (i // 2, i % 2, 0, 0, 0)),
            pl.BlockSpec((2, 48, half), lambda i: (0, 0, 0)),
            pl.BlockSpec((ITEM_ROWS, width), lambda i: (0, 0)),
            pl.BlockSpec((2, 8, part), lambda i: (0, 0, 0)),
        ],
        out_specs=[
            pl.BlockSpec((rows // steps, width), lambda i: (i, 0)),
            pl.BlockSpec((rows // steps, width), lambda i: (i, 0)),
            pl.BlockSpec((classes, part), lambda i: (0, 0)),
            pl.BlockSpec((COMPONENTS, 256, part), lambda i: (0, i, 0)),
            pl.BlockSpec((3, 256, part), lambda i: (0, i, 0)),
            pl.BlockSpec((64, width), lambda i: (i, 0)),
            pl.BlockSpec((256, hidden), lambda i: (i, 0)),
            pl.BlockSpec((256, width), lambda i: (i, 0)),
        ],
        compiler_params=pltpu.CompilerParams(vmem_limit_bytes=VMEM_BYTES),
    )(
        class_ids, output, d_tokens, qkv_sum, out_sum, fc1_sum, fc2_sum, mode_grad, cond, cond_grad
    )
    return output, d_tokens, table, ada, qkv.transpose(1, 0, 2), out, fc1, fc2


def on_block(
    tokens,
    class_ids,
    slot_item,
    slot_scale,
    class_table,
    w_ada,
    w_qkv,
    w_out,
    w_fc1,
    w_fc2,
    cotangent,
):
    rows, width = tokens.shape
    part, hidden = w_qkv.shape[2], w_fc1.shape[1]
    items, classes = class_ids.shape[0], class_table.shape[0]
    own, half = rows // 4, width // 2
    dims = (rows, width, part, hidden, items, classes)
    scratch = [pltpu.VMEM(shape, dtype) for shape, dtype in buffers(dims).values()]
    anywhere = pl.BlockSpec(memory_space=pl.ANY)
    vmem = pl.BlockSpec(memory_space=pltpu.VMEM)
    smem = pl.BlockSpec(memory_space=pltpu.SMEM)
    output, d_tokens, qkv_sum, out_sum, fc1_sum, fc2_sum, mode_grad, cond, cond_grad = pl.pallas_call(
        functools.partial(block_kernel, dims),
        out_shape=[
            jax.ShapeDtypeStruct((4, own, width), BF),
            jax.ShapeDtypeStruct((4, own, width), BF),
            jax.ShapeDtypeStruct((2, 4, 2, 96, half), BF),
            jax.ShapeDtypeStruct((2, 4, 32, width), BF),
            jax.ShapeDtypeStruct((2, 4, 2, 64, width), BF),
            jax.ShapeDtypeStruct((2, 4, 2, 64, width), BF),
            jax.ShapeDtypeStruct((2, 48, half), F32),
            jax.ShapeDtypeStruct((ITEM_ROWS, width), F32),
            jax.ShapeDtypeStruct((2, 8, part), F32),
        ],
        in_specs=[anywhere, smem, vmem, vmem] + [anywhere] * 7,
        out_specs=[anywhere] * 9,
        scratch_shapes=[
            pltpu.SemaphoreType.DMA((COPIES,)),
            pltpu.SemaphoreType.DMA((COPIES,)),
            pltpu.SemaphoreType.DMA((LOADS,)),
            *scratch,
        ],
        compiler_params=pltpu.CompilerParams(
            collective_id=0, has_side_effects=True, vmem_limit_bytes=VMEM_BYTES
        ),
        cost_estimate=pl.CostEstimate(
            flops=10_000_000_000, bytes_accessed=40_000_000, transcendentals=3_000_000
        ),
    )(
        tokens,
        class_ids,
        slot_item.reshape(8, 1, rows),
        slot_scale.reshape(8, 1, rows),
        class_table,
        w_ada,
        w_qkv.transpose(1, 0, 2),
        w_out.reshape(4, 2, 32, width),
        w_fc1,
        w_fc2,
        cotangent,
    )
    return finish(
        class_ids, output, d_tokens, qkv_sum, out_sum, fc1_sum, fc2_sum, mode_grad, cond, cond_grad,
        classes,
    )


def fits(mesh):
    return mesh.shape["tok"] == 8 and mesh.shape["head"] == 4


def layer_norm(values):
    centre = jnp.mean(values, axis=-1, keepdims=True)
    shifted = values - centre
    spread = jnp.mean(shifted * shifted, axis=-1, keepdims=True)
    return shifted * lax.rsqrt(spread + EPS)


def modulate(values, scale_in, shift_in):
    return layer_norm(values) * (1.0 + scale_in) + shift_in


def pair_scores(queries, key_block, query_item, key_item, query_scale, key_scale):
    scores = (
        jnp.einsum("qhd,khd->hqk", queries, key_block, preferred_element_type=jnp.float32) * 0.125
    )
    allowed = (
        (query_item[:, None] == key_item[None, :]) & (key_scale[None, :] <= query_scale[:, None])
    )[None]
    return (jnp.where(allowed, scores, -1e30), allowed)


def on_device(
    tokens,
    class_ids,
    slot_item,
    slot_scale,
    class_table,
    w_ada,
    w_qkv,
    w_out,
    w_fc1,
    w_fc2,
    cotangent,
):
    tok_rows, full_width = tokens.shape
    slot_count = slot_item.shape[0]
    item_count = class_ids.shape[0]
    class_count = class_table.shape[0]
    local_width = w_qkv.shape[2]
    local_heads = local_width // HEAD_DIM
    anchor = lax.axis_index("tok") * tok_rows
    first_col = lax.axis_index("head") * local_width
    my_item = lax.dynamic_slice_in_dim(slot_item, anchor, tok_rows)
    my_scale = lax.dynamic_slice_in_dim(slot_scale, anchor, tok_rows)
    class_pick = (class_ids[:, None] == jnp.arange(class_count, dtype=jnp.int32)[None, :]).astype(
        jnp.bfloat16
    )
    cond = jnp.dot(class_pick, class_table, preferred_element_type=jnp.float32)
    silu_cond, silu_back = jax.vjp(jax.nn.silu, cond)
    cond_low = silu_cond.astype(jnp.bfloat16)
    modes = jnp.einsum("id,cde->ice", cond_low, w_ada, preferred_element_type=jnp.float32)
    item_pick = (my_item[:, None] == jnp.arange(item_count, dtype=jnp.int32)[None, :]).astype(
        jnp.float32
    )
    per_token = jnp.dot(
        item_pick, modes.reshape(item_count, 6 * full_width), precision=HIGH
    ).reshape(tok_rows, 6, full_width)
    gamma_one = per_token[:, 0]
    gamma_two = per_token[:, 1]
    scale_one = per_token[:, 2]
    scale_two = per_token[:, 3]
    shift_one = per_token[:, 4]
    shift_two = per_token[:, 5]
    tok_float = tokens.astype(jnp.float32)
    a_pre, a_back = jax.vjp(modulate, tok_float, scale_one, shift_one)
    a_low = a_pre.astype(jnp.bfloat16)
    qkv_low = jnp.einsum("td,dce->tce", a_low, w_qkv, preferred_element_type=jnp.float32).astype(
        jnp.bfloat16
    )
    queries = qkv_low[:, 0]
    key_own = qkv_low[:, 1]
    value_own = qkv_low[:, 2]
    query_heads = queries.reshape(tok_rows, local_heads, HEAD_DIM)
    key_all, value_all = (
        lax.all_gather(key_own, "tok", axis=0, tiled=True),
        lax.all_gather(value_own, "tok", axis=0, tiled=True),
    )
    block_rows = math.gcd(slot_count, 2048)
    blocks = slot_count // block_rows
    key_blocks = key_all.reshape(blocks, block_rows, local_heads, HEAD_DIM)
    value_blocks = value_all.reshape(blocks, block_rows, local_heads, HEAD_DIM)
    item_blocks = slot_item.reshape(blocks, block_rows)
    scale_blocks = slot_scale.reshape(blocks, block_rows)
    key_wanted = jnp.min(scale_blocks, axis=1) <= jnp.max(my_scale)

    def first_pass(running, inputs):
        key_block, item_block, scale_block, wanted = inputs

        def first_compute_block(state_now):
            scores, allowed = pair_scores(
                query_heads, key_block, my_item, item_block, my_scale, scale_block
            )
            new_peak = jnp.maximum(state_now[0], jnp.max(scores, axis=2))
            terms = jnp.where(allowed, jnp.exp(scores - new_peak[:, :, None]), 0.0)
            return (
                new_peak,
                state_now[1] * jnp.exp(state_now[0] - new_peak) + jnp.sum(terms, axis=2),
            )

        return (lax.cond(wanted, first_compute_block, lambda state_now: state_now, running), None)

    initial = (
        jnp.full((local_heads, tok_rows), -1e30, jnp.float32),
        jnp.zeros((local_heads, tok_rows), jnp.float32),
    )
    (row_peak, summed), _ = lax.scan(
        first_pass, initial, (key_blocks, item_blocks, scale_blocks, key_wanted)
    )
    log_total = row_peak + jnp.log(summed)

    def second_pass(running, inputs):
        key_block, value_block, item_block, scale_block, wanted = inputs

        def second_compute_block(total_now):
            scores, allowed = pair_scores(
                query_heads, key_block, my_item, item_block, my_scale, scale_block
            )
            rounded = jnp.where(allowed, jnp.exp(scores - log_total[:, :, None]), 0.0).astype(
                jnp.bfloat16
            )
            return total_now + jnp.einsum(
                "hqk,khd->qhd", rounded, value_block, preferred_element_type=jnp.float32
            )

        return (lax.cond(wanted, second_compute_block, lambda total_now: total_now, running), None)

    heads_out, _ = lax.scan(
        second_pass,
        jnp.zeros((tok_rows, local_heads, HEAD_DIM), jnp.float32),
        (key_blocks, value_blocks, item_blocks, scale_blocks, key_wanted),
    )
    heads_low = heads_out.reshape(tok_rows, local_width).astype(jnp.bfloat16)
    attn_out = lax.psum(
        jnp.dot(heads_low, w_out, preferred_element_type=jnp.float32).astype(jnp.bfloat16), "head"
    ).astype(jnp.float32)
    hidden = tok_float + gamma_one * attn_out
    b_pre, b_back = jax.vjp(modulate, hidden, scale_two, shift_two)
    b_low = b_pre.astype(jnp.bfloat16)
    up_proj = jnp.dot(b_low, w_fc1, preferred_element_type=jnp.float32)
    act_pre, act_back = jax.vjp(lambda values: jax.nn.gelu(values, approximate=True), up_proj)
    act_low = act_pre.astype(jnp.bfloat16)
    mlp_out = lax.psum(
        jnp.dot(act_low, w_fc2, preferred_element_type=jnp.float32).astype(jnp.bfloat16), "head"
    ).astype(jnp.float32)
    output = (hidden + gamma_two * mlp_out).astype(jnp.bfloat16)
    out_grad = cotangent.astype(jnp.float32)
    mlp_grad = (gamma_two * out_grad).astype(jnp.bfloat16)
    fc2_weight_grad = jnp.einsum("tf,td->fd", act_low, mlp_grad, preferred_element_type=jnp.float32)
    act_grad = jnp.einsum("td,fd->tf", mlp_grad, w_fc2, preferred_element_type=jnp.float32)
    up_grad = act_back(act_grad)[0].astype(jnp.bfloat16)
    fc1_weight_grad = jnp.einsum("td,tf->df", b_low, up_grad, preferred_element_type=jnp.float32)
    b_grad = lax.psum(
        jnp.einsum("tf,df->td", up_grad, w_fc1, preferred_element_type=jnp.float32).astype(
            jnp.bfloat16
        ),
        "head",
    ).astype(jnp.float32)
    hidden_part, scale_two_grad, shift_two_grad = b_back(b_grad)
    hidden_grad = out_grad + hidden_part
    attn_grad = (gamma_one * hidden_grad).astype(jnp.bfloat16)
    out_weight_grad = jnp.einsum(
        "tf,te->fe", heads_low, attn_grad, preferred_element_type=jnp.float32
    )
    grad_low = jnp.einsum("te,fe->tf", attn_grad, w_out, preferred_element_type=jnp.float32).astype(
        jnp.bfloat16
    )
    grad_heads = grad_low.reshape(tok_rows, local_heads, HEAD_DIM)
    delta = jnp.einsum("qhd,qhd->hq", grad_heads.astype(jnp.float32), heads_out)

    def step_block(running, inputs):
        key_block, value_block, item_block, scale_block, wanted = inputs

        def step_compute_block(total_now):
            scores, allowed = pair_scores(
                query_heads, key_block, my_item, item_block, my_scale, scale_block
            )
            weights = jnp.where(allowed, jnp.exp(scores - log_total[:, :, None]), 0.0)
            weight_grad = jnp.einsum(
                "qhd,khd->hqk", grad_heads, value_block, preferred_element_type=jnp.float32
            )
            score_grad = (weights * (weight_grad - delta[:, :, None])).astype(jnp.bfloat16)
            total_now = (
                total_now
                + jnp.einsum(
                    "hqk,khd->qhd", score_grad, key_block, preferred_element_type=jnp.float32
                )
                * 0.125
            )
            key_term = (
                jnp.einsum(
                    "hqk,qhd->khd", score_grad, query_heads, preferred_element_type=jnp.float32
                )
                * 0.125
            )
            value_term = jnp.einsum(
                "hqk,qhd->khd",
                weights.astype(jnp.bfloat16),
                grad_heads,
                preferred_element_type=jnp.float32,
            )
            return (total_now, (key_term, value_term))

        def skip_block(total_now):
            nothing = jnp.zeros((block_rows, local_heads, HEAD_DIM), jnp.float32)
            return (total_now, (nothing, nothing))

        return lax.cond(wanted, step_compute_block, skip_block, running)

    query_grad, (key_terms, value_terms) = lax.scan(
        step_block,
        jnp.zeros((tok_rows, local_heads, HEAD_DIM), jnp.float32),
        (key_blocks, value_blocks, item_blocks, scale_blocks, key_wanted),
    )
    key_grad, value_grad = (
        lax.psum_scatter(
            key_terms.reshape(slot_count, local_width), "tok", scatter_dimension=0, tiled=True
        ),
        lax.psum_scatter(
            value_terms.reshape(slot_count, local_width), "tok", scatter_dimension=0, tiled=True
        ),
    )
    qkv_grad = jnp.stack(
        [query_grad.reshape(tok_rows, local_width), key_grad, value_grad], axis=1
    ).astype(jnp.bfloat16)
    qkv_weight_grad = jnp.einsum("td,tce->dce", a_low, qkv_grad, preferred_element_type=jnp.float32)
    a_grad = lax.psum(
        jnp.einsum("tce,dce->td", qkv_grad, w_qkv, preferred_element_type=jnp.float32).astype(
            jnp.bfloat16
        ),
        "head",
    ).astype(jnp.float32)
    tok_part, scale_one_grad, shift_one_grad = a_back(a_grad)
    d_tokens = (hidden_grad + tok_part).astype(jnp.bfloat16)
    token_modes = jnp.stack(
        [
            hidden_grad * attn_out,
            out_grad * mlp_out,
            scale_one_grad,
            scale_two_grad,
            shift_one_grad,
            shift_two_grad,
        ],
        axis=1,
    )
    mode_part = jnp.einsum(
        "ti,tf->if", item_pick, token_modes.reshape(tok_rows, 6 * full_width), precision=HIGH
    ).reshape(item_count, 6, full_width)
    qkv_sum, out_sum, fc1_sum, fc2_sum, mode_grad = lax.psum(
        (qkv_weight_grad, out_weight_grad, fc1_weight_grad, fc2_weight_grad, mode_part), "tok"
    )
    cond_grad = jnp.zeros((item_count, full_width), jnp.float32)
    for component in range(6):
        cond_grad = cond_grad + jnp.dot(
            mode_grad[:, component], w_ada[component].astype(jnp.float32).T, precision=HIGH
        )
    pre_grad = silu_back(cond_grad)[0]
    own_pre = lax.dynamic_slice_in_dim(pre_grad, first_col, local_width, 1)
    table_grad = jnp.einsum("ic,id->cd", class_pick.astype(jnp.float32), own_pre, precision=HIGH)
    own_modes = lax.dynamic_slice_in_dim(mode_grad, first_col, local_width, 2)
    ada_grad = jnp.einsum("id,ice->cde", cond_low.astype(jnp.float32), own_modes, precision=HIGH)
    return (output, d_tokens, table_grad, ada_grad, qkv_sum, out_sum, fc1_sum, fc2_sum)


def solution(mesh):
    placed = (
        P("tok", None),
        P(),
        P(),
        P(),
        P(),
        P(),
        P(None, None, "head"),
        P("head", None),
        P(None, "head"),
        P("head", None),
        P("tok", None),
    )
    return jax.shard_map(
        on_block if fits(mesh) else on_device,
        mesh=mesh,
        in_specs=placed,
        out_specs=(
            P("tok", None),
            P("tok", None),
            P(None, "head"),
            P(None, None, "head"),
            P(None, None, "head"),
            P("head", None),
            P(None, "head"),
            P("head", None),
        ),
        check_vma=False,
    )
```

```python
import functools
import math
import types

import jax
import jax.numpy as jnp
from jax import lax
from jax.experimental import pallas as pl
from jax.experimental.pallas import tpu as pltpu
from jax.sharding import PartitionSpec as P

HEAD_DIM = 64
COMPONENTS = 6


EPS = 1e-06
HIGH = lax.Precision.HIGHEST
BF = jnp.bfloat16
F32 = jnp.float32
MESH = pl.DeviceIdType.MESH
BARRED = -1e30
EIGHTH_LOG2 = 0.125 * math.log2(math.e)
GELU_A = math.sqrt(2.0 / math.pi)
GELU_B = 0.044715
COPIES = 164
SENDS = 48
LOADS = 22
VMEM_BYTES = 62 * 1024 * 1024
ITEM_ROWS = 16


def dot(left, right):
    return lax.dot_general(left, right, (((1,), (0,)), ((), ())), preferred_element_type=F32)


def dot_nt(left, right):
    return lax.dot_general(left, right, (((1,), (1,)), ((), ())), preferred_element_type=F32)


def dot_tn(left, right):
    return lax.dot_general(left, right, (((0,), (0,)), ((), ())), preferred_element_type=F32)


def turned(block):
    return block.astype(F32).T


def norm_rows(values):
    shifted = values - jnp.mean(values, axis=-1, keepdims=True)
    inverse = lax.rsqrt(jnp.mean(shifted * shifted, axis=-1, keepdims=True) + EPS)
    return shifted * inverse, inverse


def norm_back(grad, normed, inverse):
    along = jnp.mean(grad * normed, axis=-1, keepdims=True)
    return (grad - jnp.mean(grad, axis=-1, keepdims=True) - normed * along) * inverse


class Net:
    def __init__(self, send, arrive):
        self.send, self.arrive = send, arrive
        self.made, self.waited = [], []

    def copy(self, source, target, device, when=None, gets=None):
        k = len(self.made)
        if k >= SENDS:
            before, its_when, _ = self.made[k - SENDS]
            on_some(its_when, before.wait_send)
        one = pltpu.make_async_remote_copy(
            src_ref=source,
            dst_ref=target,
            send_sem=self.send.at[k % SENDS],
            recv_sem=self.arrive.at[k],
            device_id=device,
            device_id_type=MESH,
        )
        self.made.append((one, when, gets))
        on_some(when, one.start)
        return k

    def arrived(self, k):
        one, _, gets = self.made[k]
        on_some(gets, one.wait_recv)
        self.waited.append(k)

    def finish(self):
        for k, (one, when, _) in enumerate(self.made):
            if k >= len(self.made) - SENDS:
                on_some(when, one.wait_send)
            if k not in self.waited:
                self.arrived(k)


def on_some(when, act):
    if when is None:
        act()
    else:
        pl.when(when)(act)


def block_kernel(dims, *refs):
    rows, width, part, hidden, items, classes = dims
    names = list(buffers(dims))
    (
        tok_h, cls_s, item_v, scale_v, table_h, ada_h, wq_h, wo_h, f1_h, f2_h, cot_h,
        out_o, dtok_o, gqkv_o, gout_o, gf1_o, gf2_o, mode_o, cond_o, cg_o,
        send_sem, arrive_sem, load_sem, *scratch,
    ) = refs
    b = types.SimpleNamespace(**dict(zip(names, scratch, strict=True)))
    own = rows // 4
    half = width // 2
    net = Net(send_sem, arrive_sem)
    loads = []

    def load(source, target):
        one = pltpu.make_async_copy(source, target, load_sem.at[len(loads)])
        one.start()
        loads.append(one)
        return one

    group = lax.axis_index("tok")
    plane = lax.axis_index("head")
    core = lax.rem(group, 2)
    chip = lax.div(group, 2)
    col, line = lax.rem(chip, 2), lax.div(chip, 2)
    chips = [chip, line * 2 + 1 - col, (1 - line) * 2 + col, 3 - chip]
    planes = [
        plane,
        lax.div(plane, 2) * 2 + 1 - lax.rem(plane, 2),
        lax.rem(plane + 2, 4),
        3 - plane,
    ]
    other = 1 - core
    inner = (plane == 1) | (plane == 2)
    outer = (plane == 0) | (plane == 3)
    offsets = [(dp, dz) for dz in range(4) for dp in range(4) if dp or dz]

    def at(dp, dz):
        return (chips[dp] * 2 + core, planes[dz])

    mate = (chip * 2 + other, plane)
    mine = pl.ds(pl.multiple_of(plane * own, own), own)

    def summed(sent, kept, arrived):
        for one in sent:
            net.arrived(one)
        total = kept.astype(F32)
        for k in range(3):
            total = total + arrived[k].astype(F32)
        return total

    ways = ((0, 1, 2), (1, 2, 1))

    def scatter(blocks, arrived):
        return [
            net.copy(blocks.at[chips[which], way], arrived.at[way, n], at(first, 0))
            for n, pick in ((1, 3), (0, None))
            for way, first, _ in ways
            for which in (pick or first,)
        ]

    def scatter_on(sent, blocks, arrived):
        for one in sent:
            net.arrived(one)
        for way, _, then in ways:
            total = blocks[chips[then], way].astype(F32) + arrived[way, 1].astype(F32)
            blocks[chips[then], way] = total.astype(BF)
        return [
            net.copy(blocks.at[chips[then], way], arrived.at[way, 2], at(then, 0))
            for way, _, then in ways
        ]

    def gather(sent, blocks, arrived, total, target):
        for one in sent:
            net.arrived(one)
        for way, _, _ in ways:
            total[way] = (
                blocks[chip, way].astype(F32)
                + arrived[way, 0].astype(F32)
                + arrived[way, 2].astype(F32)
            ).astype(BF)
        load(total, target.at[core, chip])
        net.copy(total, target.at[core, chip], mate)
        return [
            net.copy(total.at[way], target.at[core, chip, way], at(dp, 0))
            for way, dp in ((0, 2), (1, 1), (0, 1), (1, 2))
        ]

    def gather_on(sent, target):
        for one in sent[:2]:
            net.arrived(one)
        return [
            net.copy(
                target.at[core, chips[then], way], target.at[core, chips[then], way], at(first, 0)
            )
            for way, first, then in ways
        ]

    def plane_scatter(blocks, arrived, far):
        far_sent = net.copy(blocks.at[planes[3]], far, at(0, 1), outer, inner)
        sent = [
            net.copy(blocks.at[planes[2]], arrived.at[1], at(0, 2), outer, inner),
            net.copy(blocks.at[planes[3]], arrived.at[2], at(0, 3), inner, inner),
            net.copy(blocks.at[planes[1]], arrived.at[0], at(0, 1)),
        ]

        @pl.when(outer)
        def _():
            arrived[2] = jnp.zeros(arrived.shape[1:], BF)

        return sent, far_sent

    def plane_scatter_on(far_sent, blocks, arrived, far):
        net.arrived(far_sent)

        @pl.when(inner)
        def _():
            total = blocks[planes[2]].astype(F32) + far[...].astype(F32)
            blocks[planes[2]] = total.astype(BF)

        return net.copy(blocks.at[planes[2]], arrived.at[1], at(0, 2), inner, outer)

    def plane_gather(source, target):
        return [
            net.copy(source, target.at[plane], at(0, 2)),
            net.copy(source, target.at[plane], at(0, 3), inner, inner),
            net.copy(source, target.at[plane], at(0, 1)),
        ]

    def plane_gather_on(sent, target):
        net.arrived(sent[0])
        return net.copy(target.at[planes[2]], target.at[planes[2]], at(0, 1), inner, outer)

    l_table = load(table_h, b.table)
    l_ada = {k: load(ada_h.at[k], b.ada.at[k]) for k in (2, 4)}
    l_tok = load(tok_h, b.tok)
    l_wq = load(wq_h, b.wq)
    barrier = pltpu.get_barrier_semaphore()
    for dp, dz in offsets:
        pl.semaphore_signal(barrier, inc=1, device_id=at(dp, dz), device_id_type=MESH)
    pl.semaphore_signal(barrier, inc=1, device_id=mate, device_id_type=MESH)

    spot = lax.rem(lax.broadcasted_iota(jnp.int32, (3 * ITEM_ROWS, rows), 0), ITEM_ROWS)
    picks = jnp.where(spot == item_v[group], 1.0, 0.0)
    b.pick[...] = picks.T.astype(BF)

    spot = lax.broadcasted_iota(jnp.int32, (ITEM_ROWS, classes), 0)
    label = lax.broadcasted_iota(jnp.int32, (ITEM_ROWS, classes), 1)
    hot = jnp.zeros((ITEM_ROWS, classes), F32)
    for i in range(items):
        hot = jnp.where((spot == i) & (label == cls_s[i]), 1.0, hot)
    l_table.wait()
    cond = dot(hot.astype(BF), b.table[...])
    b.cond[...] = cond
    cond_low = (cond / (1.0 + jnp.exp(-cond))).astype(BF)

    def make_mode(k):
        l_ada[k].wait()
        value = dot(cond_low, b.ada[k])
        high = value.astype(BF)
        rest = value - high.astype(F32)
        middle = rest.astype(BF)
        b.modes[k, 0:ITEM_ROWS] = high
        b.modes[k, ITEM_ROWS : 2 * ITEM_ROWS] = middle
        b.modes[k, 2 * ITEM_ROWS : 3 * ITEM_ROWS] = (rest - middle.astype(F32)).astype(BF)

    def per_token(k, which):
        return dot(b.pick[which], b.modes[k])

    def chunks(body):
        def step(i, carry):
            body(pl.ds(pl.multiple_of(i * 64, 64), 64))
            return carry

        lax.fori_loop(0, rows // 64, step, 0)

    make_mode(2)
    make_mode(4)

    l_tok.wait()

    def first_norm(which):
        normed, _ = norm_rows(b.tok[which].astype(F32))
        value = (normed * (1.0 + per_token(2, which)) + per_token(4, which)).astype(BF)
        b.a[0, which] = value[:, :half]
        b.a[1, which] = value[:, half:]

    for i in range(0, rows, 64):
        first_norm(slice(i, i + 64))
    l_wq.wait()
    l_wo = load(wo_h, b.wo.at[plane])
    l_ada.update({k: load(ada_h.at[k], b.ada.at[k]) for k in (0, 3, 5, 1)})
    l_cot = load(cot_h, b.cot)
    l_f2 = load(f2_h, b.f2)
    l_f1 = load(f1_h, b.f1)
    first_store = len(loads)
    for k in range(3):
        value = dot(b.a[0], b.wq[k, :half]) + dot(b.a[1], b.wq[k, half:])
        value = value.T.astype(BF)
        for h in range(4):
            b.q_out[h, k * 64 : (k + 1) * 64] = value[h * 64 : (h + 1) * 64]
    pl.semaphore_wait(barrier, len(offsets) + 1)
    sent_q = {
        (dp, n): net.copy(b.q_out.at[chips[dp], part_of], b.q_in.at[dp, part_of], at(dp, 0))
        for n, part_of in enumerate((slice(64, 192), slice(0, 64)))
        for dp in (3, 1, 2)
    }
    b.q_in[0] = b.q_out[chip]
    sent_k = [net.copy(b.q_in.at[0, 64:192], b.k_in.at[0], mate)]
    sent_a = net.copy(b.a.at[other], b.a_in, mate)
    sent_wo = [
        net.copy(wo_h.at[chip, core], b.wo.at[plane, chip, core], at(0, dz)) for dz in (3, 2, 1)
    ]

    spot = lax.broadcasted_iota(jnp.int32, (64, rows), 0)
    for s in range(4):
        for k, parity in enumerate((core, other)):
            item, scale = item_v[chips[s] * 2 + parity], scale_v[chips[s] * 2 + parity]
            by_item = jnp.where(item != spot - 1, BARRED, 0.0)
            by_scale = jnp.where((spot < 32) & (scale > spot - 16), BARRED, 0.0)
            b.kt[k * 4 + s, 64:128] = jnp.where(spot < 16, by_item, by_scale).astype(BF)
        item, scale = item_v[chips[s] * 2 + core], scale_v[chips[s] * 2 + core]
        by_item = jnp.where(item == spot - 1, 1.0, 0.0)
        by_scale = jnp.where((spot < 32) & (scale == spot - 16), 1.0, 0.0)
        b.qt[s, 64:128] = jnp.where(spot < 16, by_item, by_scale).astype(BF)
    make_mode(0)
    make_mode(3)
    make_mode(5)
    make_mode(1)
    l_cot.wait()

    def mlp_grad(which):
        b.mg[which] = (per_token(1, which) * b.cot[which].astype(F32)).astype(BF)

    chunks(mlp_grad)
    for dp in (3, 1, 2):
        net.arrived(sent_q[dp, 0])
        sent_k.append(net.copy(b.q_in.at[dp, 64:192], b.k_in.at[dp], mate))

    def take_keys(s, block):
        b.kt[s, 0:64] = block[0:64]
        b.ktw[:, s * 256 : (s + 1) * 256] = block[0:64]
        b.vt[s] = block[64:128]
        b.ka[s] = turned(b.kt[s]).astype(BF)

    for s in range(4):
        take_keys(s, b.q_in[s, 64:192])
    for dp in (3, 1, 2):
        net.arrived(sent_q[dp, 1])
    for s in range(4):
        b.qt[s, 0:64] = b.q_in[s, 0:64]
    for one in sent_k:
        net.arrived(one)
    for s in range(4):
        take_keys(4 + s, b.k_in[s])
    sent_mg = net.copy(b.mg, b.mg_in, mate)

    sent_h = {}
    for dp in (3, 1, 2, 0):
        queries = b.qt[dp]
        peak = None
        for s in range(8):
            scores = dot(b.ka[s], queries)
            b.scores[s] = scores
            top = jnp.max(scores, axis=0, keepdims=True)
            peak = top if peak is None else jnp.maximum(peak, top)
        total = jnp.zeros((1, rows), F32)
        result = jnp.zeros((64, rows), F32)
        cols = slice(dp * 256, (dp + 1) * 256)
        for s in range(8):
            terms = jnp.exp2((b.scores[s] - peak) * EIGHTH_LOG2)
            total = total + jnp.sum(terms, axis=0, keepdims=True)
            low = terms.astype(BF)
            b.pairs[s * 256 : (s + 1) * 256, 1024 + dp * 256 : 1280 + dp * 256] = low
            result = result + dot(b.vt[s], low)
        share = 1.0 / total
        b.share[:, cols] = share
        result = result * share
        b.heads[:, cols] = result
        b.h_out[dp] = result.astype(BF)
        for dz in (3, 2, 1, 0):
            if dp or dz:
                sent_h[dp, dz] = net.copy(b.h_out.at[dp], b.h_in.at[plane, chip], at(dp, dz))
        if dp == 3:
            for one in sent_wo:
                net.arrived(one)
            sent_wo2 = {
                (to, dz): net.copy(
                    b.wo.at[planes[dz], chip, core], b.wo.at[planes[dz], chip, core], at(to, 0)
                )
                for dz in (1, 2, 3)
                for to in (3, 1, 2)
            }
    b.h_in[plane, chip] = b.h_out[0]

    for s in range(8):
        b.vn[s] = turned(b.vt[s]).astype(BF)
    for s in range(4):
        some = turned(b.q_in[s, 0:64])
        b.wide[s * 256 : (s + 1) * 256] = jnp.concatenate(
            [some * 0.125, jnp.zeros((rows, 64), F32)], axis=1
        ).astype(BF)
    l_f2.wait()
    for n in range(4):
        cols = slice(n * 256, (n + 1) * 256)
        b.dact[:, cols] = dot_nt(b.mg[...], b.f2[cols])
    l_wo.wait()
    for one in sent_wo2.values():
        net.arrived(one)
    sent_wo3 = [
        net.copy(b.wo.at[planes[dz], :, core], b.wo.at[planes[dz], :, core], mate)
        for dz in (1, 2, 3)
    ]

    for dz in range(4):
        for dp in range(4):
            if dp or dz:
                net.arrived(sent_h[dp, dz])
        if dz:
            net.arrived(sent_wo3[dz - 1])
        left = turned(b.h_in[planes[dz]].reshape(256, rows)).astype(BF)
        right = b.wo[planes[dz]].reshape(256, width)
        if dz:
            b.attn[...] += dot(left, right)
        else:
            b.attn[...] = dot(left, right)
    sent_hx = net.copy(b.h_in.at[plane, pl.ds(2 * other, 2)], b.h_mate, mate)


    def second_norm(which):
        value = b.tok[which].astype(F32) + per_token(0, which) * b.attn[which]
        b.hid[which] = value
        normed, _ = norm_rows(value)
        value = (normed * (1.0 + per_token(3, which)) + per_token(5, which)).astype(BF)
        b.b[0, which] = value[:, :half]
        b.b[1, which] = value[:, half:]

    for i in range(0, rows, 64):
        second_norm(slice(i, i + 64))
    l_f1.wait()
    for n in range(4):
        cols = slice(n * 256, (n + 1) * 256)
        up = dot(b.b[0], b.f1[:half, cols]) + dot(b.b[1], b.f1[half:, cols])
        square = up * up
        bent = jnp.tanh(GELU_A * up * (1.0 + GELU_B * square))
        gate = 0.5 * (1.0 + bent)
        slope = gate + 0.5 * up * (1.0 - bent * bent) * (GELU_A * (1.0 + 3.0 * GELU_B * square))
        b.act[n // 2, :, (n % 2) * 256 : (n % 2 + 1) * 256] = (up * gate).astype(BF)
        b.ug[:, cols] = (b.dact[:, cols] * slope).astype(BF)
    for n in range(4):
        cols = slice(n * 256, (n + 1) * 256)
        value = dot_nt(b.ug[...], b.f1[cols])
        b.bg_out[:, :, cols] = value.astype(BF).reshape(4, own, 256)
    sent_bg, far_bg = plane_scatter(b.bg_out, b.bg_in, b.bg_far)

    sent_x = [
        net.copy(b.act.at[other], b.act_in, mate),
        net.copy(b.b.at[other], b.b_in, mate),
        net.copy(b.ug, b.ug_in, mate),
    ]
    b.left[0] = turned(b.act[core]).astype(BF)
    net.arrived(sent_mg)
    net.arrived(sent_x[0])
    b.left[1] = turned(b.act_in[...]).astype(BF)
    for n in range(4):
        some = slice(n * 128, (n + 1) * 128)
        value = dot(b.left[0, some], b.mg[...]) + dot(b.left[1, some], b.mg_in[...])
        b.g2_out[n] = value.astype(BF).reshape(2, 64, width)
    sent_g2 = scatter(b.g2_out, b.g2_in)
    sent_bg.append(plane_scatter_on(far_bg, b.bg_out, b.bg_in, b.bg_far))
    b.left[0] = turned(b.b[core]).astype(BF)
    net.arrived(sent_x[1])
    b.left[1] = turned(b.b_in[...]).astype(BF)
    net.arrived(sent_x[2])
    for n in range(4):
        some = slice(n * 128, (n + 1) * 128)
        value = dot(b.left[0, some], b.ug[...]) + dot(b.left[1, some], b.ug_in[...])
        b.g1_out[n] = value.astype(BF).reshape(2, 64, width)
    sent_g1 = scatter(b.g1_out, b.g1_in)
    for n in range(4):
        cols = slice(n * 256, (n + 1) * 256)
        value = dot(b.act[0], b.f2[:half, cols]) + dot(b.act[1], b.f2[half:, cols])
        b.mo_out[:, :, cols] = value.astype(BF).reshape(4, own, 256)

    def mode_sums(k, value):
        high = value.astype(BF)
        low = (value - high.astype(F32)).astype(BF)
        picked = turned(b.pick[mine])[0:ITEM_ROWS].astype(BF)
        value = (dot(picked, high) + dot(picked, low))[0:8]
        b.ms[0, k * 8 : (k + 1) * 8] = value[:, :half]
        b.ms[1, k * 8 : (k + 1) * 8] = value[:, half:]

    b_grad = summed(sent_bg, b.bg_out[plane], b.bg_in)
    normed, inverse = norm_rows(b.hid[mine])
    h_grad = b.cot[mine].astype(F32) + norm_back(
        b_grad * (1.0 + per_token(3, mine)), normed, inverse
    )
    b.hg[...] = h_grad
    attn_grad = (per_token(0, mine) * h_grad).astype(BF)
    b.ag[plane] = attn_grad
    for n in range(4):
        value = dot_nt(attn_grad, b.wo[n].reshape(256, width)).astype(BF)
        for h in range(4):
            some = value[:, h * 64 : (h + 1) * 64]
            b.do_out[n, h] = jnp.concatenate([some[: own // 2], some[own // 2 :]], axis=1)
    sent_do = {
        (dp, dz): net.copy(
            b.do_out.at[planes[dz], chips[dp]], b.do_in.at[dp, plane], at(dp, dz)
        )
        for dp, dz in reversed(offsets)
    }
    b.do_in[0, plane] = b.do_out[plane, chip]
    sent_mo, far_mo = plane_scatter(b.mo_out, b.mo_in, b.mo_far)
    sent_ag = plane_gather(b.ag.at[plane], b.ag)
    mode_sums(0, h_grad * b.attn[mine])
    mode_sums(3, b_grad * normed)
    mode_sums(5, b_grad)
    sent_g2 = scatter_on(sent_g2, b.g2_out, b.g2_in)
    sent_g1 = scatter_on(sent_g1, b.g1_out, b.g1_in)

    for one in sent_do.values():
        net.arrived(one)
    for s in range(4):
        cols = slice(s * 256, (s + 1) * 256)
        for n in range(4):
            both = b.do_in[s, n]
            b.dn[n * own : n * own + own // 2] = both[:, 0:64]
            b.dn[n * own + own // 2 : (n + 1) * own] = both[:, 64:128]
        value = turned(b.dn[...])
        b.dt[:, cols] = value.astype(BF)
        b.delta[:, cols] = jnp.sum(value * b.heads[:, cols], axis=0, keepdims=True)
        b.wide[1024 + s * 256 : 1280 + s * 256] = jnp.concatenate(
            [jnp.zeros((rows, 64), F32), (value * b.share[:, cols]).T], axis=1
        ).astype(BF)

    def attend_back(s):
        keys = slice(s * 256, (s + 1) * 256)
        for q in range(4):
            cols = slice(q * 256, (q + 1) * 256)
            pull = (dot(b.vn[s], b.dt[:, cols]) - b.delta[:, cols]) * b.share[:, cols]
            terms = b.pairs[keys, 1024 + q * 256 : 1280 + q * 256]
            b.pairs[keys, cols] = (pull * terms.astype(F32)).astype(BF)
        b.dkv[s] = dot(b.pairs[keys], b.wide[...]).T

    for s in range(4, 8):
        attend_back(s)
    sent_dkv = net.copy(b.dkv.at[4:8], b.dkv_in, mate)
    for s in range(4):
        attend_back(s)
    value = (dot(b.ktw[...], b.pairs[:, 0:1024]) * 0.125).astype(BF)
    for s in range(4):
        b.dx_out[s, 0:64] = value[:, s * 256 : (s + 1) * 256]
    b.dx_in[chip, 0:64] = b.dx_out[0, 0:64]
    sent_dx = [
        net.copy(b.dx_out.at[dp, 0:64], b.dx_in.at[chip, 0:64], at(dp, 0)) for dp in (3, 1, 2)
    ]
    net.arrived(sent_dkv)
    for s in range(4):
        b.dx_out[s, 64:192] = (b.dkv[s] + b.dkv_in[s]).astype(BF)
    b.dx_in[chip, 64:192] = b.dx_out[0, 64:192]
    sent_dx += [
        net.copy(b.dx_out.at[dp, 64:192], b.dx_in.at[chip, 64:192], at(dp, 0)) for dp in (3, 1, 2)
    ]
    sent_mo.append(plane_scatter_on(far_mo, b.mo_out, b.mo_in, b.mo_far))
    sent_g2b = gather(sent_g2, b.g2_out, b.g2_in, b.g2, gf2_o)
    sent_g1b = gather(sent_g1, b.g1_out, b.g1_in, b.g1, gf1_o)
    sent_ag.append(plane_gather_on(sent_ag, b.ag))

    for one in sent_dx:
        net.arrived(one)
    sent_dxm = net.copy(b.dx_in, b.dx_mate, mate)
    for k in range(3):
        value = b.dx_in[:, k * 64 : (k + 1) * 64].reshape(256, rows)
        b.dx[k] = turned(value).astype(BF)
    for n in range(4):
        cols = slice(n * 256, (n + 1) * 256)
        value = dot_nt(b.dx[0], b.wq[0, cols])
        value = value + dot_nt(b.dx[1], b.wq[1, cols])
        value = value + dot_nt(b.dx[2], b.wq[2, cols])
        b.xg_out[:, :, cols] = value.astype(BF).reshape(4, own, 256)
    sent_xg, far_xg = plane_scatter(b.xg_out, b.xg_in, b.xg_far)

    net.arrived(sent_a)
    net.arrived(sent_dxm)
    for h in range(4):
        value = dot(b.dx_in[h], b.a[core]) + dot(b.dx_mate[h], b.a_in[...])
        b.gq_out[h] = value.astype(BF).reshape(2, 96, half)
    sent_gq = scatter(b.gq_out, b.gq_in)
    sent_xg.append(plane_scatter_on(far_xg, b.xg_out, b.xg_in, b.xg_far))

    sent_g2b += gather_on(sent_g2b, gf2_o)
    sent_g1b += gather_on(sent_g1b, gf1_o)

    mlp_out = summed(sent_mo, b.mo_out[plane], b.mo_in)
    b.out[...] = (b.hid[mine] + per_token(1, mine) * mlp_out).astype(BF)
    sent_out = plane_gather(b.out, out_o)
    load(b.out, out_o.at[plane])
    mode_sums(1, b.cot[mine].astype(F32) * mlp_out)

    for one in sent_ag[1:]:
        net.arrived(one)
    sent_agm = net.copy(b.ag, b.ag_in, mate)
    value = dot(
        b.h_in[plane, pl.ds(2 * core, 2)].reshape(128, rows), b.ag[...].reshape(rows, width)
    )
    net.arrived(sent_hx)
    net.arrived(sent_agm)
    value = value + dot(b.h_mate[...].reshape(128, rows), b.ag_in[...].reshape(rows, width))
    b.go_out[...] = value.astype(BF).reshape(4, 32, width)
    sent_go = [
        net.copy(b.go_out.at[chips[dp]], b.go_in.at[dp - 1], at(dp, 0)) for dp in (3, 1, 2)
    ]

    sent_gq = scatter_on(sent_gq, b.gq_out, b.gq_in)
    plane_gather_on(sent_out, out_o)

    a_grad = summed(sent_xg, b.xg_out[plane], b.xg_in)
    normed, inverse = norm_rows(b.tok[mine].astype(F32))
    mode_sums(2, a_grad * normed)
    mode_sums(4, a_grad)
    sent_ms = net.copy(b.ms.at[other], b.ms_in, mate)
    value = b.hg[...] + norm_back(a_grad * (1.0 + per_token(2, mine)), normed, inverse)
    b.dtok[...] = value.astype(BF)
    net.arrived(sent_ms)
    b.m1[...] = (b.ms[core] + b.ms_in[...]).astype(BF)
    sent_m1 = [net.copy(b.m1, b.m1_in.at[dz - 1], at(0, dz)) for dz in (3, 2, 1)]
    sent_dt = plane_gather(b.dtok, dtok_o)
    load(b.dtok, dtok_o.at[plane])

    sent_gqb = gather(sent_gq, b.gq_out, b.gq_in, b.gq, gqkv_o)
    b.go[...] = summed(sent_go, b.go_out[chip], b.go_in).astype(BF)
    sent_gob = [net.copy(b.go, gout_o.at[core, chip], at(dp, 0)) for dp in (3, 1, 2)]
    load(b.go, gout_o.at[core, chip])
    net.copy(b.go, gout_o.at[core, chip], mate)
    b.m2[...] = summed(sent_m1, b.m1[...], b.m1_in).astype(BF)
    sent_m2 = [net.copy(b.m2, b.m2_in.at[dp - 1], at(dp, 0)) for dp in (3, 1, 2)]
    plane_gather_on(sent_dt, dtok_o)

    def pass_on(sent, array):
        for one in sent:
            net.arrived(one)
        for dp in (1, 2, 3):
            where = (core, chips[dp])
            net.copy(array.at[where], array.at[where], mate)

    pass_on(sent_g2b[2:], gf2_o)
    pass_on(sent_g1b[2:], gf1_o)
    sent_gqb += gather_on(sent_gqb, gqkv_o)
    b.m3[...] = summed(sent_m2, b.m2[...], b.m2_in)
    net.copy(b.m3, mode_o.at[core], mate)
    load(b.m3, mode_o.at[core])
    some = pl.ds(pl.multiple_of(plane * part, part), part)
    side = pl.ds(pl.multiple_of(core * half, half), half)
    value = jnp.zeros((16, part), F32)
    for k in range(COMPONENTS):
        sums = b.m3[k * 8 : (k + 1) * 8]
        high = sums.astype(BF).astype(F32)
        both = jnp.concatenate([high, sums - high], axis=0).astype(BF)
        value = value + dot_nt(both, b.ada[k, some, side])
    b.cg[...] = value[0:8] + value[8:16]
    net.copy(b.cg, cg_o.at[core], mate)
    load(b.cg, cg_o.at[core])
    load(b.cond, cond_o)
    pass_on(sent_gob, gout_o)
    pass_on(sent_gqb[2:], gqkv_o)
    assert len(net.made) == COPIES and len(loads) == LOADS
    net.finish()
    for one in loads[first_store:]:
        one.wait()


def buffers(dims):
    rows, width, part, hidden, items, classes = dims
    own, half = rows // 4, width // 2
    return dict(
        tok=((rows, width), BF),
        cot=((rows, width), BF),
        table=((classes, width), BF),
        ada=((COMPONENTS, width, width), BF),
        wq=((3, width, part), BF),
        wo=((4, 4, 2, 32, width), BF),
        f1=((width, hidden), BF),
        f2=((hidden, width), BF),
        modes=((COMPONENTS, 3 * ITEM_ROWS, width), BF),
        pick=((rows, 3 * ITEM_ROWS), BF),
        cond=((ITEM_ROWS, width), F32),
        a=((2, rows, half), BF),
        a_in=((rows, half), BF),
        q_out=((4, 192, rows), BF),
        q_in=((4, 192, rows), BF),
        k_in=((4, 128, rows), BF),
        kt=((8, 128, rows), BF),
        ka=((8, rows, 128), BF),
        vt=((8, 64, rows), BF),
        vn=((8, rows, 64), BF),
        qt=((4, 128, rows), BF),
        ktw=((64, 2048), BF),
        wide=((2048, 128), BF),
        scores=((8, rows, rows), F32),
        pairs=((2048, 2048), BF),
        share=((1, 1024), F32),
        heads=((64, 1024), F32),
        h_out=((4, 64, rows), BF),
        h_in=((4, 4, 64, rows), BF),
        h_mate=((2, 64, rows), BF),
        attn=((rows, width), F32),
        hid=((rows, width), F32),
        b=((2, rows, half), BF),
        b_in=((rows, half), BF),
        act=((2, rows, half), BF),
        act_in=((rows, half), BF),
        mg=((rows, width), BF),
        mg_in=((rows, width), BF),
        ug=((rows, hidden), BF),
        ug_in=((rows, hidden), BF),
        dact=((rows, hidden), F32),
        left=((2, half, rows), BF),
        bg_out=((4, own, width), BF),
        bg_in=((3, own, width), BF),
        mo_out=((4, own, width), BF),
        mo_in=((3, own, width), BF),
        mo_far=((own, width), BF),
        bg_far=((own, width), BF),
        xg_far=((own, width), BF),
        xg_out=((4, own, width), BF),
        xg_in=((3, own, width), BF),
        g1_out=((4, 2, 64, width), BF),
        g1_in=((2, 3, 64, width), BF),
        g1=((2, 64, width), BF),
        g2_out=((4, 2, 64, width), BF),
        g2_in=((2, 3, 64, width), BF),
        g2=((2, 64, width), BF),
        hg=((own, width), F32),
        ag=((4, own, width), BF),
        ag_in=((4, own, width), BF),
        do_out=((4, 4, own // 2, 128), BF),
        do_in=((4, 4, own // 2, 128), BF),
        dn=((rows, 64), BF),
        dt=((64, 1024), BF),
        delta=((1, 1024), F32),
        dkv=((8, 128, rows), F32),
        dkv_in=((4, 128, rows), F32),
        dx_out=((4, 192, rows), BF),
        dx_mate=((4, 192, rows), BF),
        dx_in=((4, 192, rows), BF),
        dx=((3, rows, part), BF),
        gq_out=((4, 2, 96, half), BF),
        gq_in=((2, 3, 96, half), BF),
        gq=((2, 96, half), BF),
        out=((own, width), BF),
        dtok=((own, width), BF),
        go_out=((4, 32, width), BF),
        go_in=((3, 32, width), BF),
        go=((32, width), BF),
        ms=((2, 48, half), F32),
        ms_in=((48, half), F32),
        m1=((48, half), BF),
        m1_in=((3, 48, half), BF),
        m2=((48, half), BF),
        m2_in=((3, 48, half), BF),
        m3=((48, half), F32),
        cg=((8, part), F32),
    )


def finish_kernel(
    cls_s, out_i, dtok_i, gqkv_i, gout_i, gf1_i, gf2_i, mode_i, cond_i, cg_i,
    out_o, dtok_o, table_o, ada_o, qkv_o, wout_o, f1_o, f2_o,
):
    step, last = pl.program_id(0), pl.num_programs(0) - 1
    plane = lax.axis_index("head")
    part = table_o.shape[1]
    mine = pl.ds(pl.multiple_of(plane * part, part), part)
    out_o[...] = out_i[0]
    dtok_o[...] = dtok_i[0]
    wout_o[...] = gout_i[0].astype(F32).reshape(wout_o.shape)
    f1_o[...] = gf1_i[0].astype(F32).reshape(f1_o.shape)
    f2_o[...] = gf2_i[0].astype(F32).reshape(f2_o.shape)
    sums = gqkv_i[0].astype(F32).reshape(4, 192, 256)
    for k in range(3):
        qkv_o[k] = sums[:, k * 64 : (k + 1) * 64].reshape(part, 256).T
    cond = cond_i[:, pl.ds(pl.multiple_of(step * 256, 256), 256)]
    cond_low = (cond / (1.0 + jnp.exp(-cond)))[0:8]
    low = jnp.concatenate([cond_low, cond_low], axis=0).astype(BF)
    side = pl.ds(pl.multiple_of(lax.rem(plane, 2) * part, part), part)
    for k in range(COMPONENTS):
        value = mode_i[lax.div(plane, 2), k * 8 : (k + 1) * 8, side]
        high = value.astype(BF).astype(F32)
        both = jnp.concatenate([high, value - high], axis=0).astype(BF)
        ada_o[k] = dot_tn(low, both)

    @pl.when(step == last)
    def _():
        own = cond_i[0:8, mine]
        gate = 1.0 / (1.0 + jnp.exp(-own))
        grad = (cg_i[0] + cg_i[1]) * gate * (1.0 + own * (1.0 - gate))
        spot = lax.broadcasted_iota(jnp.int32, table_o.shape, 0)
        total = jnp.zeros(table_o.shape, F32)
        for i in range(cls_s.shape[0]):
            total = total + jnp.where(spot == cls_s[i], grad[i : i + 1], 0.0)
        table_o[...] = total


def finish(
    class_ids,
    output,
    d_tokens,
    qkv_sum,
    out_sum,
    fc1_sum,
    fc2_sum,
    mode_grad,
    cond,
    cond_grad,
    classes,
):
    steps = 4
    own, width = output.shape[1:]
    half, part, hidden = width // 2, width // 4, 1024
    rows = own * 4
    smem = pl.BlockSpec(memory_space=pltpu.SMEM)
    few = pl.BlockSpec((1, own, width), lambda i: (i, 0, 0))
    table, ada, qkv, out, fc1, fc2 = (
        (classes, part),
        (COMPONENTS, width, part),
        (3, width, part),
        (part, width),
        (width, hidden),
        (hidden, width),
    )
    output, d_tokens, table, ada, qkv, out, fc1, fc2 = pl.pallas_call(
        finish_kernel,
        grid=(steps,),
        out_shape=[
            jax.ShapeDtypeStruct((rows, width), BF),
            jax.ShapeDtypeStruct((rows, width), BF),
        ]
        + [jax.ShapeDtypeStruct(shape, F32) for shape in (table, ada, qkv, out, fc1, fc2)],
        in_specs=[
            smem,
            few,
            few,
            pl.BlockSpec((1, 4, 2, 96, half // 2), lambda i: (i // 2, 0, 0, 0, i % 2)),
            pl.BlockSpec((1, 2, 32, width), lambda i: (i // 2, i % 2, 0, 0)),
            pl.BlockSpec((1, 2, 2, 64, hidden), lambda i: (i // 2, i % 2, 0, 0, 0)),
            pl.BlockSpec((1, 2, 2, 64, width), lambda i: (i // 2, i % 2, 0, 0, 0)),
            pl.BlockSpec((2, 48, half), lambda i: (0, 0, 0)),
            pl.BlockSpec((ITEM_ROWS, width), lambda i: (0, 0)),
            pl.BlockSpec((2, 8, part), lambda i: (0, 0, 0)),
        ],
        out_specs=[
            pl.BlockSpec((rows // steps, width), lambda i: (i, 0)),
            pl.BlockSpec((rows // steps, width), lambda i: (i, 0)),
            pl.BlockSpec((classes, part), lambda i: (0, 0)),
            pl.BlockSpec((COMPONENTS, 256, part), lambda i: (0, i, 0)),
            pl.BlockSpec((3, 256, part), lambda i: (0, i, 0)),
            pl.BlockSpec((64, width), lambda i: (i, 0)),
            pl.BlockSpec((256, hidden), lambda i: (i, 0)),
            pl.BlockSpec((256, width), lambda i: (i, 0)),
        ],
        compiler_params=pltpu.CompilerParams(vmem_limit_bytes=VMEM_BYTES),
    )(
        class_ids, output, d_tokens, qkv_sum, out_sum, fc1_sum, fc2_sum, mode_grad, cond, cond_grad
    )
    return output, d_tokens, table, ada, qkv.transpose(1, 0, 2), out, fc1, fc2


def on_block(
    tokens,
    class_ids,
    slot_item,
    slot_scale,
    class_table,
    w_ada,
    w_qkv,
    w_out,
    w_fc1,
    w_fc2,
    cotangent,
):
    rows, width = tokens.shape
    part, hidden = w_qkv.shape[2], w_fc1.shape[1]
    items, classes = class_ids.shape[0], class_table.shape[0]
    own, half = rows // 4, width // 2
    dims = (rows, width, part, hidden, items, classes)
    scratch = [pltpu.VMEM(shape, dtype) for shape, dtype in buffers(dims).values()]
    anywhere = pl.BlockSpec(memory_space=pl.ANY)
    vmem = pl.BlockSpec(memory_space=pltpu.VMEM)
    smem = pl.BlockSpec(memory_space=pltpu.SMEM)
    output, d_tokens, qkv_sum, out_sum, fc1_sum, fc2_sum, mode_grad, cond, cond_grad = pl.pallas_call(
        functools.partial(block_kernel, dims),
        out_shape=[
            jax.ShapeDtypeStruct((4, own, width), BF),
            jax.ShapeDtypeStruct((4, own, width), BF),
            jax.ShapeDtypeStruct((2, 4, 2, 96, half), BF),
            jax.ShapeDtypeStruct((2, 4, 32, width), BF),
            jax.ShapeDtypeStruct((2, 4, 2, 64, width), BF),
            jax.ShapeDtypeStruct((2, 4, 2, 64, width), BF),
            jax.ShapeDtypeStruct((2, 48, half), F32),
            jax.ShapeDtypeStruct((ITEM_ROWS, width), F32),
            jax.ShapeDtypeStruct((2, 8, part), F32),
        ],
        in_specs=[anywhere, smem, vmem, vmem] + [anywhere] * 7,
        out_specs=[anywhere] * 9,
        scratch_shapes=[
            pltpu.SemaphoreType.DMA((SENDS,)),
            pltpu.SemaphoreType.DMA((COPIES,)),
            pltpu.SemaphoreType.DMA((LOADS,)),
            *scratch,
        ],
        compiler_params=pltpu.CompilerParams(
            collective_id=0, has_side_effects=True, vmem_limit_bytes=VMEM_BYTES
        ),
        cost_estimate=pl.CostEstimate(
            flops=10_000_000_000, bytes_accessed=40_000_000, transcendentals=3_000_000
        ),
    )(
        tokens,
        class_ids,
        slot_item.reshape(8, 1, rows),
        slot_scale.reshape(8, 1, rows),
        class_table,
        w_ada,
        w_qkv.transpose(1, 0, 2),
        w_out.reshape(4, 2, 32, width),
        w_fc1,
        w_fc2,
        cotangent,
    )
    return finish(
        class_ids, output, d_tokens, qkv_sum, out_sum, fc1_sum, fc2_sum, mode_grad, cond, cond_grad,
        classes,
    )


def fits(mesh):
    return mesh.shape["tok"] == 8 and mesh.shape["head"] == 4


def layer_norm(values):
    centre = jnp.mean(values, axis=-1, keepdims=True)
    shifted = values - centre
    spread = jnp.mean(shifted * shifted, axis=-1, keepdims=True)
    return shifted * lax.rsqrt(spread + EPS)


def modulate(values, scale_in, shift_in):
    return layer_norm(values) * (1.0 + scale_in) + shift_in


def pair_scores(queries, key_block, query_item, key_item, query_scale, key_scale):
    scores = (
        jnp.einsum("qhd,khd->hqk", queries, key_block, preferred_element_type=jnp.float32) * 0.125
    )
    allowed = (
        (query_item[:, None] == key_item[None, :]) & (key_scale[None, :] <= query_scale[:, None])
    )[None]
    return (jnp.where(allowed, scores, -1e30), allowed)


def on_device(
    tokens,
    class_ids,
    slot_item,
    slot_scale,
    class_table,
    w_ada,
    w_qkv,
    w_out,
    w_fc1,
    w_fc2,
    cotangent,
):
    tok_rows, full_width = tokens.shape
    slot_count = slot_item.shape[0]
    item_count = class_ids.shape[0]
    class_count = class_table.shape[0]
    local_width = w_qkv.shape[2]
    local_heads = local_width // HEAD_DIM
    anchor = lax.axis_index("tok") * tok_rows
    first_col = lax.axis_index("head") * local_width
    my_item = lax.dynamic_slice_in_dim(slot_item, anchor, tok_rows)
    my_scale = lax.dynamic_slice_in_dim(slot_scale, anchor, tok_rows)
    class_pick = (class_ids[:, None] == jnp.arange(class_count, dtype=jnp.int32)[None, :]).astype(
        jnp.bfloat16
    )
    cond = jnp.dot(class_pick, class_table, preferred_element_type=jnp.float32)
    silu_cond, silu_back = jax.vjp(jax.nn.silu, cond)
    cond_low = silu_cond.astype(jnp.bfloat16)
    modes = jnp.einsum("id,cde->ice", cond_low, w_ada, preferred_element_type=jnp.float32)
    item_pick = (my_item[:, None] == jnp.arange(item_count, dtype=jnp.int32)[None, :]).astype(
        jnp.float32
    )
    per_token = jnp.dot(
        item_pick, modes.reshape(item_count, 6 * full_width), precision=HIGH
    ).reshape(tok_rows, 6, full_width)
    gamma_one = per_token[:, 0]
    gamma_two = per_token[:, 1]
    scale_one = per_token[:, 2]
    scale_two = per_token[:, 3]
    shift_one = per_token[:, 4]
    shift_two = per_token[:, 5]
    tok_float = tokens.astype(jnp.float32)
    a_pre, a_back = jax.vjp(modulate, tok_float, scale_one, shift_one)
    a_low = a_pre.astype(jnp.bfloat16)
    qkv_low = jnp.einsum("td,dce->tce", a_low, w_qkv, preferred_element_type=jnp.float32).astype(
        jnp.bfloat16
    )
    queries = qkv_low[:, 0]
    key_own = qkv_low[:, 1]
    value_own = qkv_low[:, 2]
    query_heads = queries.reshape(tok_rows, local_heads, HEAD_DIM)
    key_all, value_all = (
        lax.all_gather(key_own, "tok", axis=0, tiled=True),
        lax.all_gather(value_own, "tok", axis=0, tiled=True),
    )
    block_rows = math.gcd(slot_count, 2048)
    blocks = slot_count // block_rows
    key_blocks = key_all.reshape(blocks, block_rows, local_heads, HEAD_DIM)
    value_blocks = value_all.reshape(blocks, block_rows, local_heads, HEAD_DIM)
    item_blocks = slot_item.reshape(blocks, block_rows)
    scale_blocks = slot_scale.reshape(blocks, block_rows)
    key_wanted = jnp.min(scale_blocks, axis=1) <= jnp.max(my_scale)

    def first_pass(running, inputs):
        key_block, item_block, scale_block, wanted = inputs

        def first_compute_block(state_now):
            scores, allowed = pair_scores(
                query_heads, key_block, my_item, item_block, my_scale, scale_block
            )
            new_peak = jnp.maximum(state_now[0], jnp.max(scores, axis=2))
            terms = jnp.where(allowed, jnp.exp(scores - new_peak[:, :, None]), 0.0)
            return (
                new_peak,
                state_now[1] * jnp.exp(state_now[0] - new_peak) + jnp.sum(terms, axis=2),
            )

        return (lax.cond(wanted, first_compute_block, lambda state_now: state_now, running), None)

    initial = (
        jnp.full((local_heads, tok_rows), -1e30, jnp.float32),
        jnp.zeros((local_heads, tok_rows), jnp.float32),
    )
    (row_peak, summed), _ = lax.scan(
        first_pass, initial, (key_blocks, item_blocks, scale_blocks, key_wanted)
    )
    log_total = row_peak + jnp.log(summed)

    def second_pass(running, inputs):
        key_block, value_block, item_block, scale_block, wanted = inputs

        def second_compute_block(total_now):
            scores, allowed = pair_scores(
                query_heads, key_block, my_item, item_block, my_scale, scale_block
            )
            rounded = jnp.where(allowed, jnp.exp(scores - log_total[:, :, None]), 0.0).astype(
                jnp.bfloat16
            )
            return total_now + jnp.einsum(
                "hqk,khd->qhd", rounded, value_block, preferred_element_type=jnp.float32
            )

        return (lax.cond(wanted, second_compute_block, lambda total_now: total_now, running), None)

    heads_out, _ = lax.scan(
        second_pass,
        jnp.zeros((tok_rows, local_heads, HEAD_DIM), jnp.float32),
        (key_blocks, value_blocks, item_blocks, scale_blocks, key_wanted),
    )
    heads_low = heads_out.reshape(tok_rows, local_width).astype(jnp.bfloat16)
    attn_out = lax.psum(
        jnp.dot(heads_low, w_out, preferred_element_type=jnp.float32).astype(jnp.bfloat16), "head"
    ).astype(jnp.float32)
    hidden = tok_float + gamma_one * attn_out
    b_pre, b_back = jax.vjp(modulate, hidden, scale_two, shift_two)
    b_low = b_pre.astype(jnp.bfloat16)
    up_proj = jnp.dot(b_low, w_fc1, preferred_element_type=jnp.float32)
    act_pre, act_back = jax.vjp(lambda values: jax.nn.gelu(values, approximate=True), up_proj)
    act_low = act_pre.astype(jnp.bfloat16)
    mlp_out = lax.psum(
        jnp.dot(act_low, w_fc2, preferred_element_type=jnp.float32).astype(jnp.bfloat16), "head"
    ).astype(jnp.float32)
    output = (hidden + gamma_two * mlp_out).astype(jnp.bfloat16)
    out_grad = cotangent.astype(jnp.float32)
    mlp_grad = (gamma_two * out_grad).astype(jnp.bfloat16)
    fc2_weight_grad = jnp.einsum("tf,td->fd", act_low, mlp_grad, preferred_element_type=jnp.float32)
    act_grad = jnp.einsum("td,fd->tf", mlp_grad, w_fc2, preferred_element_type=jnp.float32)
    up_grad = act_back(act_grad)[0].astype(jnp.bfloat16)
    fc1_weight_grad = jnp.einsum("td,tf->df", b_low, up_grad, preferred_element_type=jnp.float32)
    b_grad = lax.psum(
        jnp.einsum("tf,df->td", up_grad, w_fc1, preferred_element_type=jnp.float32).astype(
            jnp.bfloat16
        ),
        "head",
    ).astype(jnp.float32)
    hidden_part, scale_two_grad, shift_two_grad = b_back(b_grad)
    hidden_grad = out_grad + hidden_part
    attn_grad = (gamma_one * hidden_grad).astype(jnp.bfloat16)
    out_weight_grad = jnp.einsum(
        "tf,te->fe", heads_low, attn_grad, preferred_element_type=jnp.float32
    )
    grad_low = jnp.einsum("te,fe->tf", attn_grad, w_out, preferred_element_type=jnp.float32).astype(
        jnp.bfloat16
    )
    grad_heads = grad_low.reshape(tok_rows, local_heads, HEAD_DIM)
    delta = jnp.einsum("qhd,qhd->hq", grad_heads.astype(jnp.float32), heads_out)

    def step_block(running, inputs):
        key_block, value_block, item_block, scale_block, wanted = inputs

        def step_compute_block(total_now):
            scores, allowed = pair_scores(
                query_heads, key_block, my_item, item_block, my_scale, scale_block
            )
            weights = jnp.where(allowed, jnp.exp(scores - log_total[:, :, None]), 0.0)
            weight_grad = jnp.einsum(
                "qhd,khd->hqk", grad_heads, value_block, preferred_element_type=jnp.float32
            )
            score_grad = (weights * (weight_grad - delta[:, :, None])).astype(jnp.bfloat16)
            total_now = (
                total_now
                + jnp.einsum(
                    "hqk,khd->qhd", score_grad, key_block, preferred_element_type=jnp.float32
                )
                * 0.125
            )
            key_term = (
                jnp.einsum(
                    "hqk,qhd->khd", score_grad, query_heads, preferred_element_type=jnp.float32
                )
                * 0.125
            )
            value_term = jnp.einsum(
                "hqk,qhd->khd",
                weights.astype(jnp.bfloat16),
                grad_heads,
                preferred_element_type=jnp.float32,
            )
            return (total_now, (key_term, value_term))

        def skip_block(total_now):
            nothing = jnp.zeros((block_rows, local_heads, HEAD_DIM), jnp.float32)
            return (total_now, (nothing, nothing))

        return lax.cond(wanted, step_compute_block, skip_block, running)

    query_grad, (key_terms, value_terms) = lax.scan(
        step_block,
        jnp.zeros((tok_rows, local_heads, HEAD_DIM), jnp.float32),
        (key_blocks, value_blocks, item_blocks, scale_blocks, key_wanted),
    )
    key_grad, value_grad = (
        lax.psum_scatter(
            key_terms.reshape(slot_count, local_width), "tok", scatter_dimension=0, tiled=True
        ),
        lax.psum_scatter(
            value_terms.reshape(slot_count, local_width), "tok", scatter_dimension=0, tiled=True
        ),
    )
    qkv_grad = jnp.stack(
        [query_grad.reshape(tok_rows, local_width), key_grad, value_grad], axis=1
    ).astype(jnp.bfloat16)
    qkv_weight_grad = jnp.einsum("td,tce->dce", a_low, qkv_grad, preferred_element_type=jnp.float32)
    a_grad = lax.psum(
        jnp.einsum("tce,dce->td", qkv_grad, w_qkv, preferred_element_type=jnp.float32).astype(
            jnp.bfloat16
        ),
        "head",
    ).astype(jnp.float32)
    tok_part, scale_one_grad, shift_one_grad = a_back(a_grad)
    d_tokens = (hidden_grad + tok_part).astype(jnp.bfloat16)
    token_modes = jnp.stack(
        [
            hidden_grad * attn_out,
            out_grad * mlp_out,
            scale_one_grad,
            scale_two_grad,
            shift_one_grad,
            shift_two_grad,
        ],
        axis=1,
    )
    mode_part = jnp.einsum(
        "ti,tf->if", item_pick, token_modes.reshape(tok_rows, 6 * full_width), precision=HIGH
    ).reshape(item_count, 6, full_width)
    qkv_sum, out_sum, fc1_sum, fc2_sum, mode_grad = lax.psum(
        (qkv_weight_grad, out_weight_grad, fc1_weight_grad, fc2_weight_grad, mode_part), "tok"
    )
    cond_grad = jnp.zeros((item_count, full_width), jnp.float32)
    for component in range(6):
        cond_grad = cond_grad + jnp.dot(
            mode_grad[:, component], w_ada[component].astype(jnp.float32).T, precision=HIGH
        )
    pre_grad = silu_back(cond_grad)[0]
    own_pre = lax.dynamic_slice_in_dim(pre_grad, first_col, local_width, 1)
    table_grad = jnp.einsum("ic,id->cd", class_pick.astype(jnp.float32), own_pre, precision=HIGH)
    own_modes = lax.dynamic_slice_in_dim(mode_grad, first_col, local_width, 2)
    ada_grad = jnp.einsum("id,ice->cde", cond_low.astype(jnp.float32), own_modes, precision=HIGH)
    return (output, d_tokens, table_grad, ada_grad, qkv_sum, out_sum, fc1_sum, fc2_sum)


def solution(mesh):
    placed = (
        P("tok", None),
        P(),
        P(),
        P(),
        P(),
        P(),
        P(None, None, "head"),
        P("head", None),
        P(None, "head"),
        P("head", None),
        P("tok", None),
    )
    return jax.shard_map(
        on_block if fits(mesh) else on_device,
        mesh=mesh,
        in_specs=placed,
        out_specs=(
            P("tok", None),
            P("tok", None),
            P(None, "head"),
            P(None, None, "head"),
            P(None, None, "head"),
            P("head", None),
            P(None, "head"),
            P("head", None),
        ),
        check_vma=False,
    )
```
